512 devices in a mesh: gx: 8 (over y), gy: 64 (over z, x, core).
Axes of the slice: x: 4, y: 8, z: 8, core: 2. Of those that a mesh axis runs over, the one named last changes fastest.
Arguments:
- source: float32 [256, 16384], P('gx', 'gy'), may hold values from -6 to 6
- potential: float32 [256, 16384], P('gx', 'gy'), may hold values from -1.5 to 1.5
- mobility_along: float32 [256, 16384], P('gx', 'gy'), may hold values from 0.3 to 3
- mobility_across: float32 [256, 16384], P('gx', 'gy'), may hold values from 0.3 to 3
- recombination: float32 [256, 16384], P('gx', 'gy'), may hold values from 0.002 to 0.05
- counts: int32 [8, 64], P('gx', 'gy'), may hold values from 8 to 32, as said below
- basis: float32 [256, 1179648], P('gx', 'gy'), may hold values from -1 to 1
- coarse_inverse: float32 [16384, 16384], P(('gx', 'gy')), may hold values from -8 to 8
Outputs:
- solution: float32 [256, 16384], P('gx', 'gy')
- residual: float32 [256, 16384], P('gx', 'gy')
The draws below stay inside these ranges and needn't reach their ends.
Inputs may be any that keep to these rules, and one draw needn't show every extreme that they name: `counts`: the number of a subdomain's rows of basis that are in use.
All inputs are finite; a program needn't handle non-finite values.
Results may differ from the reference program's by a relative error of at most 0.003.
Values sent between devices are 32-bit elements; how exact they have to be, the bound alone decides.
No kernel may reach another device: no remote copies, remote signals or barrier semaphores. Data moves between devices by JAX's collectives and lax.ppermute only.
A program may use at most 64 MiB of HBM per device.

```python
import math
import jax
import jax.numpy as jnp
from jax import lax

CX = 32
CY = 256
OV = 16
KMAX = 32
SWEEPS = 8
SUBX = 8
SUBY = 64
SUBS = 512
NX = 256
NY = 16384
PX = 64
PY = 288
EXTC = 18432
NC = 16384


def draw_counts(key, part):
    key = jax.random.fold_in(key, 11)
    values = jax.random.randint(key, (SUBX, SUBY), KMAX // 4, KMAX + 1)
    values = values.at[0, 0].set(KMAX)
    values = values.at[0, 1].set(KMAX // 4)
    return values.astype(jnp.int32)


def draw_basis(key, part):
    key = jax.random.fold_in(key, 31)
    keys = jax.random.split(key, 5)
    shape = (SUBX, KMAX, SUBY)
    freq_rows = jax.random.uniform(keys[0], shape, jnp.float32, 0.0, 3.0 * math.pi / PX)
    freq_cols = jax.random.uniform(keys[1], shape, jnp.float32, 0.0, 6.0 * math.pi / PY)
    phase_rows = jax.random.uniform(keys[2], shape, jnp.float32, -math.pi, math.pi)
    phase_cols = jax.random.uniform(keys[3], shape, jnp.float32, -math.pi, math.pi)
    row_coord = jnp.arange(PX, dtype=jnp.float32) + 0.5
    col_coord = jnp.arange(PY, dtype=jnp.float32) + 0.5
    wave_rows = jnp.cos(freq_rows[..., None] * row_coord + phase_rows[..., None])
    wave_cols = jnp.cos(freq_cols[..., None] * col_coord + phase_cols[..., None])
    smooth_part = wave_rows[..., :, None] * wave_cols[..., None, :]
    full_shape = (SUBX, KMAX, SUBY, PX, PY)
    rough_part = jnp.clip(jax.random.normal(keys[4], full_shape, jnp.float32), -4.0, 4.0)
    values = (2.0 * smooth_part + 0.25 * rough_part) / math.sqrt(EXTC)
    return values.reshape(SUBX * KMAX, SUBY * EXTC)


def draw_coarse_inverse(key, part):
    key = jax.random.fold_in(key, 23)
    noise_key, diagonal_key = jax.random.split(key)
    noise = jnp.clip(jax.random.normal(noise_key, (NC, NC), jnp.float32), -3.0, 3.0)
    diagonal_values = jnp.exp(jax.random.uniform(diagonal_key, (NC,), jnp.float32, math.log(2.0), math.log(8.0)))
    diagonal_values = jnp.where(jnp.arange(NC) == 0, 8.0, diagonal_values)
    row_index = lax.broadcasted_iota(jnp.int32, (NC, NC), 0)
    column_index = lax.broadcasted_iota(jnp.int32, (NC, NC), 1)
    row_sub = row_index // KMAX
    column_sub = column_index // KMAX
    distance = (jnp.abs(row_sub // SUBY - column_sub // SUBY) + jnp.abs(row_sub % SUBY - column_sub % SUBY)).astype(jnp.float32)
    scale = 1.5 * jnp.exp(-0.5 * distance) / math.sqrt(KMAX) + 4.0 / math.sqrt(NC)
    on_diagonal = row_index == column_index
    return jnp.where(on_diagonal, diagonal_values[:, None], noise * scale)


def block_levels(rng, dims, cuts, low, high):
    def one(position, blocks):
        heights = jax.random.uniform(jax.random.fold_in(jax.random.fold_in(rng, 6), position), (blocks,), jnp.float32, low / len(cuts), high / len(cuts))
        return jnp.repeat(jnp.exp(heights), dims[position] // blocks).reshape((-1,) + (1,) * (len(dims) - position - 1))

    factor_of = one(*cuts[0])
    for cut in cuts[1:]:
        factor_of = factor_of * one(*cut)
    return factor_of


def gaussian(stream_key, extent, width, most, pieces=(), kind=jnp.bfloat16):
    gain = block_levels(stream_key, extent, pieces, -0.22, 0.18) if pieces else 1.0
    values = jax.random.normal(stream_key, extent, jnp.float32) * width * gain
    return jnp.minimum(jnp.maximum(values, -most), most).astype(kind)


def setup_inputs(seed: int = 0) -> dict:
    key_of = jax.random.split(jax.random.key(seed), 9)
    source = gaussian(key_of[0], (NX, NY), 1.0, 6.0, ((0, 8), (1, 64)), jnp.float32)
    potential = jnp.clip(jax.random.uniform(key_of[1], (NX, NY), jnp.float32, -1.5, 1.5) * block_levels(key_of[1], (NX, NY), ((0, 8), (1, 64)), -0.4, 0.0), -1.5, 1.5)
    mobility_along = jnp.clip(jnp.exp(math.log(3.0) - 2.3025851 * jax.random.uniform(key_of[2], (NX, NY), jnp.float32) ** block_levels(key_of[2], (NX, NY), ((0, 8), (1, 64)), -0.2, 0.2)), 0.3, 3.0)
    mobility_across = jnp.clip(jnp.exp(math.log(3.0) - 2.3025851 * jax.random.uniform(key_of[3], (NX, NY), jnp.float32) ** block_levels(key_of[3], (NX, NY), ((0, 8), (1, 64)), -0.2, 0.2)), 0.3, 3.0)
    recombination = jnp.clip(jnp.exp(math.log(0.05) - 3.218876 * jax.random.uniform(key_of[4], (NX, NY), jnp.float32) ** block_levels(key_of[4], (NX, NY), ((0, 8), (1, 64)), -0.2, 0.2)), 0.002, 0.05)
    counts = draw_counts(jax.random.fold_in(key_of[8], 71), 0)
    basis = draw_basis(jax.random.fold_in(key_of[8], 71), 0)
    coarse_inverse = draw_coarse_inverse(jax.random.fold_in(key_of[8], 71), 0)
    return dict(source=source, potential=potential, mobility_along=mobility_along, mobility_across=mobility_across, recombination=recombination, counts=counts, basis=basis, coarse_inverse=coarse_inverse)


OMEGA = 0.8
EPSILON = 1e-06
HIGHEST_PRECISION = lax.Precision.HIGHEST

def face_weights(potential, mobility_along, mobility_across):
    along_first = jnp.sqrt(mobility_along[:-1, :] * mobility_along[1:, :])
    along_second = jnp.sqrt(mobility_across[:, :-1] * mobility_across[:, 1:])
    rise_first = potential[1:, :] - potential[:-1, :]
    rise_second = potential[:, 1:] - potential[:, :-1]
    downward = along_first * jnp.exp(0.5 * rise_first)
    upward = along_first * jnp.exp(-0.5 * rise_first)
    eastward = along_second * jnp.exp(0.5 * rise_second)
    westward = along_second * jnp.exp(-0.5 * rise_second)
    return (downward, upward, eastward, westward)

def build(potential, mobility_along, mobility_across, recombination):
    downward, upward, eastward, westward = face_weights(potential, mobility_along, mobility_across)
    diagonal = recombination + jnp.pad(upward, ((0, 1), (0, 0))) + jnp.pad(downward, ((1, 0), (0, 0)))
    diagonal = diagonal + jnp.pad(westward, ((0, 0), (0, 1))) + jnp.pad(eastward, ((0, 0), (1, 0)))
    return (diagonal, (downward, upward, eastward, westward))

def coupled(field, faces):
    downward, upward, eastward, westward = faces
    total = jnp.pad(downward * field[1:, :], ((0, 1), (0, 0)))
    total = total + jnp.pad(upward * field[:-1, :], ((1, 0), (0, 0)))
    total = total + jnp.pad(eastward * field[:, 1:], ((0, 0), (0, 1)))
    total = total + jnp.pad(westward * field[:, :-1], ((0, 0), (1, 0)))
    return total

def smooth(vector_patch, diagonal, faces):
    field = jnp.zeros_like(vector_patch)
    for sweep in range(SWEEPS):
        field = field + OMEGA * (vector_patch - (diagonal * field - coupled(field, faces))) / diagonal
    return field

def least_squares(source_norm, first_first, second_first, first_second, second_second, third_second):
    radius = jnp.sqrt(first_first * first_first + second_first * second_first)
    cosine = first_first / radius
    sine = second_first / radius
    upper_right = cosine * first_second + sine * second_second
    lower_right = cosine * second_second - sine * first_second
    radius_two = jnp.sqrt(lower_right * lower_right + third_second * third_second)
    weight_two = lower_right / radius_two * (-sine * source_norm) / radius_two
    weight_one = (cosine * source_norm - upper_right * weight_two) / radius
    remainder_one = source_norm - first_first * weight_one - first_second * weight_two
    remainder_two = -second_first * weight_one - second_second * weight_two
    remainder_three = -third_second * weight_two
    return (weight_one, weight_two, remainder_one, remainder_two, remainder_three)

def fold(parts):
    middle = parts[:, :, OV:-OV, :]
    from_above = jnp.pad(parts[:-1, :, -OV:, :], ((1, 0), (0, 0), (0, 0), (0, 0)))
    from_below = jnp.pad(parts[1:, :, :OV, :], ((0, 1), (0, 0), (0, 0), (0, 0)))
    middle = middle.at[:, :, :OV, :].add(from_above)
    middle = middle.at[:, :, -OV:, :].add(from_below)
    inner = middle[:, :, :, OV:-OV]
    from_left = jnp.pad(middle[:, :-1, :, -OV:], ((0, 0), (1, 0), (0, 0), (0, 0)))
    from_right = jnp.pad(middle[:, 1:, :, :OV], ((0, 0), (0, 1), (0, 0), (0, 0)))
    inner = inner.at[:, :, :, :OV].add(from_left)
    inner = inner.at[:, :, :, -OV:].add(from_right)
    return inner

def reference(source, potential, mobility_along, mobility_across, recombination, counts, basis, coarse_inverse):
    grid_diagonal, grid_faces = build(potential, mobility_along, mobility_across, recombination)

    def apply(field):
        return grid_diagonal * field - coupled(field, grid_faces)
    padded_fields = [jnp.pad(array, OV) for array in (potential, mobility_along, mobility_across, recombination)]
    live_all = (lax.broadcasted_iota(jnp.int32, (SUBX, SUBY, KMAX), 2) < counts[:, :, None]).astype(jnp.float32)
    live_all = live_all.reshape(SUBS, KMAX)
    indices = jnp.arange(SUBS, dtype=jnp.int32)

    def corner_of(index):
        row_block = (index // SUBY).astype(jnp.int32)
        column_block = (index % SUBY).astype(jnp.int32)
        return (row_block, column_block)

    def precondition(vector):
        padded = jnp.pad(vector, OV)

        def local(index):
            row_block, column_block = corner_of(index)
            start = (row_block * CX, column_block * CY)
            fields = [lax.dynamic_slice(array, start, (PX, PY)) for array in padded_fields]
            diagonal, faces = build(fields[0], fields[1], fields[2], fields[3])
            row_place = row_block * CX - OV + lax.broadcasted_iota(jnp.int32, (PX, PY), 0)
            column_place = column_block * CY - OV + lax.broadcasted_iota(jnp.int32, (PX, PY), 1)
            inside = ((row_place >= 0) & (row_place < NX) & (column_place >= 0) & (column_place < NY)).astype(jnp.float32)
            diagonal = diagonal + (1.0 - inside)
            vector_patch = lax.dynamic_slice(padded, start, (PX, PY))
            solved = smooth(vector_patch, diagonal, faces)[OV:OV + CX, OV:OV + CY]
            block = lax.dynamic_slice(basis, (row_block * KMAX, column_block * EXTC), (KMAX, EXTC))
            restricted = jnp.dot(block, vector_patch.reshape(EXTC), precision=HIGHEST_PRECISION)
            return (solved, restricted)
        solved, restricted = lax.map(local, indices)
        restricted = restricted * live_all
        coarse = jnp.dot(coarse_inverse, restricted.reshape(NC), precision=HIGHEST_PRECISION)
        coarse = coarse.reshape(SUBS, KMAX) * live_all

        def spread(items):
            index, weights = items
            row_block, column_block = corner_of(index)
            block = lax.dynamic_slice(basis, (row_block * KMAX, column_block * EXTC), (KMAX, EXTC))
            return jnp.dot(weights, block, precision=HIGHEST_PRECISION).reshape(PX, PY)
        parts = lax.map(spread, (indices, coarse))
        folded = fold(parts.reshape(SUBX, SUBY, PX, PY))
        total = solved.reshape(SUBX, SUBY, CX, CY) + folded
        return total.transpose(0, 2, 1, 3).reshape(NX, NY)
    source_norm = jnp.sqrt(jnp.sum(source * source) + EPSILON)
    first = source / source_norm
    first_dir = precondition(first)
    image = apply(first_dir)
    first_first = jnp.sum(first * image)
    image = image - first_first * first
    second_first = jnp.sqrt(jnp.sum(image * image) + EPSILON)
    second = image / second_first
    second_dir = precondition(second)
    image = apply(second_dir)
    first_second = jnp.sum(first * image)
    second_second = jnp.sum(second * image)
    image = image - first_second * first - second_second * second
    third_second = jnp.sqrt(jnp.sum(image * image) + EPSILON)
    third = image / third_second
    weight_one, weight_two, remainder_one, remainder_two, remainder_three = least_squares(source_norm, first_first, second_first, first_second, second_second, third_second)
    solution = weight_one * first_dir + weight_two * second_dir
    residual = remainder_one * first + remainder_two * second + remainder_three * third
    return (solution, residual)
```

```python
import jax
import jax.numpy as jnp
from jax import lax
from jax.experimental import pallas as pl
from jax.experimental.pallas import tpu as pltpu
from jax.sharding import PartitionSpec as P

OV = 16
SWEEPS = 8
OMEGA = 0.8
EPSILON = 1e-06
CX = 32
CY = 256
K = 32
PX = CX + 2 * OV
PY = CY + 2 * OV
LW = 384
GROUPS = PX // 4
STRIP = 24
SCALARS = 96
f32 = jnp.float32
AXES = ("gx", "gy")


def lanes_of(shape):
    return lax.broadcasted_iota(jnp.int32, shape, len(shape) - 1)


def rows_of(shape):
    return lax.broadcasted_iota(jnp.int32, shape, len(shape) - 2)


def left(x):
    return pltpu.roll(x, LW - 1, 1)


def right(x):
    return pltpu.roll(x, 1, 1)


def up(x):
    return pltpu.roll(x, x.shape[0] - 1, 0)


def down(x):
    return pltpu.roll(x, 1, 0)


def own_mask(shape, first):
    rows, lanes = rows_of(shape) + first, lanes_of(shape)
    return (rows >= OV) & (rows < OV + CX) & (lanes >= OV) & (lanes < OV + CY)


def total(x):
    return jnp.sum(jnp.sum(x, axis=0, keepdims=True), axis=1, keepdims=True)


def to_row(column):
    shape = (K, 128)
    spread = jnp.broadcast_to(column, shape)
    return jnp.sum(jnp.where(rows_of(shape) == lanes_of(shape), spread, 0.0), axis=0, keepdims=True)


def restrict(basis, patch, tiles, flat):
    for t in range(3):
        tiles[t] = patch[:, t * 128 : (t + 1) * 128]
    parts = [None] * 9
    for m in range(4):
        rows = jnp.concatenate(
            [tiles[t, pl.ds(m, GROUPS, stride=4), :] for t in range(3)], axis=1
        )
        if m:
            rows = pltpu.roll(rows, 32 * m, 1)
        for t in range(3):
            piece = rows[:, t * 128 : (t + 1) * 128]
            at = 2 * m + t
            parts[at] = piece if parts[at] is None else parts[at] + piece
    for t in range(9):
        flat[t] = parts[t]
    sums = [jnp.zeros((K, 128), f32) for _ in range(3)]
    for g in range(GROUPS):
        for t in range(9):
            block = (g * 9 + t) * 128
            row = jnp.broadcast_to(flat[t, pl.ds(g, 1), :], (K, 128))
            sums[t % 3] = sums[t % 3] + basis[:, block : block + 128] * row
    return jnp.sum(sums[0] + sums[1] + sums[2], axis=1, keepdims=True)


def prolong(basis, weights, tiles, flat):
    wide = jnp.broadcast_to(weights, (K, 128))
    for g in range(GROUPS):
        for t in range(9):
            block = (g * 9 + t) * 128
            flat[t, pl.ds(g, 1), :] = jnp.sum(
                basis[:, block : block + 128] * wide, axis=0, keepdims=True
            )
    for m in range(4):
        rows = jnp.concatenate([flat[2 * m + t] for t in range(3)], axis=1)
        if m:
            rows = pltpu.roll(rows, LW - 32 * m, 1)
        rows = jnp.where(lanes_of(rows.shape) < PY, rows, 0.0)
        for t in range(3):
            tiles[t, pl.ds(m, GROUPS, stride=4), :] = rows[:, t * 128 : (t + 1) * 128]
    return jnp.concatenate([tiles[t] for t in range(3)], axis=1)


def gathered(rows, coarse, suby):
    count = rows.shape[0] // 4
    shift = suby // 4
    taken = [rows[pl.ds(q, count, stride=4), :] for q in range(4)]
    zero = jnp.zeros((shift, 128), f32)
    lanes = lanes_of((count, 128))
    result = None
    for s in range(4):
        own = taken[s]
        later = jnp.concatenate([zero, taken[(s + 1) % 4][: count - shift]], axis=0)
        earlier = jnp.concatenate([taken[(s + 2) % 4][shift:], zero], axis=0)
        piece = jnp.where(
            lanes < 32, own, jnp.where(lanes < 64, later, jnp.where(lanes < 96, earlier, 0.0))
        )
        if s:
            piece = pltpu.roll(piece, 32 * s, 1)
        result = piece if result is None else result + piece
    coarse[...] = result
    return jnp.sum(taken[0] + taken[1] + (taken[2] + taken[3]), axis=0, keepdims=True)


def pick(row, lane):
    return jnp.sum(jnp.where(lanes_of(row.shape) == lane, row, 0.0), axis=1, keepdims=True)


def coarse_solve(inverse, coarse):
    sums = [jnp.zeros((K, 128), f32) for _ in range(4)]
    for b in range(coarse.shape[0]):
        row = jnp.broadcast_to(coarse[pl.ds(b, 1), :], (K, 128))
        sums[b % 4] = sums[b % 4] + inverse[:, b * 128 : (b + 1) * 128] * row
    return jnp.sum((sums[0] + sums[1]) + (sums[2] + sums[3]), axis=1, keepdims=True)


def live_of(counts):
    return (rows_of((K, 1)) < counts[0, 0]).astype(f32)


def relax(vector, diagonal, faces):
    inverse = OMEGA / jnp.where(diagonal > 0.0, diagonal, 1.0)
    below, above, east, west = [inverse * face for face in faces]
    start = inverse * vector
    field = start
    for _ in range(SWEEPS - 1):
        moved = below * up(field) + above * down(field)
        moved = moved + (east * left(field) + west * right(field))
        field = (start + (1.0 - OMEGA) * field) + moved
    return field


def operate(field, diagonal, faces):
    below, above, east, west = faces
    moved = below * up(field) + above * down(field)
    moved = moved + (east * left(field) + west * right(field))
    return diagonal * field - moved


def pack_rows(counts, source, potential, along, across, recombination, head, tail, ahead, behind):
    live = live_of(counts)
    fields = (source, potential, along, across, recombination)
    for f, field in enumerate(fields):
        for t in range(2):
            at = (2 * f + t) * OV
            cols = slice(t * 128, (t + 1) * 128)
            ahead[at : at + OV, :] = field[CX - OV :, cols]
            behind[at : at + OV, :] = field[:OV, cols]
    for t in range(3):
        at = 160 + t * K
        cols = slice(t * 128, (t + 1) * 128)
        ahead[at : at + K, :] = tail[:, cols] * live
        behind[at : at + K, :] = head[:, cols] * live


def pack_columns(
    source, potential, along, across, recombination, before, after, rows, rightward, leftward
):
    fields = (source, potential, along, across, recombination)
    lanes = lanes_of((PX, 128))
    to_right = to_left = None
    for f, field in enumerate(fields):
        tiles = []
        for t in range(2):
            at = (2 * f + t) * OV
            cols = slice(t * 128, (t + 1) * 128)
            tile = jnp.concatenate(
                [before[at : at + OV, :], field[:, cols], after[at : at + OV, :]], axis=0
            )
            rows[f, :, cols] = tile
            tiles.append(tile)
        last = pltpu.roll(jnp.where(lanes >= 111, tiles[1], 0.0), 17 + STRIP * f, 1)
        first = jnp.where(lanes < 17, tiles[0], 0.0)
        if f:
            first = pltpu.roll(first, STRIP * f, 1)
        to_right = last if f == 0 else to_right + last
        to_left = first if f == 0 else to_left + first
    rightward[...] = to_right
    leftward[...] = to_left


def prepare(suby, counts, rows, from_left, from_right, basis, patch, coefs, solved, gather, tiles, flat):
    zero = jnp.zeros((PX, LW - CY), f32)
    lanes = lanes_of((PX, 128))
    fields = []
    for f in range(5):
        middle = pltpu.roll(jnp.concatenate([rows[f], zero], axis=1), OV, 1)
        band = (lanes >= STRIP * f) & (lanes < STRIP * f + 17)
        wide = jnp.zeros((PX, LW - 128), f32)
        one = jnp.concatenate([jnp.where(band, from_left[...], 0.0), wide], axis=1)
        two = jnp.concatenate([jnp.where(band, from_right[...], 0.0), wide], axis=1)
        one = pltpu.roll(one, LW - 1 - STRIP * f, 1)
        two = pltpu.roll(two, OV + CY - STRIP * f, 1)
        fields.append(middle + one + two)
    source, potential, along, across, recombination = fields
    weight = jnp.sqrt(along * up(along))
    rise = 0.5 * (up(potential) - potential)
    below = weight * jnp.exp(rise)
    above = weight * jnp.exp(-rise)
    diagonal = recombination + above + down(below)
    weight = jnp.sqrt(across * left(across))
    rise = 0.5 * (left(potential) - potential)
    east = weight * jnp.exp(rise)
    west = weight * jnp.exp(-rise)
    diagonal = diagonal + west + right(east)
    faces = (below, down(above), east, right(west))
    coefs[0] = diagonal
    for f in range(4):
        coefs[1 + f] = faces[f]
    source = jnp.where(lanes_of((PX, LW)) < PY, source, 0.0)
    patch[...] = source
    own = own_mask((PX, LW), 0)
    square = total(jnp.where(own, source * source, 0.0))
    local = relax(source[8:56], diagonal[8:56], [face[8:56] for face in faces])
    solved[...] = jnp.where(own_mask((48, LW), 8), local, 0.0)
    residual = restrict(basis, source, tiles, flat) * live_of(counts)
    row = to_row(residual)
    row = jnp.where(lanes_of((1, 128)) == SCALARS, square, row)
    gather[...] = jnp.broadcast_to(row, gather.shape)


def put(scalars, at, value):
    scalars[pl.ds(at, 1), :] = jnp.broadcast_to(value, (1, 128))


def got(scalars, at):
    return scalars[pl.ds(at, 1), :][:, 0:1]


def spread_first(
    suby, counts, rows, inverse, basis, solved, part, weights, scalars, coarse, tiles, flat
):
    sums = gathered(rows, coarse, suby)
    square = pick(sums, SCALARS)
    norm = jnp.sqrt(square + EPSILON)
    scale = 1.0 / norm
    solution = coarse_solve(inverse, coarse) * live_of(counts) * scale
    weights[...] = jnp.broadcast_to(solution, (K, 128))
    put(scalars, 0, norm)
    put(scalars, 1, square / (square + EPSILON))
    part[...] = prolong(basis, solution, tiles, flat)
    part[8:56, :] = part[8:56, :] + solved[...] * scale


def fold_rows(part, before, after, folded, rightward, leftward):
    height = folded.shape[0]
    first = (PX - height) // 2
    half = height // 2
    whole = part[first : first + height, :] + jnp.concatenate(
        [before[PX // 2 - half :, :] if before.shape[0] > half else before[...],
         after[:half, :] if after.shape[0] > half else after[...]],
        axis=0,
    )
    folded[...] = whole
    lanes = lanes_of((height, 128))
    moved = pltpu.roll(whole, LW - 255, 1)
    rightward[...] = jnp.where(lanes < 33, moved[:, :128], 0.0)
    leftward[...] = jnp.where(lanes < 33, whole[:, :128], 0.0)


def folded_columns(folded, from_left, from_right):
    height = folded.shape[0]
    zero = jnp.zeros((height, 256), f32)
    one = pltpu.roll(jnp.concatenate([from_left[...], zero], axis=1), LW - 1, 1)
    two = jnp.concatenate([zero, from_right[...]], axis=1)
    return folded[...] + one + two


def apply_first(
    suby, counts, folded, from_left, from_right, coefs, patch, scalars, basis, before, after,
    direction, image, solved, gather, tiles, flat,
):
    field = folded_columns(folded, from_left, from_right)
    direction[...] = field[OV : OV + CX]
    diagonal = coefs[0]
    faces = [coefs[1 + f] for f in range(4)]
    shape = (PX, LW)
    rows, lanes = rows_of(shape), lanes_of(shape)
    inner = (rows >= 1) & (rows < PX - 1) & (lanes < PY)
    vector = jnp.where(inner, operate(field, diagonal, faces), 0.0)
    image[...] = vector[OV : OV + CX]
    own = own_mask((CX, LW), OV)
    mine = jnp.where(own, vector[OV : OV + CX], 0.0)
    first = patch[OV : OV + CX] * (1.0 / got(scalars, 0))
    cross = total(mine * first)
    square = total(mine * mine)
    local = relax(vector[8:56], diagonal[8:56], [face[8:56] for face in faces])
    solved[...] = jnp.where(own_mask((48, LW), 8), local, 0.0)
    residual = restrict(basis, vector, tiles, flat) * live_of(counts)
    fourth = vector[32:40]
    third = pltpu.roll(vector[24:32], 96, 1)
    for_next = for_before = jnp.zeros((K, 128), f32)
    for t in range(3):
        cols = slice(t * 128, (t + 1) * 128)
        at = 160 + t * K
        for_next = for_next + after[at : at + K, :] * fourth[0:1, cols]
        for_before = for_before + before[at : at + K, :] * third[7:8, cols]
    row = to_row(residual)
    row = row + pltpu.roll(to_row(jnp.sum(for_next, axis=1, keepdims=True)), 32, 1)
    row = row + pltpu.roll(to_row(jnp.sum(for_before, axis=1, keepdims=True)), 64, 1)
    lanes = lanes_of((1, 128))
    row = jnp.where(lanes == SCALARS, cross, jnp.where(lanes == SCALARS + 1, square, row))
    gather[...] = jnp.broadcast_to(row, gather.shape)


def spread_second(
    suby, counts, rows, inverse, basis, solved_first, solved, weights, scalars_in,
    part, scalars, coarse, tiles, flat,
):
    sums = gathered(rows, coarse, suby)
    cross = pick(sums, SCALARS)
    square = pick(sums, SCALARS + 1)
    norm = got(scalars_in, 0)
    unit = got(scalars_in, 1)
    rest = square - 2.0 * cross * cross + cross * cross * unit
    second = jnp.sqrt(jnp.maximum(rest, 0.0) + EPSILON)
    scale = 1.0 / second
    solution = coarse_solve(inverse, coarse) * live_of(counts)
    solution = (solution - cross * weights[:, 0:1]) * scale
    put(scalars, 0, norm)
    put(scalars, 1, unit)
    put(scalars, 2, cross)
    put(scalars, 3, second)
    part[...] = prolong(basis, solution, tiles, flat)
    local = (solved[...] - (cross / norm) * solved_first[...]) * scale
    part[8:56, :] = part[8:56, :] + local


def apply_second(
    folded, from_left, from_right, coefs, patch, image, scalars, direction, third, gather
):
    field = folded_columns(folded, from_left, from_right)
    vector = operate(field, coefs[0, 8:56, :], [coefs[1 + f, 8:56, :] for f in range(4)])
    own = own_mask((CX, LW), OV)
    direction[...] = field[8 : 8 + CX]
    vector = jnp.where(own, vector[8 : 8 + CX], 0.0)
    third[...] = vector
    first = jnp.where(own, patch[OV : OV + CX] * (1.0 / got(scalars, 0)), 0.0)
    second = (image[...] - got(scalars, 2) * first) * (1.0 / got(scalars, 3))
    second = jnp.where(own, second, 0.0)
    lanes = lanes_of((1, 128))
    row = jnp.zeros((1, 128), f32)
    for lane, value in enumerate(
        (first * vector, second * vector, vector * vector, first * second, second * second)
    ):
        row = jnp.where(lanes == lane, total(value), row)
    gather[...] = jnp.broadcast_to(row, gather.shape)


def finish(rows, patch, image, third_image, direction_one, direction_two, scalars, solution, residual):
    sums = jnp.sum(rows[...], axis=0, keepdims=True)
    first_second = pick(sums, 0)
    second_second = pick(sums, 1)
    square = pick(sums, 2)
    cross = pick(sums, 3)
    unit_two = pick(sums, 4)
    source_norm = got(scalars, 0)
    unit = got(scalars, 1)
    first_first = got(scalars, 2)
    second_first = got(scalars, 3)
    rest = square - first_second * first_second * (2.0 - unit)
    rest = rest - second_second * second_second * (2.0 - unit_two)
    rest = rest + 2.0 * first_second * second_second * cross
    third_second = jnp.sqrt(jnp.maximum(rest, 0.0) + EPSILON)
    radius = jnp.sqrt(first_first * first_first + second_first * second_first)
    cosine = first_first / radius
    sine = second_first / radius
    upper_right = cosine * first_second + sine * second_second
    lower_right = cosine * second_second - sine * first_second
    radius_two = jnp.sqrt(lower_right * lower_right + third_second * third_second)
    weight_two = lower_right / radius_two * (-sine * source_norm) / radius_two
    weight_one = (cosine * source_norm - upper_right * weight_two) / radius
    remainder_one = source_norm - first_first * weight_one - first_second * weight_two
    remainder_two = -second_first * weight_one - second_second * weight_two
    remainder_three = -third_second * weight_two
    first = patch[OV : OV + CX] * (1.0 / source_norm)
    second = (image[...] - first_first * first) * (1.0 / second_first)
    third = (third_image[...] - first_second * first - second_second * second) * (1.0 / third_second)
    found = weight_one * direction_one[...] + weight_two * direction_two[...]
    left_over = remainder_one * first + remainder_two * second + remainder_three * third
    solution[...] = pltpu.roll(found, LW - OV, 1)[:, :CY]
    residual[...] = pltpu.roll(left_over, LW - OV, 1)[:, :CY]


def shape_of(*dims):
    return jax.ShapeDtypeStruct(dims, f32)


VMEM = pl.BlockSpec(memory_space=pltpu.VMEM)
SMEM = pl.BlockSpec(memory_space=pltpu.SMEM)
PARAMS = pltpu.CompilerParams(vmem_limit_bytes=24 * 1024 * 1024)


def kernel(body, outs, scratch=(), first_smem=False):
    def call(*args):
        specs = [VMEM] * len(args)
        if first_smem:
            specs[0] = SMEM
        return pl.pallas_call(
            body,
            out_shape=outs,
            in_specs=specs,
            out_specs=[VMEM] * len(outs),
            scratch_shapes=list(scratch),
            compiler_params=PARAMS,
        )(*args)

    return call


def swap(axis, forward, backward):
    count = lax.axis_size(axis)
    before = lax.ppermute(forward, axis, [(i, i + 1) for i in range(count - 1)])
    after = lax.ppermute(backward, axis, [(i + 1, i) for i in range(count - 1)])
    return before, after


def everywhere(rows):
    count = rows.shape[0]
    return lax.all_to_all(rows.reshape(count, 1, 128), AXES, 0, 0).reshape(count, 128)


def on_device(
    source, potential, mobility_along, mobility_across, recombination, counts, basis, coarse_inverse
):
    suby = lax.axis_size("gy")
    devices = lax.axis_size("gx") * suby
    rows = shape_of(devices, 128)
    patch_shape, own_shape = shape_of(PX, LW), shape_of(CX, LW)
    tiles = pltpu.VMEM((3, PX, 128), f32)
    flat = pltpu.VMEM((9, GROUPS, 128), f32)
    coarse = pltpu.VMEM((devices // 4, 128), f32)
    fields = (source, potential, mobility_along, mobility_across, recombination)

    def bind(body):
        def run(*refs):
            return body(suby, *refs)

        return run

    whole = lambda shape: pl.BlockSpec(shape, lambda i: (0,) * len(shape))
    edge = 3 * 128
    last = basis.shape[1] // edge - 1
    ahead, behind = pl.pallas_call(
        pack_rows,
        grid=(1,),
        out_shape=[shape_of(256, 128)] * 2,
        in_specs=[SMEM]
        + [whole((CX, CY))] * 5
        + [pl.BlockSpec((K, edge), lambda i: (0, 0)), pl.BlockSpec((K, edge), lambda i: (0, last))],
        out_specs=[whole((256, 128))] * 2,
        compiler_params=PARAMS,
    )(counts, *fields, basis, basis)
    before, after = swap("gx", ahead, behind)
    strip = shape_of(PX, 128)
    grown, rightward, leftward = kernel(pack_columns, [shape_of(5, PX, CY), strip, strip])(
        *fields, before, after
    )
    from_left, from_right = swap("gy", rightward, leftward)
    patch, coefs, solved_one, row = kernel(
        bind(prepare),
        [patch_shape, shape_of(5, PX, LW), shape_of(48, LW), rows],
        [tiles, flat],
        True,
    )(counts, grown, from_left, from_right, basis)
    part, weights, scalars_one = kernel(
        bind(spread_first),
        [patch_shape, shape_of(K, 128), shape_of(8, 128)],
        [coarse, tiles, flat],
        True,
    )(counts, everywhere(row), coarse_inverse, basis, solved_one)
    over, under = swap("gx", part[PX // 2 :], part[: PX // 2])
    folded, rightward, leftward = kernel(fold_rows, [patch_shape, strip, strip])(part, over, under)
    from_left, from_right = swap("gy", rightward, leftward)
    direction_one, image_one, solved_two, row = kernel(
        bind(apply_first),
        [own_shape, own_shape, shape_of(48, LW), rows],
        [tiles, flat],
        True,
    )(
        counts, folded, from_left, from_right, coefs, patch, scalars_one, basis, before, after
    )
    part, scalars_two = kernel(
        bind(spread_second),
        [patch_shape, shape_of(8, 128)],
        [coarse, tiles, flat],
        True,
    )(
        counts, everywhere(row), coarse_inverse, basis, solved_one, solved_two, weights, scalars_one
    )
    over, under = swap("gx", part[40:], part[:24])
    strip = shape_of(48, 128)
    folded, rightward, leftward = kernel(fold_rows, [shape_of(48, LW), strip, strip])(
        part, over, under
    )
    from_left, from_right = swap("gy", rightward, leftward)
    direction_two, image_two, row = kernel(apply_second, [own_shape, own_shape, rows])(
        folded, from_left, from_right, coefs, patch, image_one, scalars_two
    )
    out = shape_of(CX, CY)
    answer, residual = kernel(finish, [out, out])(
        everywhere(row), patch, image_one, image_two, direction_one, direction_two, scalars_two
    )
    return answer, residual


def solution(mesh):
    grid = P("gx", "gy")
    return jax.shard_map(
        on_device,
        mesh=mesh,
        in_specs=(grid,) * 7 + (P(("gx", "gy"), None),),
        out_specs=(grid, grid),
        check_vma=False,
    )
```

```python
import jax
import jax.numpy as jnp
from jax import lax
from jax.experimental import pallas as pl
from jax.experimental.pallas import tpu as pltpu
from jax.sharding import PartitionSpec as P

OV = 16
SWEEPS = 8
OMEGA = 0.8
EPSILON = 1e-06
CX = 32
CY = 256
K = 32
PX = CX + 2 * OV
PY = CY + 2 * OV
LW = 384
GROUPS = PX // 4
STRIP = 24
SCALARS = 96
f32 = jnp.float32
AXES = ("gx", "gy")


def lanes_of(shape):
    return lax.broadcasted_iota(jnp.int32, shape, len(shape) - 1)


def rows_of(shape):
    return lax.broadcasted_iota(jnp.int32, shape, len(shape) - 2)


def left(x):
    return pltpu.roll(x, LW - 1, 1)


def right(x):
    return pltpu.roll(x, 1, 1)


def up(x):
    return pltpu.roll(x, x.shape[0] - 1, 0)


def down(x):
    return pltpu.roll(x, 1, 0)


def own_mask(shape, first):
    rows, lanes = rows_of(shape) + first, lanes_of(shape)
    return (rows >= OV) & (rows < OV + CX) & (lanes >= OV) & (lanes < OV + CY)


def total(x):
    return jnp.sum(jnp.sum(x, axis=0, keepdims=True), axis=1, keepdims=True)


def to_row(column):
    shape = (K, 128)
    spread = jnp.broadcast_to(column, shape)
    return jnp.sum(jnp.where(rows_of(shape) == lanes_of(shape), spread, 0.0), axis=0, keepdims=True)


def restrict(basis, patch, tiles, flat):
    for t in range(3):
        tiles[t] = patch[:, t * 128 : (t + 1) * 128]
    parts = [None] * 9
    for m in range(4):
        rows = jnp.concatenate(
            [tiles[t, pl.ds(m, GROUPS, stride=4), :] for t in range(3)], axis=1
        )
        if m:
            rows = pltpu.roll(rows, 32 * m, 1)
        for t in range(3):
            piece = rows[:, t * 128 : (t + 1) * 128]
            at = 2 * m + t
            parts[at] = piece if parts[at] is None else parts[at] + piece
    for t in range(9):
        flat[t] = parts[t]
    sums = [jnp.zeros((K, 128), f32) for _ in range(3)]
    for g in range(GROUPS):
        for t in range(9):
            block = (g * 9 + t) * 128
            row = jnp.broadcast_to(flat[t, pl.ds(g, 1), :], (K, 128))
            sums[t % 3] = sums[t % 3] + basis[:, block : block + 128] * row
    return jnp.sum(sums[0] + sums[1] + sums[2], axis=1, keepdims=True)


def prolong(basis, weights, tiles, flat):
    wide = jnp.broadcast_to(weights, (K, 128))
    for g in range(GROUPS):
        for t in range(9):
            block = (g * 9 + t) * 128
            flat[t, pl.ds(g, 1), :] = jnp.sum(
                basis[:, block : block + 128] * wide, axis=0, keepdims=True
            )
    for m in range(4):
        rows = jnp.concatenate([flat[2 * m + t] for t in range(3)], axis=1)
        if m:
            rows = pltpu.roll(rows, LW - 32 * m, 1)
        rows = jnp.where(lanes_of(rows.shape) < PY, rows, 0.0)
        for t in range(3):
            tiles[t, pl.ds(m, GROUPS, stride=4), :] = rows[:, t * 128 : (t + 1) * 128]
    return jnp.concatenate([tiles[t] for t in range(3)], axis=1)


def gathered(rows, coarse, suby):
    count = rows.shape[0] // 4
    shift = suby // 4
    taken = [rows[pl.ds(q, count, stride=4), :] for q in range(4)]
    zero = jnp.zeros((shift, 128), f32)
    lanes = lanes_of((count, 128))
    result = None
    for s in range(4):
        own = taken[s]
        later = jnp.concatenate([zero, taken[(s + 1) % 4][: count - shift]], axis=0)
        earlier = jnp.concatenate([taken[(s + 2) % 4][shift:], zero], axis=0)
        piece = jnp.where(
            lanes < 32, own, jnp.where(lanes < 64, later, jnp.where(lanes < 96, earlier, 0.0))
        )
        if s:
            piece = pltpu.roll(piece, 32 * s, 1)
        result = piece if result is None else result + piece
    coarse[...] = result
    return jnp.sum(taken[0] + taken[1] + (taken[2] + taken[3]), axis=0, keepdims=True)


def pick(row, lane):
    return jnp.sum(jnp.where(lanes_of(row.shape) == lane, row, 0.0), axis=1, keepdims=True)


def coarse_solve(inverse, coarse):
    sums = [jnp.zeros((K, 128), f32) for _ in range(4)]
    for b in range(coarse.shape[0]):
        row = jnp.broadcast_to(coarse[pl.ds(b, 1), :], (K, 128))
        sums[b % 4] = sums[b % 4] + inverse[:, b * 128 : (b + 1) * 128] * row
    return jnp.sum((sums[0] + sums[1]) + (sums[2] + sums[3]), axis=1, keepdims=True)


def live_of(counts):
    return (rows_of((K, 1)) < counts[0, 0]).astype(f32)


def relax(vector, diagonal, faces):
    inverse = OMEGA / jnp.where(diagonal > 0.0, diagonal, 1.0)
    below, above, east, west = [inverse * face for face in faces]
    start = inverse * vector
    field = start
    for _ in range(SWEEPS - 1):
        moved = below * up(field) + above * down(field)
        moved = moved + (east * left(field) + west * right(field))
        field = (start + (1.0 - OMEGA) * field) + moved
    return field


def operate(field, diagonal, faces):
    below, above, east, west = faces
    moved = below * up(field) + above * down(field)
    moved = moved + (east * left(field) + west * right(field))
    return diagonal * field - moved


def pack_rows(
    counts, source, potential, along, across, recombination, basis, held, ahead, behind,
    head, tail, sems,
):
    edge = head.shape[1]
    copies = [
        pltpu.make_async_copy(field, held.at[f], sems.at[f])
        for f, field in enumerate((source, potential, along, across, recombination))
    ]
    copies.append(pltpu.make_async_copy(basis.at[:, :edge], head, sems.at[5]))
    copies.append(
        pltpu.make_async_copy(basis.at[:, basis.shape[1] - edge :], tail, sems.at[6])
    )
    for copy in copies:
        copy.start()
    live = live_of(counts)
    for copy in copies:
        copy.wait()
    for f in range(5):
        for t in range(2):
            at = (2 * f + t) * OV
            cols = slice(t * 128, (t + 1) * 128)
            ahead[at : at + OV, :] = held[f, CX - OV :, cols]
            behind[at : at + OV, :] = held[f, :OV, cols]
    for t in range(3):
        at = 160 + t * K
        cols = slice(t * 128, (t + 1) * 128)
        ahead[at : at + K, :] = tail[:, cols] * live
        behind[at : at + K, :] = head[:, cols] * live


def pack_columns(held, before, after, rows, rightward, leftward):
    lanes = lanes_of((PX, 128))
    to_right = to_left = None
    for f in range(5):
        tiles = []
        for t in range(2):
            at = (2 * f + t) * OV
            cols = slice(t * 128, (t + 1) * 128)
            tile = jnp.concatenate(
                [before[at : at + OV, :], held[f, :, cols], after[at : at + OV, :]], axis=0
            )
            rows[f, :, cols] = tile
            tiles.append(tile)
        last = pltpu.roll(jnp.where(lanes >= 111, tiles[1], 0.0), 17 + STRIP * f, 1)
        first = jnp.where(lanes < 17, tiles[0], 0.0)
        if f:
            first = pltpu.roll(first, STRIP * f, 1)
        to_right = last if f == 0 else to_right + last
        to_left = first if f == 0 else to_left + first
    rightward[...] = to_right
    leftward[...] = to_left


def prepare(suby, counts, rows, from_left, from_right, basis, patch, coefs, solved, gather, tiles, flat):
    zero = jnp.zeros((PX, LW - CY), f32)
    lanes = lanes_of((PX, 128))
    fields = []
    for f in range(5):
        middle = pltpu.roll(jnp.concatenate([rows[f], zero], axis=1), OV, 1)
        band = (lanes >= STRIP * f) & (lanes < STRIP * f + 17)
        wide = jnp.zeros((PX, LW - 128), f32)
        one = jnp.concatenate([jnp.where(band, from_left[...], 0.0), wide], axis=1)
        two = jnp.concatenate([jnp.where(band, from_right[...], 0.0), wide], axis=1)
        one = pltpu.roll(one, LW - 1 - STRIP * f, 1)
        two = pltpu.roll(two, OV + CY - STRIP * f, 1)
        fields.append(middle + one + two)
    source, potential, along, across, recombination = fields
    weight = jnp.sqrt(along * up(along))
    rise = 0.5 * (up(potential) - potential)
    below = weight * jnp.exp(rise)
    above = weight * jnp.exp(-rise)
    diagonal = recombination + above + down(below)
    weight = jnp.sqrt(across * left(across))
    rise = 0.5 * (left(potential) - potential)
    east = weight * jnp.exp(rise)
    west = weight * jnp.exp(-rise)
    diagonal = diagonal + west + right(east)
    faces = (below, down(above), east, right(west))
    coefs[0] = diagonal
    for f in range(4):
        coefs[1 + f] = faces[f]
    source = jnp.where(lanes_of((PX, LW)) < PY, source, 0.0)
    patch[...] = source
    own = own_mask((PX, LW), 0)
    square = total(jnp.where(own, source * source, 0.0))
    local = relax(source[8:56], diagonal[8:56], [face[8:56] for face in faces])
    solved[...] = jnp.where(own_mask((48, LW), 8), local, 0.0)
    residual = restrict(basis, source, tiles, flat) * live_of(counts)
    row = to_row(residual)
    row = jnp.where(lanes_of((1, 128)) == SCALARS, square, row)
    gather[...] = jnp.broadcast_to(row, gather.shape)


def put(scalars, at, value):
    scalars[pl.ds(at, 1), :] = jnp.broadcast_to(value, (1, 128))


def got(scalars, at):
    return scalars[pl.ds(at, 1), :][:, 0:1]


def spread_first(
    suby, counts, rows, inverse, basis, solved, part, weights, scalars, coarse, tiles, flat
):
    sums = gathered(rows, coarse, suby)
    square = pick(sums, SCALARS)
    norm = jnp.sqrt(square + EPSILON)
    scale = 1.0 / norm
    solution = coarse_solve(inverse, coarse) * live_of(counts) * scale
    weights[...] = jnp.broadcast_to(solution, (K, 128))
    put(scalars, 0, norm)
    put(scalars, 1, square / (square + EPSILON))
    part[...] = prolong(basis, solution, tiles, flat)
    part[8:56, :] = part[8:56, :] + solved[...] * scale


def fold_rows(part, before, after, folded, rightward, leftward):
    height = folded.shape[0]
    first = (PX - height) // 2
    half = height // 2
    whole = part[first : first + height, :] + jnp.concatenate(
        [before[PX // 2 - half :, :] if before.shape[0] > half else before[...],
         after[:half, :] if after.shape[0] > half else after[...]],
        axis=0,
    )
    folded[...] = whole
    lanes = lanes_of((height, 128))
    moved = pltpu.roll(whole, LW - 255, 1)
    rightward[...] = jnp.where(lanes < 33, moved[:, :128], 0.0)
    leftward[...] = jnp.where(lanes < 33, whole[:, :128], 0.0)


def folded_columns(folded, from_left, from_right):
    height = folded.shape[0]
    zero = jnp.zeros((height, 256), f32)
    one = pltpu.roll(jnp.concatenate([from_left[...], zero], axis=1), LW - 1, 1)
    two = jnp.concatenate([zero, from_right[...]], axis=1)
    return folded[...] + one + two


def apply_first(
    suby, counts, folded, from_left, from_right, coefs, patch, scalars, basis, before, after,
    direction, image, solved, gather, tiles, flat,
):
    field = folded_columns(folded, from_left, from_right)
    direction[...] = field[OV : OV + CX]
    diagonal = coefs[0]
    faces = [coefs[1 + f] for f in range(4)]
    shape = (PX, LW)
    rows, lanes = rows_of(shape), lanes_of(shape)
    inner = (rows >= 1) & (rows < PX - 1) & (lanes < PY)
    vector = jnp.where(inner, operate(field, diagonal, faces), 0.0)
    image[...] = vector[OV : OV + CX]
    own = own_mask((CX, LW), OV)
    mine = jnp.where(own, vector[OV : OV + CX], 0.0)
    first = patch[OV : OV + CX] * (1.0 / got(scalars, 0))
    cross = total(mine * first)
    square = total(mine * mine)
    local = relax(vector[8:56], diagonal[8:56], [face[8:56] for face in faces])
    solved[...] = jnp.where(own_mask((48, LW), 8), local, 0.0)
    residual = restrict(basis, vector, tiles, flat) * live_of(counts)
    fourth = vector[32:40]
    third = pltpu.roll(vector[24:32], 96, 1)
    for_next = for_before = jnp.zeros((K, 128), f32)
    for t in range(3):
        cols = slice(t * 128, (t + 1) * 128)
        at = 160 + t * K
        for_next = for_next + after[at : at + K, :] * fourth[0:1, cols]
        for_before = for_before + before[at : at + K, :] * third[7:8, cols]
    row = to_row(residual)
    row = row + pltpu.roll(to_row(jnp.sum(for_next, axis=1, keepdims=True)), 32, 1)
    row = row + pltpu.roll(to_row(jnp.sum(for_before, axis=1, keepdims=True)), 64, 1)
    lanes = lanes_of((1, 128))
    row = jnp.where(lanes == SCALARS, cross, jnp.where(lanes == SCALARS + 1, square, row))
    gather[...] = jnp.broadcast_to(row, gather.shape)


def spread_second(
    suby, counts, rows, inverse, basis, solved_first, solved, weights, scalars_in,
    part, scalars, coarse, tiles, flat,
):
    sums = gathered(rows, coarse, suby)
    cross = pick(sums, SCALARS)
    square = pick(sums, SCALARS + 1)
    norm = got(scalars_in, 0)
    unit = got(scalars_in, 1)
    rest = square - 2.0 * cross * cross + cross * cross * unit
    second = jnp.sqrt(jnp.maximum(rest, 0.0) + EPSILON)
    scale = 1.0 / second
    solution = coarse_solve(inverse, coarse) * live_of(counts)
    solution = (solution - cross * weights[:, 0:1]) * scale
    put(scalars, 0, norm)
    put(scalars, 1, unit)
    put(scalars, 2, cross)
    put(scalars, 3, second)
    part[...] = prolong(basis, solution, tiles, flat)
    local = (solved[...] - (cross / norm) * solved_first[...]) * scale
    part[8:56, :] = part[8:56, :] + local


def apply_second(
    folded, from_left, from_right, coefs, patch, image, scalars, direction, third, gather
):
    field = folded_columns(folded, from_left, from_right)
    vector = operate(field, coefs[0, 8:56, :], [coefs[1 + f, 8:56, :] for f in range(4)])
    own = own_mask((CX, LW), OV)
    direction[...] = field[8 : 8 + CX]
    vector = jnp.where(own, vector[8 : 8 + CX], 0.0)
    third[...] = vector
    first = jnp.where(own, patch[OV : OV + CX] * (1.0 / got(scalars, 0)), 0.0)
    second = (image[...] - got(scalars, 2) * first) * (1.0 / got(scalars, 3))
    second = jnp.where(own, second, 0.0)
    lanes = lanes_of((1, 128))
    row = jnp.zeros((1, 128), f32)
    for lane, value in enumerate(
        (first * vector, second * vector, vector * vector, first * second, second * second)
    ):
        row = jnp.where(lanes == lane, total(value), row)
    gather[...] = jnp.broadcast_to(row, gather.shape)


def add_rows(rows, gather):
    row = jnp.sum(rows[...], axis=0, keepdims=True)
    gather[...] = jnp.broadcast_to(row, gather.shape)


def finish(rows, patch, image, third_image, direction_one, direction_two, scalars, solution, residual):
    sums = jnp.sum(rows[...], axis=0, keepdims=True)
    first_second = pick(sums, 0)
    second_second = pick(sums, 1)
    square = pick(sums, 2)
    cross = pick(sums, 3)
    unit_two = pick(sums, 4)
    source_norm = got(scalars, 0)
    unit = got(scalars, 1)
    first_first = got(scalars, 2)
    second_first = got(scalars, 3)
    rest = square - first_second * first_second * (2.0 - unit)
    rest = rest - second_second * second_second * (2.0 - unit_two)
    rest = rest + 2.0 * first_second * second_second * cross
    third_second = jnp.sqrt(jnp.maximum(rest, 0.0) + EPSILON)
    radius = jnp.sqrt(first_first * first_first + second_first * second_first)
    cosine = first_first / radius
    sine = second_first / radius
    upper_right = cosine * first_second + sine * second_second
    lower_right = cosine * second_second - sine * first_second
    radius_two = jnp.sqrt(lower_right * lower_right + third_second * third_second)
    weight_two = lower_right / radius_two * (-sine * source_norm) / radius_two
    weight_one = (cosine * source_norm - upper_right * weight_two) / radius
    remainder_one = source_norm - first_first * weight_one - first_second * weight_two
    remainder_two = -second_first * weight_one - second_second * weight_two
    remainder_three = -third_second * weight_two
    first = patch[OV : OV + CX] * (1.0 / source_norm)
    second = (image[...] - first_first * first) * (1.0 / second_first)
    third = (third_image[...] - first_second * first - second_second * second) * (1.0 / third_second)
    found = weight_one * direction_one[...] + weight_two * direction_two[...]
    left_over = remainder_one * first + remainder_two * second + remainder_three * third
    solution[...] = pltpu.roll(found, LW - OV, 1)[:, :CY]
    residual[...] = pltpu.roll(left_over, LW - OV, 1)[:, :CY]


def shape_of(*dims):
    return jax.ShapeDtypeStruct(dims, f32)


VMEM = pl.BlockSpec(memory_space=pltpu.VMEM)
SMEM = pl.BlockSpec(memory_space=pltpu.SMEM)
PARAMS = pltpu.CompilerParams(vmem_limit_bytes=24 * 1024 * 1024)


def kernel(body, outs, scratch=(), first_smem=False):
    def call(*args):
        specs = [VMEM] * len(args)
        if first_smem:
            specs[0] = SMEM
        return pl.pallas_call(
            body,
            out_shape=outs,
            in_specs=specs,
            out_specs=[VMEM] * len(outs),
            scratch_shapes=list(scratch),
            compiler_params=PARAMS,
        )(*args)

    return call


def swap(axis, forward, backward):
    count = lax.axis_size(axis)
    before = lax.ppermute(forward, axis, [(i, i + 1) for i in range(count - 1)])
    after = lax.ppermute(backward, axis, [(i + 1, i) for i in range(count - 1)])
    return before, after


def everywhere(rows, axes=AXES):
    count = rows.shape[0]
    return lax.all_to_all(rows.reshape(count, 1, 128), axes, 0, 0).reshape(count, 128)


def on_device(
    source, potential, mobility_along, mobility_across, recombination, counts, basis, coarse_inverse
):
    suby = lax.axis_size("gy")
    devices = lax.axis_size("gx") * suby
    rows = shape_of(devices, 128)
    patch_shape, own_shape = shape_of(PX, LW), shape_of(CX, LW)
    tiles = pltpu.VMEM((3, PX, 128), f32)
    flat = pltpu.VMEM((9, GROUPS, 128), f32)
    coarse = pltpu.VMEM((devices // 4, 128), f32)
    fields = (source, potential, mobility_along, mobility_across, recombination)

    def bind(body):
        def run(*refs):
            return body(suby, *refs)

        return run

    edge = pltpu.VMEM((K, 3 * 128), f32)
    held, ahead, behind = pl.pallas_call(
        pack_rows,
        out_shape=[shape_of(5, CX, CY), shape_of(256, 128), shape_of(256, 128)],
        in_specs=[SMEM] + [pl.BlockSpec(memory_space=pltpu.HBM)] * 6,
        out_specs=[VMEM] * 3,
        scratch_shapes=[edge, edge, pltpu.SemaphoreType.DMA((7,))],
        compiler_params=PARAMS,
    )(counts, *[pltpu.with_memory_space_constraint(x, pltpu.HBM) for x in (*fields, basis)])
    before, after = swap("gx", ahead, behind)
    strip = shape_of(PX, 128)
    grown, rightward, leftward = kernel(pack_columns, [shape_of(5, PX, CY), strip, strip])(
        held, before, after
    )
    from_left, from_right = swap("gy", rightward, leftward)
    patch, coefs, solved_one, row = kernel(
        bind(prepare),
        [patch_shape, shape_of(5, PX, LW), shape_of(48, LW), rows],
        [tiles, flat],
        True,
    )(counts, grown, from_left, from_right, basis)
    part, weights, scalars_one = kernel(
        bind(spread_first),
        [patch_shape, shape_of(K, 128), shape_of(8, 128)],
        [coarse, tiles, flat],
        True,
    )(counts, everywhere(row), coarse_inverse, basis, solved_one)
    over, under = swap("gx", part[PX // 2 :], part[: PX // 2])
    folded, rightward, leftward = kernel(fold_rows, [patch_shape, strip, strip])(part, over, under)
    from_left, from_right = swap("gy", rightward, leftward)
    direction_one, image_one, solved_two, row = kernel(
        bind(apply_first),
        [own_shape, own_shape, shape_of(48, LW), rows],
        [tiles, flat],
        True,
    )(
        counts, folded, from_left, from_right, coefs, patch, scalars_one, basis, before, after
    )
    part, scalars_two = kernel(
        bind(spread_second),
        [patch_shape, shape_of(8, 128)],
        [coarse, tiles, flat],
        True,
    )(
        counts, everywhere(row), coarse_inverse, basis, solved_one, solved_two, weights, scalars_one
    )
    over, under = swap("gx", part[40:], part[:24])
    strip = shape_of(48, 128)
    folded, rightward, leftward = kernel(fold_rows, [shape_of(48, LW), strip, strip])(
        part, over, under
    )
    from_left, from_right = swap("gy", rightward, leftward)
    direction_two, image_two, row = kernel(
        apply_second, [own_shape, own_shape, shape_of(devices // suby, 128)]
    )(
        folded, from_left, from_right, coefs, patch, image_one, scalars_two
    )
    (row,) = kernel(add_rows, [shape_of(suby, 128)])(everywhere(row, "gx"))
    out = shape_of(CX, CY)
    answer, residual = kernel(finish, [out, out])(
        everywhere(row, "gy"), patch, image_one, image_two, direction_one, direction_two, scalars_two
    )
    return answer, residual


def solution(mesh):
    grid = P("gx", "gy")
    return jax.shard_map(
        on_device,
        mesh=mesh,
        in_specs=(grid,) * 7 + (P(("gx", "gy"), None),),
        out_specs=(grid, grid),
        check_vma=False,
    )
```

```python
import jax
import jax.numpy as jnp
from jax import lax
from jax.experimental import pallas as pl
from jax.experimental.pallas import tpu as pltpu
from jax.sharding import PartitionSpec as P

OV = 16
SWEEPS = 8
OMEGA = 0.8
EPSILON = 1e-06
CX = 32
CY = 256
K = 32
PX = CX + 2 * OV
PY = CY + 2 * OV
LW = 384
GROUPS = PX // 4
STRIP = 24
SCALARS = 96
f32 = jnp.float32
AXES = ("gx", "gy")


def lanes_of(shape):
    return lax.broadcasted_iota(jnp.int32, shape, len(shape) - 1)


def rows_of(shape):
    return lax.broadcasted_iota(jnp.int32, shape, len(shape) - 2)


def left(x):
    return pltpu.roll(x, LW - 1, 1)


def right(x):
    return pltpu.roll(x, 1, 1)


def up(x):
    return pltpu.roll(x, x.shape[0] - 1, 0)


def down(x):
    return pltpu.roll(x, 1, 0)


def own_mask(shape, first):
    rows, lanes = rows_of(shape) + first, lanes_of(shape)
    return (rows >= OV) & (rows < OV + CX) & (lanes >= OV) & (lanes < OV + CY)


def is_even():
    return lax.rem(lax.axis_index("gy"), 2) == 0


def to_pairs(rightward, leftward):
    even = is_even()
    return jnp.where(even, leftward, rightward), jnp.where(even, rightward, leftward)


def from_pairs(odd, even_pairs):
    even = is_even()
    return jnp.where(even, odd, even_pairs), jnp.where(even, even_pairs, odd)


def total(x):
    return jnp.sum(jnp.sum(x, axis=0, keepdims=True), axis=1, keepdims=True)


def to_row(column):
    shape = (K, 128)
    spread = jnp.broadcast_to(column, shape)
    return jnp.sum(jnp.where(rows_of(shape) == lanes_of(shape), spread, 0.0), axis=0, keepdims=True)


def restrict(basis, patch, tiles, flat):
    for t in range(3):
        tiles[t] = patch[:, t * 128 : (t + 1) * 128]
    parts = [None] * 9
    for m in range(4):
        rows = jnp.concatenate(
            [tiles[t, pl.ds(m, GROUPS, stride=4), :] for t in range(3)], axis=1
        )
        if m:
            rows = pltpu.roll(rows, 32 * m, 1)
        for t in range(3):
            piece = rows[:, t * 128 : (t + 1) * 128]
            at = 2 * m + t
            parts[at] = piece if parts[at] is None else parts[at] + piece
    for t in range(9):
        flat[t] = parts[t]
    sums = [jnp.zeros((K, 128), f32) for _ in range(3)]
    for g in range(GROUPS):
        for t in range(9):
            block = (g * 9 + t) * 128
            row = jnp.broadcast_to(flat[t, pl.ds(g, 1), :], (K, 128))
            sums[t % 3] = sums[t % 3] + basis[:, block : block + 128] * row
    return jnp.sum(sums[0] + sums[1] + sums[2], axis=1, keepdims=True)


def prolong(basis, weights, tiles, flat):
    wide = jnp.broadcast_to(weights, (K, 128))
    for g in range(GROUPS):
        for t in range(9):
            block = (g * 9 + t) * 128
            flat[t, pl.ds(g, 1), :] = jnp.sum(
                basis[:, block : block + 128] * wide, axis=0, keepdims=True
            )
    for m in range(4):
        rows = jnp.concatenate([flat[2 * m + t] for t in range(3)], axis=1)
        if m:
            rows = pltpu.roll(rows, LW - 32 * m, 1)
        rows = jnp.where(lanes_of(rows.shape) < PY, rows, 0.0)
        for t in range(3):
            tiles[t, pl.ds(m, GROUPS, stride=4), :] = rows[:, t * 128 : (t + 1) * 128]
    return jnp.concatenate([tiles[t] for t in range(3)], axis=1)


def gathered(rows, coarse, suby):
    count = rows.shape[0] // 4
    shift = suby // 4
    taken = [rows[pl.ds(q, count, stride=4), :] for q in range(4)]
    zero = jnp.zeros((shift, 128), f32)
    lanes = lanes_of((count, 128))
    result = None
    for s in range(4):
        own = taken[s]
        later = jnp.concatenate([zero, taken[(s + 1) % 4][: count - shift]], axis=0)
        earlier = jnp.concatenate([taken[(s + 2) % 4][shift:], zero], axis=0)
        piece = jnp.where(
            lanes < 32, own, jnp.where(lanes < 64, later, jnp.where(lanes < 96, earlier, 0.0))
        )
        if s:
            piece = pltpu.roll(piece, 32 * s, 1)
        result = piece if result is None else result + piece
    coarse[...] = result
    return jnp.sum(taken[0] + taken[1] + (taken[2] + taken[3]), axis=0, keepdims=True)


def pick(row, lane):
    return jnp.sum(jnp.where(lanes_of(row.shape) == lane, row, 0.0), axis=1, keepdims=True)


def coarse_solve(inverse, coarse):
    sums = [jnp.zeros((K, 128), f32) for _ in range(4)]
    for b in range(coarse.shape[0]):
        row = jnp.broadcast_to(coarse[pl.ds(b, 1), :], (K, 128))
        sums[b % 4] = sums[b % 4] + inverse[:, b * 128 : (b + 1) * 128] * row
    return jnp.sum((sums[0] + sums[1]) + (sums[2] + sums[3]), axis=1, keepdims=True)


def live_of(counts):
    return (rows_of((K, 1)) < counts[0, 0]).astype(f32)


def relax(vector, diagonal, faces):
    inverse = OMEGA / jnp.where(diagonal > 0.0, diagonal, 1.0)
    below, above, east, west = [inverse * face for face in faces]
    start = inverse * vector
    field = start
    for _ in range(SWEEPS - 1):
        moved = below * up(field) + above * down(field)
        moved = moved + (east * left(field) + west * right(field))
        field = (start + (1.0 - OMEGA) * field) + moved
    return field


def operate(field, diagonal, faces):
    below, above, east, west = faces
    moved = below * up(field) + above * down(field)
    moved = moved + (east * left(field) + west * right(field))
    return diagonal * field - moved


def pack_rows(
    counts, source, potential, along, across, recombination, basis, held, ahead, behind,
    head, tail, sems,
):
    edge = head.shape[1]
    copies = [
        pltpu.make_async_copy(field, held.at[f], sems.at[f])
        for f, field in enumerate((source, potential, along, across, recombination))
    ]
    copies.append(pltpu.make_async_copy(basis.at[:, :edge], head, sems.at[5]))
    copies.append(
        pltpu.make_async_copy(basis.at[:, basis.shape[1] - edge :], tail, sems.at[6])
    )
    for copy in copies:
        copy.start()
    live = live_of(counts)
    for copy in copies:
        copy.wait()
    for f in range(5):
        for t in range(2):
            at = (2 * f + t) * OV
            cols = slice(t * 128, (t + 1) * 128)
            ahead[at : at + OV, :] = held[f, CX - OV :, cols]
            behind[at : at + OV, :] = held[f, :OV, cols]
    for t in range(3):
        at = 160 + t * K
        cols = slice(t * 128, (t + 1) * 128)
        ahead[at : at + K, :] = tail[:, cols] * live
        behind[at : at + K, :] = head[:, cols] * live


def pack_columns(held, before, after, rows, odd, even):
    lanes = lanes_of((PX, 128))
    to_right = to_left = None
    for f in range(5):
        tiles = []
        for t in range(2):
            at = (2 * f + t) * OV
            cols = slice(t * 128, (t + 1) * 128)
            tile = jnp.concatenate(
                [before[at : at + OV, :], held[f, :, cols], after[at : at + OV, :]], axis=0
            )
            rows[f, :, cols] = tile
            tiles.append(tile)
        last = pltpu.roll(jnp.where(lanes >= 111, tiles[1], 0.0), 17 + STRIP * f, 1)
        first = jnp.where(lanes < 17, tiles[0], 0.0)
        if f:
            first = pltpu.roll(first, STRIP * f, 1)
        to_right = last if f == 0 else to_right + last
        to_left = first if f == 0 else to_left + first
    odd[...], even[...] = to_pairs(to_right, to_left)


def prepare(suby, counts, rows, odd, even, basis, patch, coefs, solved, gather, tiles, flat):
    zero = jnp.zeros((PX, LW - CY), f32)
    lanes = lanes_of((PX, 128))
    from_left, from_right = from_pairs(odd[...], even[...])
    fields = []
    for f in range(5):
        middle = pltpu.roll(jnp.concatenate([rows[f], zero], axis=1), OV, 1)
        band = (lanes >= STRIP * f) & (lanes < STRIP * f + 17)
        wide = jnp.zeros((PX, LW - 128), f32)
        one = jnp.concatenate([jnp.where(band, from_left, 0.0), wide], axis=1)
        two = jnp.concatenate([jnp.where(band, from_right, 0.0), wide], axis=1)
        one = pltpu.roll(one, LW - 1 - STRIP * f, 1)
        two = pltpu.roll(two, OV + CY - STRIP * f, 1)
        fields.append(middle + one + two)
    source, potential, along, across, recombination = fields
    weight = jnp.sqrt(along * up(along))
    rise = 0.5 * (up(potential) - potential)
    below = weight * jnp.exp(rise)
    above = weight * jnp.exp(-rise)
    diagonal = recombination + above + down(below)
    weight = jnp.sqrt(across * left(across))
    rise = 0.5 * (left(potential) - potential)
    east = weight * jnp.exp(rise)
    west = weight * jnp.exp(-rise)
    diagonal = diagonal + west + right(east)
    faces = (below, down(above), east, right(west))
    coefs[0] = diagonal
    for f in range(4):
        coefs[1 + f] = faces[f]
    source = jnp.where(lanes_of((PX, LW)) < PY, source, 0.0)
    patch[...] = source
    own = own_mask((PX, LW), 0)
    square = total(jnp.where(own, source * source, 0.0))
    local = relax(source[8:56], diagonal[8:56], [face[8:56] for face in faces])
    solved[...] = jnp.where(own_mask((48, LW), 8), local, 0.0)
    residual = restrict(basis, source, tiles, flat) * live_of(counts)
    row = to_row(residual)
    row = jnp.where(lanes_of((1, 128)) == SCALARS, square, row)
    gather[...] = jnp.broadcast_to(row, gather.shape)


def put(scalars, at, value):
    scalars[pl.ds(at, 1), :] = jnp.broadcast_to(value, (1, 128))


def got(scalars, at):
    return scalars[pl.ds(at, 1), :][:, 0:1]


def spread_first(
    suby, counts, rows, inverse, basis, solved, part, weights, scalars, coarse, tiles, flat
):
    sums = gathered(rows, coarse, suby)
    square = pick(sums, SCALARS)
    norm = jnp.sqrt(square + EPSILON)
    scale = 1.0 / norm
    solution = coarse_solve(inverse, coarse) * live_of(counts) * scale
    weights[...] = jnp.broadcast_to(solution, (K, 128))
    put(scalars, 0, norm)
    put(scalars, 1, square / (square + EPSILON))
    part[...] = prolong(basis, solution, tiles, flat)
    part[8:56, :] = part[8:56, :] + solved[...] * scale


def fold_rows(part, before, after, folded, odd, even):
    height = folded.shape[0]
    first = (PX - height) // 2
    half = height // 2
    whole = part[first : first + height, :] + jnp.concatenate(
        [before[PX // 2 - half :, :] if before.shape[0] > half else before[...],
         after[:half, :] if after.shape[0] > half else after[...]],
        axis=0,
    )
    folded[...] = whole
    lanes = lanes_of((height, 128))
    moved = pltpu.roll(whole, LW - 255, 1)
    odd[...], even[...] = to_pairs(
        jnp.where(lanes < 33, moved[:, :128], 0.0), jnp.where(lanes < 33, whole[:, :128], 0.0)
    )


def folded_columns(folded, odd, even):
    height = folded.shape[0]
    zero = jnp.zeros((height, 256), f32)
    from_left, from_right = from_pairs(odd[...], even[...])
    one = pltpu.roll(jnp.concatenate([from_left, zero], axis=1), LW - 1, 1)
    two = jnp.concatenate([zero, from_right], axis=1)
    return folded[...] + one + two


def apply_first(
    suby, counts, folded, odd, even, coefs, patch, scalars, basis, before, after,
    direction, image, solved, gather, tiles, flat,
):
    field = folded_columns(folded, odd, even)
    direction[...] = field[OV : OV + CX]
    diagonal = coefs[0]
    faces = [coefs[1 + f] for f in range(4)]
    shape = (PX, LW)
    rows, lanes = rows_of(shape), lanes_of(shape)
    inner = (rows >= 1) & (rows < PX - 1) & (lanes < PY)
    vector = jnp.where(inner, operate(field, diagonal, faces), 0.0)
    image[...] = vector[OV : OV + CX]
    own = own_mask((CX, LW), OV)
    mine = jnp.where(own, vector[OV : OV + CX], 0.0)
    first = patch[OV : OV + CX] * (1.0 / got(scalars, 0))
    cross = total(mine * first)
    square = total(mine * mine)
    local = relax(vector[8:56], diagonal[8:56], [face[8:56] for face in faces])
    solved[...] = jnp.where(own_mask((48, LW), 8), local, 0.0)
    residual = restrict(basis, vector, tiles, flat) * live_of(counts)
    fourth = vector[32:40]
    third = pltpu.roll(vector[24:32], 96, 1)
    for_next = for_before = jnp.zeros((K, 128), f32)
    for t in range(3):
        cols = slice(t * 128, (t + 1) * 128)
        at = 160 + t * K
        for_next = for_next + after[at : at + K, :] * fourth[0:1, cols]
        for_before = for_before + before[at : at + K, :] * third[7:8, cols]
    row = to_row(residual)
    row = row + pltpu.roll(to_row(jnp.sum(for_next, axis=1, keepdims=True)), 32, 1)
    row = row + pltpu.roll(to_row(jnp.sum(for_before, axis=1, keepdims=True)), 64, 1)
    lanes = lanes_of((1, 128))
    row = jnp.where(lanes == SCALARS, cross, jnp.where(lanes == SCALARS + 1, square, row))
    gather[...] = jnp.broadcast_to(row, gather.shape)


def spread_second(
    suby, counts, rows, inverse, basis, solved_first, solved, weights, scalars_in,
    part, scalars, coarse, tiles, flat,
):
    sums = gathered(rows, coarse, suby)
    cross = pick(sums, SCALARS)
    square = pick(sums, SCALARS + 1)
    norm = got(scalars_in, 0)
    unit = got(scalars_in, 1)
    rest = square - 2.0 * cross * cross + cross * cross * unit
    second = jnp.sqrt(jnp.maximum(rest, 0.0) + EPSILON)
    scale = 1.0 / second
    solution = coarse_solve(inverse, coarse) * live_of(counts)
    solution = (solution - cross * weights[:, 0:1]) * scale
    put(scalars, 0, norm)
    put(scalars, 1, unit)
    put(scalars, 2, cross)
    put(scalars, 3, second)
    part[...] = prolong(basis, solution, tiles, flat)
    local = (solved[...] - (cross / norm) * solved_first[...]) * scale
    part[8:56, :] = part[8:56, :] + local


def apply_second(
    folded, odd, even, coefs, patch, image, scalars, direction, third, gather
):
    field = folded_columns(folded, odd, even)
    vector = operate(field, coefs[0, 8:56, :], [coefs[1 + f, 8:56, :] for f in range(4)])
    own = own_mask((CX, LW), OV)
    direction[...] = field[8 : 8 + CX]
    vector = jnp.where(own, vector[8 : 8 + CX], 0.0)
    third[...] = vector
    first = jnp.where(own, patch[OV : OV + CX] * (1.0 / got(scalars, 0)), 0.0)
    second = (image[...] - got(scalars, 2) * first) * (1.0 / got(scalars, 3))
    second = jnp.where(own, second, 0.0)
    lanes = lanes_of((1, 128))
    row = jnp.zeros((1, 128), f32)
    for lane, value in enumerate(
        (first * vector, second * vector, vector * vector, first * second, second * second)
    ):
        row = jnp.where(lanes == lane, total(value), row)
    gather[...] = jnp.broadcast_to(row, gather.shape)


def add_rows(rows, gather):
    row = jnp.sum(rows[...], axis=0, keepdims=True)
    gather[...] = jnp.broadcast_to(row, gather.shape)


def finish(rows, patch, image, third_image, direction_one, direction_two, scalars, solution, residual):
    sums = jnp.sum(rows[...], axis=0, keepdims=True)
    first_second = pick(sums, 0)
    second_second = pick(sums, 1)
    square = pick(sums, 2)
    cross = pick(sums, 3)
    unit_two = pick(sums, 4)
    source_norm = got(scalars, 0)
    unit = got(scalars, 1)
    first_first = got(scalars, 2)
    second_first = got(scalars, 3)
    rest = square - first_second * first_second * (2.0 - unit)
    rest = rest - second_second * second_second * (2.0 - unit_two)
    rest = rest + 2.0 * first_second * second_second * cross
    third_second = jnp.sqrt(jnp.maximum(rest, 0.0) + EPSILON)
    radius = jnp.sqrt(first_first * first_first + second_first * second_first)
    cosine = first_first / radius
    sine = second_first / radius
    upper_right = cosine * first_second + sine * second_second
    lower_right = cosine * second_second - sine * first_second
    radius_two = jnp.sqrt(lower_right * lower_right + third_second * third_second)
    weight_two = lower_right / radius_two * (-sine * source_norm) / radius_two
    weight_one = (cosine * source_norm - upper_right * weight_two) / radius
    remainder_one = source_norm - first_first * weight_one - first_second * weight_two
    remainder_two = -second_first * weight_one - second_second * weight_two
    remainder_three = -third_second * weight_two
    first = patch[OV : OV + CX] * (1.0 / source_norm)
    second = (image[...] - first_first * first) * (1.0 / second_first)
    third = (third_image[...] - first_second * first - second_second * second) * (1.0 / third_second)
    found = weight_one * direction_one[...] + weight_two * direction_two[...]
    left_over = remainder_one * first + remainder_two * second + remainder_three * third
    solution[...] = pltpu.roll(found, LW - OV, 1)[:, :CY]
    residual[...] = pltpu.roll(left_over, LW - OV, 1)[:, :CY]


def shape_of(*dims):
    return jax.ShapeDtypeStruct(dims, f32)


VMEM = pl.BlockSpec(memory_space=pltpu.VMEM)
SMEM = pl.BlockSpec(memory_space=pltpu.SMEM)
PARAMS = pltpu.CompilerParams(vmem_limit_bytes=24 * 1024 * 1024)


def kernel(body, outs, scratch=(), first_smem=False):
    def call(*args):
        specs = [VMEM] * len(args)
        if first_smem:
            specs[0] = SMEM
        return pl.pallas_call(
            body,
            out_shape=outs,
            in_specs=specs,
            out_specs=[VMEM] * len(outs),
            scratch_shapes=list(scratch),
            compiler_params=PARAMS,
        )(*args)

    return call


def swap(axis, forward, backward):
    count = lax.axis_size(axis)
    before = lax.ppermute(forward, axis, [(i, i + 1) for i in range(count - 1)])
    after = lax.ppermute(backward, axis, [(i + 1, i) for i in range(count - 1)])
    return before, after


def swap_columns(odd, even):
    count = lax.axis_size("gy")
    inside = [(i, i ^ 1) for i in range(count)]
    across = [(i, i + 1 if i % 2 else i - 1) for i in range(1, count - 1)]
    even = lax.ppermute(even, "gy", inside)
    odd = lax.ppermute(odd, "gy", across)
    return odd, even


def everywhere(rows, axes=AXES):
    count = rows.shape[0]
    return lax.all_to_all(rows.reshape(count, 1, 128), axes, 0, 0).reshape(count, 128)


def on_device(
    source, potential, mobility_along, mobility_across, recombination, counts, basis, coarse_inverse
):
    suby = lax.axis_size("gy")
    devices = lax.axis_size("gx") * suby
    rows = shape_of(devices, 128)
    patch_shape, own_shape = shape_of(PX, LW), shape_of(CX, LW)
    tiles = pltpu.VMEM((3, PX, 128), f32)
    flat = pltpu.VMEM((9, GROUPS, 128), f32)
    coarse = pltpu.VMEM((devices // 4, 128), f32)
    fields = (source, potential, mobility_along, mobility_across, recombination)

    def bind(body):
        def run(*refs):
            return body(suby, *refs)

        return run

    edge = pltpu.VMEM((K, 3 * 128), f32)
    held, ahead, behind = pl.pallas_call(
        pack_rows,
        out_shape=[shape_of(5, CX, CY), shape_of(256, 128), shape_of(256, 128)],
        in_specs=[SMEM] + [pl.BlockSpec(memory_space=pltpu.HBM)] * 6,
        out_specs=[VMEM] * 3,
        scratch_shapes=[edge, edge, pltpu.SemaphoreType.DMA((7,))],
        compiler_params=PARAMS,
    )(counts, *[pltpu.with_memory_space_constraint(x, pltpu.HBM) for x in (*fields, basis)])
    before, after = swap("gx", ahead, behind)
    strip = shape_of(PX, 128)
    grown, odd, even = kernel(pack_columns, [shape_of(5, PX, CY), strip, strip])(
        held, before, after
    )
    odd, even = swap_columns(odd, even)
    patch, coefs, solved_one, row = kernel(
        bind(prepare),
        [patch_shape, shape_of(5, PX, LW), shape_of(48, LW), rows],
        [tiles, flat],
        True,
    )(counts, grown, odd, even, basis)
    part, weights, scalars_one = kernel(
        bind(spread_first),
        [patch_shape, shape_of(K, 128), shape_of(8, 128)],
        [coarse, tiles, flat],
        True,
    )(counts, everywhere(row), coarse_inverse, basis, solved_one)
    over, under = swap("gx", part[PX // 2 :], part[: PX // 2])
    folded, odd, even = kernel(fold_rows, [patch_shape, strip, strip])(part, over, under)
    odd, even = swap_columns(odd, even)
    direction_one, image_one, solved_two, row = kernel(
        bind(apply_first),
        [own_shape, own_shape, shape_of(48, LW), rows],
        [tiles, flat],
        True,
    )(
        counts, folded, odd, even, coefs, patch, scalars_one, basis, before, after
    )
    part, scalars_two = kernel(
        bind(spread_second),
        [patch_shape, shape_of(8, 128)],
        [coarse, tiles, flat],
        True,
    )(
        counts, everywhere(row), coarse_inverse, basis, solved_one, solved_two, weights, scalars_one
    )
    over, under = swap("gx", part[40:], part[:24])
    strip = shape_of(48, 128)
    folded, odd, even = kernel(fold_rows, [shape_of(48, LW), strip, strip])(
        part, over, under
    )
    odd, even = swap_columns(odd, even)
    direction_two, image_two, row = kernel(
        apply_second, [own_shape, own_shape, shape_of(devices // suby, 128)]
    )(
        folded, odd, even, coefs, patch, image_one, scalars_two
    )
    (row,) = kernel(add_rows, [shape_of(suby, 128)])(everywhere(row, "gx"))
    out = shape_of(CX, CY)
    answer, residual = kernel(finish, [out, out])(
        everywhere(row, "gy"), patch, image_one, image_two, direction_one, direction_two, scalars_two
    )
    return answer, residual


def solution(mesh):
    grid = P("gx", "gy")
    return jax.shard_map(
        on_device,
        mesh=mesh,
        in_specs=(grid,) * 7 + (P(("gx", "gy"), None),),
        out_specs=(grid, grid),
        check_vma=False,
    )
```

```python
import jax
import jax.numpy as jnp
from jax import lax
from jax.experimental import pallas as pl
from jax.experimental.pallas import tpu as pltpu
from jax.sharding import PartitionSpec as P

OV = 16
SWEEPS = 8
OMEGA = 0.8
EPSILON = 1e-06
CX = 32
CY = 256
K = 32
PX = CX + 2 * OV
PY = CY + 2 * OV
LW = 384
GROUPS = PX // 4
STRIP = 24
SCALARS = 96
f32 = jnp.float32
AXES = ("gx", "gy")


def lanes_of(shape):
    return lax.broadcasted_iota(jnp.int32, shape, len(shape) - 1)


def rows_of(shape):
    return lax.broadcasted_iota(jnp.int32, shape, len(shape) - 2)


def left(x):
    return pltpu.roll(x, LW - 1, 1)


def right(x):
    return pltpu.roll(x, 1, 1)


def up(x):
    return pltpu.roll(x, x.shape[0] - 1, 0)


def down(x):
    return pltpu.roll(x, 1, 0)


def own_mask(shape, first):
    rows, lanes = rows_of(shape) + first, lanes_of(shape)
    return (rows >= OV) & (rows < OV + CX) & (lanes >= OV) & (lanes < OV + CY)


def is_even():
    return lax.rem(lax.axis_index("gy"), 2) == 0


def to_pairs(rightward, leftward):
    even = is_even()
    return jnp.where(even, leftward, rightward), jnp.where(even, rightward, leftward)


def from_pairs(odd, even_pairs):
    even = is_even()
    return jnp.where(even, odd, even_pairs), jnp.where(even, even_pairs, odd)


def total(x):
    return jnp.sum(jnp.sum(x, axis=0, keepdims=True), axis=1, keepdims=True)


def to_row(column):
    shape = (K, 128)
    spread = jnp.broadcast_to(column, shape)
    return jnp.sum(jnp.where(rows_of(shape) == lanes_of(shape), spread, 0.0), axis=0, keepdims=True)


def restrict(basis, patch, tiles, flat):
    for t in range(3):
        tiles[t] = patch[:, t * 128 : (t + 1) * 128]
    parts = [None] * 9
    for m in range(4):
        rows = jnp.concatenate(
            [tiles[t, pl.ds(m, GROUPS, stride=4), :] for t in range(3)], axis=1
        )
        if m:
            rows = pltpu.roll(rows, 32 * m, 1)
        for t in range(3):
            piece = rows[:, t * 128 : (t + 1) * 128]
            at = 2 * m + t
            parts[at] = piece if parts[at] is None else parts[at] + piece
    for t in range(9):
        flat[t] = parts[t]
    sums = [jnp.zeros((K, 128), f32) for _ in range(3)]
    for g in range(GROUPS):
        for t in range(9):
            block = (g * 9 + t) * 128
            row = jnp.broadcast_to(flat[t, pl.ds(g, 1), :], (K, 128))
            sums[t % 3] = sums[t % 3] + basis[:, block : block + 128] * row
    return jnp.sum(sums[0] + sums[1] + sums[2], axis=1, keepdims=True)


def prolong(basis, weights, tiles, flat):
    wide = jnp.broadcast_to(weights, (K, 128))
    for g in range(GROUPS):
        for t in range(9):
            block = (g * 9 + t) * 128
            flat[t, pl.ds(g, 1), :] = jnp.sum(
                basis[:, block : block + 128] * wide, axis=0, keepdims=True
            )
    for m in range(4):
        rows = jnp.concatenate([flat[2 * m + t] for t in range(3)], axis=1)
        if m:
            rows = pltpu.roll(rows, LW - 32 * m, 1)
        rows = jnp.where(lanes_of(rows.shape) < PY, rows, 0.0)
        for t in range(3):
            tiles[t, pl.ds(m, GROUPS, stride=4), :] = rows[:, t * 128 : (t + 1) * 128]
    return jnp.concatenate([tiles[t] for t in range(3)], axis=1)


def gathered(rows, coarse, suby):
    count = rows.shape[0] // 4
    shift = suby // 4
    taken = [rows[pl.ds(q, count, stride=4), :] for q in range(4)]
    zero = jnp.zeros((shift, 128), f32)
    lanes = lanes_of((count, 128))
    result = None
    for s in range(4):
        own = taken[s]
        later = jnp.concatenate([zero, taken[(s + 1) % 4][: count - shift]], axis=0)
        earlier = jnp.concatenate([taken[(s + 2) % 4][shift:], zero], axis=0)
        piece = jnp.where(
            lanes < 32, own, jnp.where(lanes < 64, later, jnp.where(lanes < 96, earlier, 0.0))
        )
        if s:
            piece = pltpu.roll(piece, 32 * s, 1)
        result = piece if result is None else result + piece
    coarse[...] = result
    return jnp.sum(taken[0] + taken[1] + (taken[2] + taken[3]), axis=0, keepdims=True)


def compact(rows, gather):
    count = rows.shape[0] // 4
    slot = slot_rows(rows.shape[0])
    taken = [rows[pl.ds(q, count, stride=4), :] for q in range(4)]
    lanes = lanes_of((count, 128))
    result = None
    for q in range(4):
        piece = jnp.where(lanes < 32, taken[q], 0.0)
        if q:
            piece = pltpu.roll(piece, 32 * q, 1)
        result = piece if result is None else result + piece
    sums = jnp.sum(taken[0] + taken[1] + (taken[2] + taken[3]), axis=0, keepdims=True)
    tail = jnp.broadcast_to(sums, (slot - count, 128))
    block = jnp.concatenate([result, tail], axis=0)
    for at in range(0, gather.shape[0], slot):
        gather[at : at + slot, :] = block


def slot_rows(suby):
    return suby // 4 + 8


def unpacked(rows, coarse, suby):
    count, slot = suby // 4, slot_rows(suby)
    sums = None
    for i in range(rows.shape[0] // slot):
        coarse[i * count : (i + 1) * count, :] = rows[i * slot : i * slot + count, :]
        row = rows[i * slot + count : i * slot + count + 1, :]
        sums = row if sums is None else sums + row
    return sums


def pick(row, lane):
    return jnp.sum(jnp.where(lanes_of(row.shape) == lane, row, 0.0), axis=1, keepdims=True)


def coarse_solve(inverse, coarse):
    sums = [jnp.zeros((K, 128), f32) for _ in range(4)]
    for b in range(coarse.shape[0]):
        row = jnp.broadcast_to(coarse[pl.ds(b, 1), :], (K, 128))
        sums[b % 4] = sums[b % 4] + inverse[:, b * 128 : (b + 1) * 128] * row
    return jnp.sum((sums[0] + sums[1]) + (sums[2] + sums[3]), axis=1, keepdims=True)


def relax(vector, diagonal, faces):
    inverse = OMEGA / jnp.where(diagonal > 0.0, diagonal, 1.0)
    below, above, east, west = [inverse * face for face in faces]
    start = inverse * vector
    field = start
    for _ in range(SWEEPS - 1):
        moved = below * up(field) + above * down(field)
        moved = moved + (east * left(field) + west * right(field))
        field = (start + (1.0 - OMEGA) * field) + moved
    return field


def operate(field, diagonal, faces):
    below, above, east, west = faces
    moved = below * up(field) + above * down(field)
    moved = moved + (east * left(field) + west * right(field))
    return diagonal * field - moved


def pack_rows(
    counts, source, potential, along, across, recombination, basis, held, ahead, behind, live_out,
    head, tail, sems,
):
    edge = head.shape[1]
    copies = [
        pltpu.make_async_copy(field, held.at[f], sems.at[f])
        for f, field in enumerate((source, potential, along, across, recombination))
    ]
    copies.append(pltpu.make_async_copy(basis.at[:, :edge], head, sems.at[5]))
    copies.append(
        pltpu.make_async_copy(basis.at[:, basis.shape[1] - edge :], tail, sems.at[6])
    )
    for copy in copies:
        copy.start()
    for copy in copies:
        copy.wait()
    live = (rows_of((K, 128)) < counts[0, 0]).astype(f32)
    live_out[...] = live
    for f in range(5):
        for t in range(2):
            at = (2 * f + t) * OV
            cols = slice(t * 128, (t + 1) * 128)
            ahead[at : at + OV, :] = held[f, CX - OV :, cols]
            behind[at : at + OV, :] = held[f, :OV, cols]
    for t in range(3):
        at = 160 + t * K
        cols = slice(t * 128, (t + 1) * 128)
        ahead[at : at + K, :] = tail[:, cols] * live
        behind[at : at + K, :] = head[:, cols] * live


def pack_columns(held, before, after, rows, odd, even):
    lanes = lanes_of((PX, 128))
    to_right = to_left = None
    for f in range(5):
        tiles = []
        for t in range(2):
            at = (2 * f + t) * OV
            cols = slice(t * 128, (t + 1) * 128)
            tile = jnp.concatenate(
                [before[at : at + OV, :], held[f, :, cols], after[at : at + OV, :]], axis=0
            )
            rows[f, :, cols] = tile
            tiles.append(tile)
        last = pltpu.roll(jnp.where(lanes >= 111, tiles[1], 0.0), 17 + STRIP * f, 1)
        first = jnp.where(lanes < 17, tiles[0], 0.0)
        if f:
            first = pltpu.roll(first, STRIP * f, 1)
        to_right = last if f == 0 else to_right + last
        to_left = first if f == 0 else to_left + first
    odd[...], even[...] = to_pairs(to_right, to_left)


def prepare(suby, live, rows, odd, even, basis, patch, coefs, solved, gather, tiles, flat):
    zero = jnp.zeros((PX, LW - CY), f32)
    lanes = lanes_of((PX, 128))
    from_left, from_right = from_pairs(odd[...], even[...])
    fields = []
    for f in range(5):
        middle = pltpu.roll(jnp.concatenate([rows[f], zero], axis=1), OV, 1)
        band = (lanes >= STRIP * f) & (lanes < STRIP * f + 17)
        wide = jnp.zeros((PX, LW - 128), f32)
        one = jnp.concatenate([jnp.where(band, from_left, 0.0), wide], axis=1)
        two = jnp.concatenate([jnp.where(band, from_right, 0.0), wide], axis=1)
        one = pltpu.roll(one, LW - 1 - STRIP * f, 1)
        two = pltpu.roll(two, OV + CY - STRIP * f, 1)
        fields.append(middle + one + two)
    source, potential, along, across, recombination = fields
    weight = jnp.sqrt(along * up(along))
    rise = 0.5 * (up(potential) - potential)
    below = weight * jnp.exp(rise)
    above = weight * jnp.exp(-rise)
    diagonal = recombination + above + down(below)
    weight = jnp.sqrt(across * left(across))
    rise = 0.5 * (left(potential) - potential)
    east = weight * jnp.exp(rise)
    west = weight * jnp.exp(-rise)
    diagonal = diagonal + west + right(east)
    faces = (below, down(above), east, right(west))
    coefs[0] = diagonal
    for f in range(4):
        coefs[1 + f] = faces[f]
    source = jnp.where(lanes_of((PX, LW)) < PY, source, 0.0)
    patch[...] = source
    own = own_mask((PX, LW), 0)
    square = total(jnp.where(own, source * source, 0.0))
    local = relax(source[8:56], diagonal[8:56], [face[8:56] for face in faces])
    solved[...] = jnp.where(own_mask((48, LW), 8), local, 0.0)
    residual = restrict(basis, source, tiles, flat) * live[:, 0:1]
    row = to_row(residual)
    row = jnp.where(lanes_of((1, 128)) == SCALARS, square, row)
    gather[...] = jnp.broadcast_to(row, gather.shape)


def put(scalars, at, value):
    scalars[pl.ds(at, 1), :] = jnp.broadcast_to(value, (1, 128))


def got(scalars, at):
    return scalars[pl.ds(at, 1), :][:, 0:1]


def spread_first(
    suby, live, rows, inverse, basis, solved, part, weights, scalars, coarse, tiles, flat
):
    sums = unpacked(rows, coarse, suby)
    square = pick(sums, SCALARS)
    norm = jnp.sqrt(square + EPSILON)
    scale = 1.0 / norm
    solution = coarse_solve(inverse, coarse) * live[:, 0:1] * scale
    weights[...] = jnp.broadcast_to(solution, (K, 128))
    put(scalars, 0, norm)
    put(scalars, 1, square / (square + EPSILON))
    part[...] = prolong(basis, solution, tiles, flat)
    part[8:56, :] = part[8:56, :] + solved[...] * scale


def fold_rows(part, before, after, folded, odd, even):
    height = folded.shape[0]
    first = (PX - height) // 2
    half = height // 2
    whole = part[first : first + height, :] + jnp.concatenate(
        [before[PX // 2 - half :, :] if before.shape[0] > half else before[...],
         after[:half, :] if after.shape[0] > half else after[...]],
        axis=0,
    )
    folded[...] = whole
    lanes = lanes_of((height, 128))
    moved = pltpu.roll(whole, LW - 255, 1)
    odd[...], even[...] = to_pairs(
        jnp.where(lanes < 33, moved[:, :128], 0.0), jnp.where(lanes < 33, whole[:, :128], 0.0)
    )


def folded_columns(folded, odd, even):
    height = folded.shape[0]
    zero = jnp.zeros((height, 256), f32)
    from_left, from_right = from_pairs(odd[...], even[...])
    one = pltpu.roll(jnp.concatenate([from_left, zero], axis=1), LW - 1, 1)
    two = jnp.concatenate([zero, from_right], axis=1)
    return folded[...] + one + two


def apply_first(
    suby, live, folded, odd, even, coefs, patch, scalars, basis, before, after,
    direction, image, solved, gather, tiles, flat,
):
    field = folded_columns(folded, odd, even)
    direction[...] = field[OV : OV + CX]
    diagonal = coefs[0]
    faces = [coefs[1 + f] for f in range(4)]
    shape = (PX, LW)
    rows, lanes = rows_of(shape), lanes_of(shape)
    inner = (rows >= 1) & (rows < PX - 1) & (lanes < PY)
    vector = jnp.where(inner, operate(field, diagonal, faces), 0.0)
    image[...] = vector[OV : OV + CX]
    own = own_mask((CX, LW), OV)
    mine = jnp.where(own, vector[OV : OV + CX], 0.0)
    first = patch[OV : OV + CX] * (1.0 / got(scalars, 0))
    cross = total(mine * first)
    square = total(mine * mine)
    local = relax(vector[8:56], diagonal[8:56], [face[8:56] for face in faces])
    solved[...] = jnp.where(own_mask((48, LW), 8), local, 0.0)
    residual = restrict(basis, vector, tiles, flat) * live[:, 0:1]
    fourth = vector[32:40]
    third = pltpu.roll(vector[24:32], 96, 1)
    for_next = for_before = jnp.zeros((K, 128), f32)
    for t in range(3):
        cols = slice(t * 128, (t + 1) * 128)
        at = 160 + t * K
        for_next = for_next + after[at : at + K, :] * fourth[0:1, cols]
        for_before = for_before + before[at : at + K, :] * third[7:8, cols]
    row = to_row(residual)
    row = row + pltpu.roll(to_row(jnp.sum(for_next, axis=1, keepdims=True)), 32, 1)
    row = row + pltpu.roll(to_row(jnp.sum(for_before, axis=1, keepdims=True)), 64, 1)
    lanes = lanes_of((1, 128))
    row = jnp.where(lanes == SCALARS, cross, jnp.where(lanes == SCALARS + 1, square, row))
    gather[...] = jnp.broadcast_to(row, gather.shape)


def spread_second(
    suby, live, rows, inverse, basis, solved_first, solved, weights, scalars_in,
    part, scalars, coarse, tiles, flat,
):
    sums = gathered(rows, coarse, suby)
    cross = pick(sums, SCALARS)
    square = pick(sums, SCALARS + 1)
    norm = got(scalars_in, 0)
    unit = got(scalars_in, 1)
    rest = square - 2.0 * cross * cross + cross * cross * unit
    second = jnp.sqrt(jnp.maximum(rest, 0.0) + EPSILON)
    scale = 1.0 / second
    solution = coarse_solve(inverse, coarse) * live[:, 0:1]
    solution = (solution - cross * weights[:, 0:1]) * scale
    put(scalars, 0, norm)
    put(scalars, 1, unit)
    put(scalars, 2, cross)
    put(scalars, 3, second)
    part[...] = prolong(basis, solution, tiles, flat)
    local = (solved[...] - (cross / norm) * solved_first[...]) * scale
    part[8:56, :] = part[8:56, :] + local


def apply_second(
    folded, odd, even, coefs, patch, image, scalars, direction, third, gather
):
    field = folded_columns(folded, odd, even)
    vector = operate(field, coefs[0, 8:56, :], [coefs[1 + f, 8:56, :] for f in range(4)])
    own = own_mask((CX, LW), OV)
    direction[...] = field[8 : 8 + CX]
    vector = jnp.where(own, vector[8 : 8 + CX], 0.0)
    third[...] = vector
    first = jnp.where(own, patch[OV : OV + CX] * (1.0 / got(scalars, 0)), 0.0)
    second = (image[...] - got(scalars, 2) * first) * (1.0 / got(scalars, 3))
    second = jnp.where(own, second, 0.0)
    lanes = lanes_of((1, 128))
    row = jnp.zeros((1, 128), f32)
    for lane, value in enumerate(
        (first * vector, second * vector, vector * vector, first * second, second * second)
    ):
        row = jnp.where(lanes == lane, total(value), row)
    gather[...] = jnp.broadcast_to(row, gather.shape)


def add_rows(rows, gather):
    row = jnp.sum(rows[...], axis=0, keepdims=True)
    gather[...] = jnp.broadcast_to(row, gather.shape)


def finish(rows, patch, image, third_image, direction_one, direction_two, scalars, solution, residual):
    sums = jnp.sum(rows[...], axis=0, keepdims=True)
    first_second = pick(sums, 0)
    second_second = pick(sums, 1)
    square = pick(sums, 2)
    cross = pick(sums, 3)
    unit_two = pick(sums, 4)
    source_norm = got(scalars, 0)
    unit = got(scalars, 1)
    first_first = got(scalars, 2)
    second_first = got(scalars, 3)
    rest = square - first_second * first_second * (2.0 - unit)
    rest = rest - second_second * second_second * (2.0 - unit_two)
    rest = rest + 2.0 * first_second * second_second * cross
    third_second = jnp.sqrt(jnp.maximum(rest, 0.0) + EPSILON)
    radius = jnp.sqrt(first_first * first_first + second_first * second_first)
    cosine = first_first / radius
    sine = second_first / radius
    upper_right = cosine * first_second + sine * second_second
    lower_right = cosine * second_second - sine * first_second
    radius_two = jnp.sqrt(lower_right * lower_right + third_second * third_second)
    weight_two = lower_right / radius_two * (-sine * source_norm) / radius_two
    weight_one = (cosine * source_norm - upper_right * weight_two) / radius
    remainder_one = source_norm - first_first * weight_one - first_second * weight_two
    remainder_two = -second_first * weight_one - second_second * weight_two
    remainder_three = -third_second * weight_two
    first = patch[OV : OV + CX] * (1.0 / source_norm)
    second = (image[...] - first_first * first) * (1.0 / second_first)
    third = (third_image[...] - first_second * first - second_second * second) * (1.0 / third_second)
    found = weight_one * direction_one[...] + weight_two * direction_two[...]
    left_over = remainder_one * first + remainder_two * second + remainder_three * third
    solution[...] = pltpu.roll(found, LW - OV, 1)[:, :CY]
    residual[...] = pltpu.roll(left_over, LW - OV, 1)[:, :CY]


def shape_of(*dims):
    return jax.ShapeDtypeStruct(dims, f32)


VMEM = pl.BlockSpec(memory_space=pltpu.VMEM)
PARAMS = pltpu.CompilerParams(vmem_limit_bytes=24 * 1024 * 1024)


def kernel(body, outs, scratch=()):
    def call(*args):
        return pl.pallas_call(
            body,
            out_shape=outs,
            in_specs=[VMEM] * len(args),
            out_specs=[VMEM] * len(outs),
            scratch_shapes=list(scratch),
            compiler_params=PARAMS,
        )(*args)

    return call


def swap(axis, forward, backward):
    count = lax.axis_size(axis)
    before = lax.ppermute(forward, axis, [(i, i + 1) for i in range(count - 1)])
    after = lax.ppermute(backward, axis, [(i + 1, i) for i in range(count - 1)])
    return before, after


def swap_columns(odd, even):
    count = lax.axis_size("gy")
    inside = [(i, i ^ 1) for i in range(count)]
    across = [(i, i + 1 if i % 2 else i - 1) for i in range(1, count - 1)]
    even = lax.ppermute(even, "gy", inside)
    odd = lax.ppermute(odd, "gy", across)
    return odd, even


def everywhere(rows, axes=AXES):
    count = lax.axis_size(axes)
    slots = rows.reshape(count, rows.shape[0] // count, 128)
    return lax.all_to_all(slots, axes, 0, 0).reshape(rows.shape)


def on_device(
    source, potential, mobility_along, mobility_across, recombination, counts, basis, coarse_inverse
):
    suby = lax.axis_size("gy")
    devices = lax.axis_size("gx") * suby
    rows = shape_of(devices, 128)
    patch_shape, own_shape = shape_of(PX, LW), shape_of(CX, LW)
    tiles = pltpu.VMEM((3, PX, 128), f32)
    flat = pltpu.VMEM((9, GROUPS, 128), f32)
    coarse = pltpu.VMEM((devices // 4, 128), f32)
    fields = (source, potential, mobility_along, mobility_across, recombination)

    def bind(body):
        def run(*refs):
            return body(suby, *refs)

        return run

    edge = pltpu.VMEM((K, 3 * 128), f32)
    held, ahead, behind, live = pl.pallas_call(
        pack_rows,
        out_shape=[
            shape_of(5, CX, CY), shape_of(256, 128), shape_of(256, 128), shape_of(K, 128)
        ],
        in_specs=[pl.BlockSpec(memory_space=pltpu.SMEM)]
        + [pl.BlockSpec(memory_space=pltpu.HBM)] * 6,
        out_specs=[VMEM] * 4,
        scratch_shapes=[
            edge, edge, pltpu.SemaphoreType.DMA((7,))
        ],
        compiler_params=PARAMS,
    )(counts, *[pltpu.with_memory_space_constraint(x, pltpu.HBM) for x in (*fields, basis)])
    before, after = swap("gx", ahead, behind)
    strip = shape_of(PX, 128)
    grown, odd, even = kernel(pack_columns, [shape_of(5, PX, CY), strip, strip])(
        held, before, after
    )
    odd, even = swap_columns(odd, even)
    patch, coefs, solved_one, row = kernel(
        bind(prepare),
        [patch_shape, shape_of(5, PX, LW), shape_of(48, LW), shape_of(suby, 128)],
        [tiles, flat],
    )(live, grown, odd, even, basis)
    (row,) = kernel(compact, [shape_of(devices // suby * slot_rows(suby), 128)])(
        everywhere(row, "gy")
    )
    part, weights, scalars_one = kernel(
        bind(spread_first),
        [patch_shape, shape_of(K, 128), shape_of(8, 128)],
        [coarse, tiles, flat],
    )(live, everywhere(row, "gx"), coarse_inverse, basis, solved_one)
    over, under = swap("gx", part[PX // 2 :], part[: PX // 2])
    folded, odd, even = kernel(fold_rows, [patch_shape, strip, strip])(part, over, under)
    odd, even = swap_columns(odd, even)
    direction_one, image_one, solved_two, row = kernel(
        bind(apply_first),
        [own_shape, own_shape, shape_of(48, LW), rows],
        [tiles, flat],
    )(
        live, folded, odd, even, coefs, patch, scalars_one, basis, before, after
    )
    part, scalars_two = kernel(
        bind(spread_second),
        [patch_shape, shape_of(8, 128)],
        [coarse, tiles, flat],
    )(
        live, everywhere(row), coarse_inverse, basis, solved_one, solved_two, weights, scalars_one
    )
    over, under = swap("gx", part[40:], part[:24])
    strip = shape_of(48, 128)
    folded, odd, even = kernel(fold_rows, [shape_of(48, LW), strip, strip])(
        part, over, under
    )
    odd, even = swap_columns(odd, even)
    direction_two, image_two, row = kernel(
        apply_second, [own_shape, own_shape, shape_of(devices // suby, 128)]
    )(
        folded, odd, even, coefs, patch, image_one, scalars_two
    )
    (row,) = kernel(add_rows, [shape_of(suby, 128)])(everywhere(row, "gx"))
    out = shape_of(CX, CY)
    answer, residual = kernel(finish, [out, out])(
        everywhere(row, "gy"), patch, image_one, image_two, direction_one, direction_two, scalars_two
    )
    return answer, residual


def solution(mesh):
    grid = P("gx", "gy")
    return jax.shard_map(
        on_device,
        mesh=mesh,
        in_specs=(grid,) * 7 + (P(("gx", "gy"), None),),
        out_specs=(grid, grid),
        check_vma=False,
    )
```

```python
import jax
import jax.numpy as jnp
from jax import lax
from jax.experimental import pallas as pl
from jax.experimental.pallas import tpu as pltpu
from jax.sharding import PartitionSpec as P

OV = 16
SWEEPS = 8
OMEGA = 0.8
EPSILON = 1e-06
CX = 32
CY = 256
K = 32
PX = CX + 2 * OV
PY = CY + 2 * OV
LW = 384
GROUPS = PX // 4
STRIP = 24
LIVE = PY
SCALARS = 96
f32 = jnp.float32
AXES = ("gx", "gy")


def lanes_of(shape):
    return lax.broadcasted_iota(jnp.int32, shape, len(shape) - 1)


def rows_of(shape):
    return lax.broadcasted_iota(jnp.int32, shape, len(shape) - 2)


def left(x):
    return pltpu.roll(x, LW - 1, 1)


def right(x):
    return pltpu.roll(x, 1, 1)


def up(x):
    return pltpu.roll(x, x.shape[0] - 1, 0)


def down(x):
    return pltpu.roll(x, 1, 0)


def own_mask(shape, first):
    rows, lanes = rows_of(shape) + first, lanes_of(shape)
    return (rows >= OV) & (rows < OV + CX) & (lanes >= OV) & (lanes < OV + CY)


def is_even(axis):
    return lax.rem(lax.axis_index(axis), 2) == 0


def to_pairs(axis, ahead, back):
    even = is_even(axis)
    return jnp.where(even, back, ahead), jnp.where(even, ahead, back)


def from_pairs(axis, odd, even_pairs):
    even = is_even(axis)
    return jnp.where(even, odd, even_pairs), jnp.where(even, even_pairs, odd)


def total(x):
    return jnp.sum(jnp.sum(x, axis=0, keepdims=True), axis=1, keepdims=True)


def to_row(column):
    shape = (K, 128)
    spread = jnp.broadcast_to(column, shape)
    return jnp.sum(jnp.where(rows_of(shape) == lanes_of(shape), spread, 0.0), axis=0, keepdims=True)


def restrict(basis, patch, tiles, flat):
    for t in range(3):
        tiles[t] = patch[:, t * 128 : (t + 1) * 128]
    parts = [None] * 9
    for m in range(4):
        rows = jnp.concatenate(
            [tiles[t, pl.ds(m, GROUPS, stride=4), :] for t in range(3)], axis=1
        )
        if m:
            rows = pltpu.roll(rows, 32 * m, 1)
        for t in range(3):
            piece = rows[:, t * 128 : (t + 1) * 128]
            at = 2 * m + t
            parts[at] = piece if parts[at] is None else parts[at] + piece
    for t in range(9):
        flat[t] = parts[t]
    sums = [jnp.zeros((K, 128), f32) for _ in range(3)]
    for g in range(GROUPS):
        for t in range(9):
            block = (g * 9 + t) * 128
            row = jnp.broadcast_to(flat[t, pl.ds(g, 1), :], (K, 128))
            sums[t % 3] = sums[t % 3] + basis[:, block : block + 128] * row
    return jnp.sum(sums[0] + sums[1] + sums[2], axis=1, keepdims=True)


def prolong(basis, weights, tiles, flat):
    wide = jnp.broadcast_to(weights, (K, 128))
    for g in range(GROUPS):
        for t in range(9):
            block = (g * 9 + t) * 128
            flat[t, pl.ds(g, 1), :] = jnp.sum(
                basis[:, block : block + 128] * wide, axis=0, keepdims=True
            )
    for m in range(4):
        rows = jnp.concatenate([flat[2 * m + t] for t in range(3)], axis=1)
        if m:
            rows = pltpu.roll(rows, LW - 32 * m, 1)
        rows = jnp.where(lanes_of(rows.shape) < PY, rows, 0.0)
        for t in range(3):
            tiles[t, pl.ds(m, GROUPS, stride=4), :] = rows[:, t * 128 : (t + 1) * 128]
    return jnp.concatenate([tiles[t] for t in range(3)], axis=1)


def gathered(rows, coarse, suby):
    count = rows.shape[0] // 4
    shift = suby // 4
    taken = [rows[pl.ds(q, count, stride=4), :] for q in range(4)]
    zero = jnp.zeros((shift, 128), f32)
    lanes = lanes_of((count, 128))
    result = None
    for s in range(4):
        own = taken[s]
        later = jnp.concatenate([zero, taken[(s + 1) % 4][: count - shift]], axis=0)
        earlier = jnp.concatenate([taken[(s + 2) % 4][shift:], zero], axis=0)
        piece = jnp.where(
            lanes < 32, own, jnp.where(lanes < 64, later, jnp.where(lanes < 96, earlier, 0.0))
        )
        if s:
            piece = pltpu.roll(piece, 32 * s, 1)
        result = piece if result is None else result + piece
    coarse[...] = result
    return jnp.sum(taken[0] + taken[1] + (taken[2] + taken[3]), axis=0, keepdims=True)


def compact(rows, gather):
    count = rows.shape[0] // 4
    slot = slot_rows(rows.shape[0])
    taken = [rows[pl.ds(q, count, stride=4), :] for q in range(4)]
    lanes = lanes_of((count, 128))
    result = None
    for q in range(4):
        piece = jnp.where(lanes < 32, taken[q], 0.0)
        if q:
            piece = pltpu.roll(piece, 32 * q, 1)
        result = piece if result is None else result + piece
    sums = jnp.sum(taken[0] + taken[1] + (taken[2] + taken[3]), axis=0, keepdims=True)
    tail = jnp.broadcast_to(sums, (slot - count, 128))
    block = jnp.concatenate([result, tail], axis=0)
    for at in range(0, gather.shape[0], slot):
        gather[at : at + slot, :] = block


def slot_rows(suby):
    return suby // 4 + 8


def unpacked(rows, coarse, suby):
    count, slot = suby // 4, slot_rows(suby)
    sums = None
    for i in range(rows.shape[0] // slot):
        coarse[i * count : (i + 1) * count, :] = rows[i * slot : i * slot + count, :]
        row = rows[i * slot + count : i * slot + count + 1, :]
        sums = row if sums is None else sums + row
    return sums


def pick(row, lane):
    return jnp.sum(jnp.where(lanes_of(row.shape) == lane, row, 0.0), axis=1, keepdims=True)


def coarse_solve(inverse, coarse):
    sums = [jnp.zeros((K, 128), f32) for _ in range(4)]
    for b in range(coarse.shape[0]):
        row = jnp.broadcast_to(coarse[pl.ds(b, 1), :], (K, 128))
        sums[b % 4] = sums[b % 4] + inverse[:, b * 128 : (b + 1) * 128] * row
    return jnp.sum((sums[0] + sums[1]) + (sums[2] + sums[3]), axis=1, keepdims=True)


def relax(vector, diagonal, faces):
    inverse = OMEGA / jnp.where(diagonal > 0.0, diagonal, 1.0)
    below, above, east, west = [inverse * face for face in faces]
    start = inverse * vector
    field = start
    for _ in range(SWEEPS - 1):
        moved = below * up(field) + above * down(field)
        moved = moved + (east * left(field) + west * right(field))
        field = (start + (1.0 - OMEGA) * field) + moved
    return field


def operate(field, diagonal, faces):
    below, above, east, west = faces
    moved = below * up(field) + above * down(field)
    moved = moved + (east * left(field) + west * right(field))
    return diagonal * field - moved


def pack_rows(
    source, potential, along, across, recombination, basis, held, odd, even, head, tail, sems
):
    edge = head.shape[1]
    copies = [
        pltpu.make_async_copy(field, held.at[f], sems.at[f])
        for f, field in enumerate((source, potential, along, across, recombination))
    ]
    copies.append(pltpu.make_async_copy(basis.at[:, :edge], head, sems.at[5]))
    copies.append(
        pltpu.make_async_copy(basis.at[:, basis.shape[1] - edge :], tail, sems.at[6])
    )
    for copy in copies:
        copy.start()
    for copy in copies:
        copy.wait()
    for f in range(5):
        for t in range(2):
            at = slice((2 * f + t) * OV, (2 * f + t + 1) * OV)
            cols = slice(t * 128, (t + 1) * 128)
            odd[at, :], even[at, :] = to_pairs(
                "gx", held[f, CX - OV :, cols], held[f, :OV, cols]
            )
    for t in range(3):
        at = slice(160 + t * K, 160 + (t + 1) * K)
        cols = slice(t * 128, (t + 1) * 128)
        odd[at, :], even[at, :] = to_pairs("gx", tail[:, cols], head[:, cols])


def pack_columns(held, row_odd, row_even, rows, odd, even):
    before, after = from_pairs("gx", row_odd[: 10 * OV, :], row_even[: 10 * OV, :])
    lanes = lanes_of((PX, 128))
    to_right = to_left = None
    for f in range(5):
        tiles = []
        for t in range(2):
            at = (2 * f + t) * OV
            cols = slice(t * 128, (t + 1) * 128)
            tile = jnp.concatenate(
                [before[at : at + OV, :], held[f, :, cols], after[at : at + OV, :]], axis=0
            )
            rows[f, :, cols] = tile
            tiles.append(tile)
        last = pltpu.roll(jnp.where(lanes >= 111, tiles[1], 0.0), 17 + STRIP * f, 1)
        first = jnp.where(lanes < 17, tiles[0], 0.0)
        if f:
            first = pltpu.roll(first, STRIP * f, 1)
        to_right = last if f == 0 else to_right + last
        to_left = first if f == 0 else to_left + first
    odd[...], even[...] = to_pairs("gy", to_right, to_left)


def prepare(suby, counts, rows, odd, even, basis, live, patch, coefs, solved, gather, tiles, flat):
    zero = jnp.zeros((PX, LW - CY), f32)
    lanes = lanes_of((PX, 128))
    from_left, from_right = from_pairs("gy", odd[...], even[...])
    fields = []
    for f in range(5):
        middle = pltpu.roll(jnp.concatenate([rows[f], zero], axis=1), OV, 1)
        band = (lanes >= STRIP * f) & (lanes < STRIP * f + 17)
        wide = jnp.zeros((PX, LW - 128), f32)
        one = jnp.concatenate([jnp.where(band, from_left, 0.0), wide], axis=1)
        two = jnp.concatenate([jnp.where(band, from_right, 0.0), wide], axis=1)
        one = pltpu.roll(one, LW - 1 - STRIP * f, 1)
        two = pltpu.roll(two, OV + CY - STRIP * f, 1)
        fields.append(middle + one + two)
    source, potential, along, across, recombination = fields
    weight = jnp.sqrt(along * up(along))
    rise = 0.5 * (up(potential) - potential)
    below = weight * jnp.exp(rise)
    above = weight * jnp.exp(-rise)
    diagonal = recombination + above + down(below)
    weight = jnp.sqrt(across * left(across))
    rise = 0.5 * (left(potential) - potential)
    east = weight * jnp.exp(rise)
    west = weight * jnp.exp(-rise)
    diagonal = diagonal + west + right(east)
    faces = (below, down(above), east, right(west))
    coefs[0] = diagonal
    for f in range(4):
        coefs[1 + f] = faces[f]
    source = jnp.where(lanes_of((PX, LW)) < PY, source, 0.0)
    patch[...] = source
    own = own_mask((PX, LW), 0)
    square = total(jnp.where(own, source * source, 0.0))
    local = relax(source[8:56], diagonal[8:56], [face[8:56] for face in faces])
    solved[...] = jnp.where(own_mask((48, LW), 8), local, 0.0)
    live[...] = (rows_of((K, 128)) < counts[0, 0]).astype(f32)
    residual = restrict(basis, source, tiles, flat) * live[:, 0:1]
    row = to_row(residual)
    row = jnp.where(lanes_of((1, 128)) == SCALARS, square, row)
    gather[...] = jnp.broadcast_to(row, gather.shape)


def put(scalars, at, value):
    scalars[pl.ds(at, 1), :] = jnp.broadcast_to(value, (1, 128))


def got(scalars, at):
    return scalars[pl.ds(at, 1), :][:, 0:1]


def spread_first(
    suby, live, rows, inverse, basis, solved, part, odd, even, weights, scalars, coarse, tiles, flat
):
    sums = unpacked(rows, coarse, suby)
    square = pick(sums, SCALARS)
    norm = jnp.sqrt(square + EPSILON)
    scale = 1.0 / norm
    solution = coarse_solve(inverse, coarse) * live[:, 0:1] * scale
    weights[...] = jnp.broadcast_to(solution, (K, 128))
    put(scalars, 0, norm)
    put(scalars, 1, square / (square + EPSILON))
    part[...] = prolong(basis, solution, tiles, flat)
    part[8:56, :] = part[8:56, :] + solved[...] * scale
    odd[...], even[...] = to_pairs("gx", part[PX // 2 :, :], part[: PX // 2, :])
    odd[:, LIVE:] = live[:, : LW - LIVE]
    even[:, LIVE:] = live[:, : LW - LIVE]


def fold_rows(part, row_odd, row_even, folded, odd, even):
    height = folded.shape[0]
    first = (PX - height) // 2
    before, after = from_pairs("gx", row_odd[...], row_even[...])
    whole = part[first : first + height, :] + jnp.concatenate([before, after], axis=0)
    whole = jnp.where(lanes_of(whole.shape) < PY, whole, 0.0)
    folded[...] = whole
    lanes = lanes_of((height, 128))
    moved = pltpu.roll(whole, LW - 255, 1)
    odd[...], even[...] = to_pairs(
        "gy",
        jnp.where(lanes < 33, moved[:, :128], 0.0),
        jnp.where(lanes < 33, whole[:, :128], 0.0),
    )


def folded_columns(folded, odd, even):
    height = folded.shape[0]
    zero = jnp.zeros((height, 256), f32)
    from_left, from_right = from_pairs("gy", odd[...], even[...])
    one = pltpu.roll(jnp.concatenate([from_left, zero], axis=1), LW - 1, 1)
    two = jnp.concatenate([zero, from_right], axis=1)
    return folded[...] + one + two


def apply_first(
    suby, live, folded, odd, even, coefs, patch, scalars, basis, row_odd, row_even, half_odd, half_even,
    direction, image, solved, gather, tiles, flat,
):
    field = folded_columns(folded, odd, even)
    direction[...] = field[OV : OV + CX]
    diagonal = coefs[0]
    faces = [coefs[1 + f] for f in range(4)]
    shape = (PX, LW)
    rows, lanes = rows_of(shape), lanes_of(shape)
    inner = (rows >= 1) & (rows < PX - 1) & (lanes < PY)
    vector = jnp.where(inner, operate(field, diagonal, faces), 0.0)
    image[...] = vector[OV : OV + CX]
    own = own_mask((CX, LW), OV)
    mine = jnp.where(own, vector[OV : OV + CX], 0.0)
    first = patch[OV : OV + CX] * (1.0 / got(scalars, 0))
    cross = total(mine * first)
    square = total(mine * mine)
    local = relax(vector[8:56], diagonal[8:56], [face[8:56] for face in faces])
    solved[...] = jnp.where(own_mask((48, LW), 8), local, 0.0)
    residual = restrict(basis, vector, tiles, flat) * live[:, 0:1]
    fourth = vector[32:40]
    third = pltpu.roll(vector[24:32], 96, 1)
    for_next = for_before = jnp.zeros((K, 128), f32)
    for t in range(3):
        cols = slice(t * 128, (t + 1) * 128)
        at = slice(160 + t * K, 160 + (t + 1) * K)
        before, after = from_pairs("gx", row_odd[at, :], row_even[at, :])
        for_next = for_next + after * fourth[0:1, cols]
        for_before = for_before + before * third[7:8, cols]
    before, after = from_pairs(
        "gx", half_odd[:, LIVE : LIVE + 1], half_even[:, LIVE : LIVE + 1]
    )
    for_next = after * jnp.sum(for_next, axis=1, keepdims=True)
    for_before = before * jnp.sum(for_before, axis=1, keepdims=True)
    row = to_row(residual)
    row = row + pltpu.roll(to_row(for_next), 32, 1)
    row = row + pltpu.roll(to_row(for_before), 64, 1)
    lanes = lanes_of((1, 128))
    row = jnp.where(lanes == SCALARS, cross, jnp.where(lanes == SCALARS + 1, square, row))
    gather[...] = jnp.broadcast_to(row, gather.shape)


def spread_second(
    suby, live, rows, inverse, basis, solved_first, solved, weights, scalars_in,
    part, odd, even, scalars, coarse, tiles, flat,
):
    sums = gathered(rows, coarse, suby)
    cross = pick(sums, SCALARS)
    square = pick(sums, SCALARS + 1)
    norm = got(scalars_in, 0)
    unit = got(scalars_in, 1)
    rest = square - 2.0 * cross * cross + cross * cross * unit
    second = jnp.sqrt(jnp.maximum(rest, 0.0) + EPSILON)
    scale = 1.0 / second
    solution = coarse_solve(inverse, coarse) * live[:, 0:1]
    solution = (solution - cross * weights[:, 0:1]) * scale
    put(scalars, 0, norm)
    put(scalars, 1, unit)
    put(scalars, 2, cross)
    put(scalars, 3, second)
    part[...] = prolong(basis, solution, tiles, flat)
    local = (solved[...] - (cross / norm) * solved_first[...]) * scale
    part[8:56, :] = part[8:56, :] + local
    odd[...], even[...] = to_pairs("gx", part[40:, :], part[:24, :])


def apply_second(
    folded, odd, even, coefs, patch, image, scalars, direction, third, gather
):
    field = folded_columns(folded, odd, even)
    vector = operate(field, coefs[0, 8:56, :], [coefs[1 + f, 8:56, :] for f in range(4)])
    own = own_mask((CX, LW), OV)
    direction[...] = field[8 : 8 + CX]
    vector = jnp.where(own, vector[8 : 8 + CX], 0.0)
    third[...] = vector
    first = jnp.where(own, patch[OV : OV + CX] * (1.0 / got(scalars, 0)), 0.0)
    second = (image[...] - got(scalars, 2) * first) * (1.0 / got(scalars, 3))
    second = jnp.where(own, second, 0.0)
    lanes = lanes_of((1, 128))
    row = jnp.zeros((1, 128), f32)
    for lane, value in enumerate(
        (first * vector, second * vector, vector * vector, first * second, second * second)
    ):
        row = jnp.where(lanes == lane, total(value), row)
    gather[...] = jnp.broadcast_to(row, gather.shape)


def add_rows(rows, gather):
    row = jnp.sum(rows[...], axis=0, keepdims=True)
    gather[...] = jnp.broadcast_to(row, gather.shape)


def finish(rows, patch, image, third_image, direction_one, direction_two, scalars, solution, residual):
    sums = jnp.sum(rows[...], axis=0, keepdims=True)
    first_second = pick(sums, 0)
    second_second = pick(sums, 1)
    square = pick(sums, 2)
    cross = pick(sums, 3)
    unit_two = pick(sums, 4)
    source_norm = got(scalars, 0)
    unit = got(scalars, 1)
    first_first = got(scalars, 2)
    second_first = got(scalars, 3)
    rest = square - first_second * first_second * (2.0 - unit)
    rest = rest - second_second * second_second * (2.0 - unit_two)
    rest = rest + 2.0 * first_second * second_second * cross
    third_second = jnp.sqrt(jnp.maximum(rest, 0.0) + EPSILON)
    radius = jnp.sqrt(first_first * first_first + second_first * second_first)
    cosine = first_first / radius
    sine = second_first / radius
    upper_right = cosine * first_second + sine * second_second
    lower_right = cosine * second_second - sine * first_second
    radius_two = jnp.sqrt(lower_right * lower_right + third_second * third_second)
    weight_two = lower_right / radius_two * (-sine * source_norm) / radius_two
    weight_one = (cosine * source_norm - upper_right * weight_two) / radius
    remainder_one = source_norm - first_first * weight_one - first_second * weight_two
    remainder_two = -second_first * weight_one - second_second * weight_two
    remainder_three = -third_second * weight_two
    first = patch[OV : OV + CX] * (1.0 / source_norm)
    second = (image[...] - first_first * first) * (1.0 / second_first)
    third = (third_image[...] - first_second * first - second_second * second) * (1.0 / third_second)
    found = weight_one * direction_one[...] + weight_two * direction_two[...]
    left_over = remainder_one * first + remainder_two * second + remainder_three * third
    solution[...] = pltpu.roll(found, LW - OV, 1)[:, :CY]
    residual[...] = pltpu.roll(left_over, LW - OV, 1)[:, :CY]


def shape_of(*dims):
    return jax.ShapeDtypeStruct(dims, f32)


VMEM = pl.BlockSpec(memory_space=pltpu.VMEM)
PARAMS = pltpu.CompilerParams(vmem_limit_bytes=24 * 1024 * 1024)


def kernel(body, outs, scratch=(), first_smem=False):
    def call(*args):
        specs = [VMEM] * len(args)
        if first_smem:
            specs[0] = pl.BlockSpec(memory_space=pltpu.SMEM)
        return pl.pallas_call(
            body,
            out_shape=outs,
            in_specs=specs,
            out_specs=[VMEM] * len(outs),
            scratch_shapes=list(scratch),
            compiler_params=PARAMS,
        )(*args)

    return call


def swap(axis, odd, even):
    count = lax.axis_size(axis)
    even = lax.ppermute(even, axis, [(i, i ^ 1) for i in range(count)])
    odd = lax.ppermute(
        odd, axis, [(i, i + 1 if i % 2 else i - 1) for i in range(1, count - 1)]
    )
    return odd, even


def everywhere(rows, axes=AXES):
    count = lax.axis_size(axes)
    slots = rows.reshape(count, rows.shape[0] // count, 128)
    return lax.all_to_all(slots, axes, 0, 0).reshape(rows.shape)


def on_device(
    source, potential, mobility_along, mobility_across, recombination, counts, basis, coarse_inverse
):
    suby = lax.axis_size("gy")
    devices = lax.axis_size("gx") * suby
    rows = shape_of(devices, 128)
    patch_shape, own_shape = shape_of(PX, LW), shape_of(CX, LW)
    tiles = pltpu.VMEM((3, PX, 128), f32)
    flat = pltpu.VMEM((9, GROUPS, 128), f32)
    coarse = pltpu.VMEM((devices // 4, 128), f32)
    fields = (source, potential, mobility_along, mobility_across, recombination)

    def bind(body):
        def run(*refs):
            return body(suby, *refs)

        return run

    edge = pltpu.VMEM((K, 3 * 128), f32)
    held, odd, even = pl.pallas_call(
        pack_rows,
        out_shape=[shape_of(5, CX, CY), shape_of(256, 128), shape_of(256, 128)],
        in_specs=[pl.BlockSpec(memory_space=pltpu.HBM)] * 6,
        out_specs=[VMEM] * 3,
        scratch_shapes=[edge, edge, pltpu.SemaphoreType.DMA((7,))],
        compiler_params=PARAMS,
    )(*[pltpu.with_memory_space_constraint(x, pltpu.HBM) for x in (*fields, basis)])
    row_odd, row_even = swap("gx", odd, even)
    strip = shape_of(PX, 128)
    grown, odd, even = kernel(pack_columns, [shape_of(5, PX, CY), strip, strip])(
        held, row_odd, row_even
    )
    odd, even = swap("gy", odd, even)
    live, patch, coefs, solved_one, row = kernel(
        bind(prepare),
        [shape_of(K, 128), patch_shape, shape_of(5, PX, LW), shape_of(48, LW), shape_of(suby, 128)],
        [tiles, flat],
        True,
    )(counts, grown, odd, even, basis)
    (row,) = kernel(compact, [shape_of(devices // suby * slot_rows(suby), 128)])(
        everywhere(row, "gy")
    )
    half = shape_of(PX // 2, LW)
    part, odd, even, weights, scalars_one = kernel(
        bind(spread_first),
        [patch_shape, half, half, shape_of(K, 128), shape_of(8, 128)],
        [coarse, tiles, flat],
    )(live, everywhere(row, "gx"), coarse_inverse, basis, solved_one)
    half_odd, half_even = swap("gx", odd, even)
    folded, odd, even = kernel(fold_rows, [patch_shape, strip, strip])(part, half_odd, half_even)
    odd, even = swap("gy", odd, even)
    direction_one, image_one, solved_two, row = kernel(
        bind(apply_first),
        [own_shape, own_shape, shape_of(48, LW), rows],
        [tiles, flat],
    )(
        live, folded, odd, even, coefs, patch, scalars_one, basis,
        row_odd, row_even, half_odd, half_even,
    )
    half = shape_of(24, LW)
    part, odd, even, scalars_two = kernel(
        bind(spread_second),
        [patch_shape, half, half, shape_of(8, 128)],
        [coarse, tiles, flat],
    )(
        live, everywhere(row), coarse_inverse, basis, solved_one, solved_two, weights, scalars_one
    )
    half_odd, half_even = swap("gx", odd, even)
    strip = shape_of(48, 128)
    folded, odd, even = kernel(fold_rows, [shape_of(48, LW), strip, strip])(
        part, half_odd, half_even
    )
    odd, even = swap("gy", odd, even)
    direction_two, image_two, row = kernel(
        apply_second, [own_shape, own_shape, shape_of(devices // suby, 128)]
    )(
        folded, odd, even, coefs, patch, image_one, scalars_two
    )
    (row,) = kernel(add_rows, [shape_of(suby, 128)])(everywhere(row, "gx"))
    out = shape_of(CX, CY)
    answer, residual = kernel(finish, [out, out])(
        everywhere(row, "gy"), patch, image_one, image_two, direction_one, direction_two, scalars_two
    )
    return answer, residual


def solution(mesh):
    grid = P("gx", "gy")
    return jax.shard_map(
        on_device,
        mesh=mesh,
        in_specs=(grid,) * 7 + (P(("gx", "gy"), None),),
        out_specs=(grid, grid),
        check_vma=False,
    )
```

```python
import jax
import jax.numpy as jnp
from jax import lax
from jax.experimental import pallas as pl
from jax.experimental.pallas import tpu as pltpu
from jax.sharding import PartitionSpec as P

OV = 16
SWEEPS = 8
OMEGA = 0.8
EPSILON = 1e-06
CX = 32
CY = 256
K = 32
PX = CX + 2 * OV
PY = CY + 2 * OV
LW = 384
GROUPS = PX // 4
STRIP = 24
LIVE = PY
SCALARS = 96
f32 = jnp.float32
AXES = ("gx", "gy")


def lanes_of(shape):
    return lax.broadcasted_iota(jnp.int32, shape, len(shape) - 1)


def rows_of(shape):
    return lax.broadcasted_iota(jnp.int32, shape, len(shape) - 2)


def left(x):
    return pltpu.roll(x, LW - 1, 1)


def right(x):
    return pltpu.roll(x, 1, 1)


def up(x):
    return pltpu.roll(x, x.shape[0] - 1, 0)


def down(x):
    return pltpu.roll(x, 1, 0)


def own_mask(shape, first):
    rows, lanes = rows_of(shape) + first, lanes_of(shape)
    return (rows >= OV) & (rows < OV + CX) & (lanes >= OV) & (lanes < OV + CY)


def is_even(axis):
    return lax.rem(lax.axis_index(axis), 2) == 0


def to_pairs(axis, ahead, back):
    even = is_even(axis)
    return jnp.where(even, back, ahead), jnp.where(even, ahead, back)


def from_pairs(axis, odd, even_pairs):
    even = is_even(axis)
    return jnp.where(even, odd, even_pairs), jnp.where(even, even_pairs, odd)


def total(x):
    return jnp.sum(jnp.sum(x, axis=0, keepdims=True), axis=1, keepdims=True)


def to_row(column):
    shape = (K, 128)
    spread = jnp.broadcast_to(column, shape)
    return jnp.sum(jnp.where(rows_of(shape) == lanes_of(shape), spread, 0.0), axis=0, keepdims=True)


def restrict(basis, patch, tiles, flat):
    for t in range(3):
        tiles[t] = patch[:, t * 128 : (t + 1) * 128]
    parts = [None] * 9
    for m in range(4):
        rows = jnp.concatenate(
            [tiles[t, pl.ds(m, GROUPS, stride=4), :] for t in range(3)], axis=1
        )
        if m:
            rows = pltpu.roll(rows, 32 * m, 1)
        for t in range(3):
            piece = rows[:, t * 128 : (t + 1) * 128]
            at = 2 * m + t
            parts[at] = piece if parts[at] is None else parts[at] + piece
    for t in range(9):
        flat[t] = parts[t]
    sums = [jnp.zeros((K, 128), f32) for _ in range(3)]
    for g in range(GROUPS):
        for t in range(9):
            block = (g * 9 + t) * 128
            row = jnp.broadcast_to(flat[t, pl.ds(g, 1), :], (K, 128))
            sums[t % 3] = sums[t % 3] + basis[:, block : block + 128] * row
    return jnp.sum(sums[0] + sums[1] + sums[2], axis=1, keepdims=True)


def prolong(basis, weights, tiles, flat):
    wide = jnp.broadcast_to(weights, (K, 128))
    for g in range(GROUPS):
        for t in range(9):
            block = (g * 9 + t) * 128
            flat[t, pl.ds(g, 1), :] = jnp.sum(
                basis[:, block : block + 128] * wide, axis=0, keepdims=True
            )
    for m in range(4):
        rows = jnp.concatenate([flat[2 * m + t] for t in range(3)], axis=1)
        if m:
            rows = pltpu.roll(rows, LW - 32 * m, 1)
        rows = jnp.where(lanes_of(rows.shape) < PY, rows, 0.0)
        for t in range(3):
            tiles[t, pl.ds(m, GROUPS, stride=4), :] = rows[:, t * 128 : (t + 1) * 128]
    return jnp.concatenate([tiles[t] for t in range(3)], axis=1)


def gathered(rows, coarse, suby):
    count = rows.shape[0] // 4
    shift = suby // 4
    taken = [rows[pl.ds(q, count, stride=4), :] for q in range(4)]
    zero = jnp.zeros((shift, 128), f32)
    lanes = lanes_of((count, 128))
    result = None
    for s in range(4):
        own = taken[s]
        later = jnp.concatenate([zero, taken[(s + 1) % 4][: count - shift]], axis=0)
        earlier = jnp.concatenate([taken[(s + 2) % 4][shift:], zero], axis=0)
        piece = jnp.where(
            lanes < 32, own, jnp.where(lanes < 64, later, jnp.where(lanes < 96, earlier, 0.0))
        )
        if s:
            piece = pltpu.roll(piece, 32 * s, 1)
        result = piece if result is None else result + piece
    coarse[...] = result
    return jnp.sum(taken[0] + taken[1] + (taken[2] + taken[3]), axis=0, keepdims=True)


def compact(rows, gather):
    count = rows.shape[0] // 4
    slot = slot_rows(rows.shape[0])
    taken = [rows[pl.ds(q, count, stride=4), :] for q in range(4)]
    lanes = lanes_of((count, 128))
    result = None
    for q in range(4):
        piece = jnp.where(lanes < 32, taken[q], 0.0)
        if q:
            piece = pltpu.roll(piece, 32 * q, 1)
        result = piece if result is None else result + piece
    sums = jnp.sum(taken[0] + taken[1] + (taken[2] + taken[3]), axis=0, keepdims=True)
    tail = jnp.broadcast_to(sums, (slot - count, 128))
    block = jnp.concatenate([result, tail], axis=0)
    for at in range(0, gather.shape[0], slot):
        gather[at : at + slot, :] = block


def slot_rows(suby):
    return suby // 4 + 8


def unpacked(rows, coarse, suby):
    count, slot = suby // 4, slot_rows(suby)
    sums = None
    for i in range(rows.shape[0] // slot):
        coarse[i * count : (i + 1) * count, :] = rows[i * slot : i * slot + count, :]
        row = rows[i * slot + count : i * slot + count + 1, :]
        sums = row if sums is None else sums + row
    return sums


def pick(row, lane):
    return jnp.sum(jnp.where(lanes_of(row.shape) == lane, row, 0.0), axis=1, keepdims=True)


def coarse_solve(inverse, coarse):
    sums = [jnp.zeros((K, 128), f32) for _ in range(4)]
    for b in range(coarse.shape[0]):
        row = jnp.broadcast_to(coarse[pl.ds(b, 1), :], (K, 128))
        sums[b % 4] = sums[b % 4] + inverse[:, b * 128 : (b + 1) * 128] * row
    return jnp.sum((sums[0] + sums[1]) + (sums[2] + sums[3]), axis=1, keepdims=True)


def relax(vector, diagonal, faces):
    inverse = OMEGA / jnp.where(diagonal > 0.0, diagonal, 1.0)
    below, above, east, west = [inverse * face for face in faces]
    start = inverse * vector
    field = start
    for _ in range(SWEEPS - 1):
        moved = below * up(field) + above * down(field)
        moved = moved + (east * left(field) + west * right(field))
        field = (start + (1.0 - OMEGA) * field) + moved
    return field


def operate(field, diagonal, faces):
    below, above, east, west = faces
    moved = below * up(field) + above * down(field)
    moved = moved + (east * left(field) + west * right(field))
    return diagonal * field - moved


def pack_rows(
    source, potential, along, across, recombination, basis, held, odd, even, head, tail, sems
):
    edge = head.shape[1]
    copies = [
        pltpu.make_async_copy(field, held.at[f], sems.at[f])
        for f, field in enumerate((source, potential, along, across, recombination))
    ]
    copies.append(pltpu.make_async_copy(basis.at[:, :edge], head, sems.at[5]))
    copies.append(
        pltpu.make_async_copy(basis.at[:, basis.shape[1] - edge :], tail, sems.at[6])
    )
    for copy in copies:
        copy.start()
    for copy in copies:
        copy.wait()
    for f in range(5):
        for t in range(2):
            at = slice((2 * f + t) * OV, (2 * f + t + 1) * OV)
            cols = slice(t * 128, (t + 1) * 128)
            odd[at, :], even[at, :] = to_pairs(
                "gx", held[f, CX - OV :, cols], held[f, :OV, cols]
            )
    for t in range(3):
        at = slice(160 + t * K, 160 + (t + 1) * K)
        cols = slice(t * 128, (t + 1) * 128)
        odd[at, :], even[at, :] = to_pairs("gx", tail[:, cols], head[:, cols])


def pack_columns(held, row_odd, row_even, rows, odd, even):
    before, after = from_pairs("gx", row_odd[: 10 * OV, :], row_even[: 10 * OV, :])
    lanes = lanes_of((PX, 128))
    to_right = to_left = None
    for f in range(5):
        tiles = []
        for t in range(2):
            at = (2 * f + t) * OV
            cols = slice(t * 128, (t + 1) * 128)
            tile = jnp.concatenate(
                [before[at : at + OV, :], held[f, :, cols], after[at : at + OV, :]], axis=0
            )
            rows[f, :, cols] = tile
            tiles.append(tile)
        last = pltpu.roll(jnp.where(lanes >= 111, tiles[1], 0.0), 17 + STRIP * f, 1)
        first = jnp.where(lanes < 17, tiles[0], 0.0)
        if f:
            first = pltpu.roll(first, STRIP * f, 1)
        to_right = last if f == 0 else to_right + last
        to_left = first if f == 0 else to_left + first
    odd[...], even[...] = to_pairs("gy", to_right, to_left)


def prepare(suby, counts, rows, odd, even, basis, live, patch, coefs, solved, gather, tiles, flat):
    zero = jnp.zeros((PX, LW - CY), f32)
    lanes = lanes_of((PX, 128))
    from_left, from_right = from_pairs("gy", odd[...], even[...])
    fields = []
    for f in range(5):
        middle = pltpu.roll(jnp.concatenate([rows[f], zero], axis=1), OV, 1)
        band = (lanes >= STRIP * f) & (lanes < STRIP * f + 17)
        wide = jnp.zeros((PX, LW - 128), f32)
        one = jnp.concatenate([jnp.where(band, from_left, 0.0), wide], axis=1)
        two = jnp.concatenate([jnp.where(band, from_right, 0.0), wide], axis=1)
        one = pltpu.roll(one, LW - 1 - STRIP * f, 1)
        two = pltpu.roll(two, OV + CY - STRIP * f, 1)
        fields.append(middle + one + two)
    source, potential, along, across, recombination = fields
    weight = jnp.sqrt(along * up(along))
    rise = 0.5 * (up(potential) - potential)
    below = weight * jnp.exp(rise)
    above = weight * jnp.exp(-rise)
    diagonal = recombination + above + down(below)
    weight = jnp.sqrt(across * left(across))
    rise = 0.5 * (left(potential) - potential)
    east = weight * jnp.exp(rise)
    west = weight * jnp.exp(-rise)
    diagonal = diagonal + west + right(east)
    faces = (below, down(above), east, right(west))
    coefs[0] = diagonal
    for f in range(4):
        coefs[1 + f] = faces[f]
    source = jnp.where(lanes_of((PX, LW)) < PY, source, 0.0)
    patch[...] = source
    own = own_mask((PX, LW), 0)
    square = total(jnp.where(own, source * source, 0.0))
    local = relax(source[8:56], diagonal[8:56], [face[8:56] for face in faces])
    solved[...] = jnp.where(own_mask((48, LW), 8), local, 0.0)
    live[...] = (rows_of((K, 128)) < counts[0, 0]).astype(f32)
    residual = restrict(basis, source, tiles, flat) * live[:, 0:1]
    row = to_row(residual)
    row = jnp.where(lanes_of((1, 128)) == SCALARS, square, row)
    gather[...] = jnp.broadcast_to(row, gather.shape)


def put(scalars, at, value):
    scalars[pl.ds(at, 1), :] = jnp.broadcast_to(value, (1, 128))


def got(scalars, at):
    return scalars[pl.ds(at, 1), :][:, 0:1]


def spread_first(
    suby, live, rows, inverse, basis, solved, part, odd, even, weights, scalars, coarse, tiles, flat
):
    sums = unpacked(rows, coarse, suby)
    square = pick(sums, SCALARS)
    norm = jnp.sqrt(square + EPSILON)
    scale = 1.0 / norm
    solution = coarse_solve(inverse, coarse) * live[:, 0:1] * scale
    weights[...] = jnp.broadcast_to(solution, (K, 128))
    put(scalars, 0, norm)
    put(scalars, 1, square / (square + EPSILON))
    part[...] = prolong(basis, solution, tiles, flat)
    part[8:56, :] = part[8:56, :] + solved[...] * scale
    odd[...], even[...] = to_pairs("gx", part[PX // 2 :, :], part[: PX // 2, :])
    odd[:, LIVE:] = live[:, : LW - LIVE]
    even[:, LIVE:] = live[:, : LW - LIVE]


def fold_rows(part, row_odd, row_even, folded, odd, even):
    height = folded.shape[0]
    first = (PX - height) // 2
    before, after = from_pairs("gx", row_odd[...], row_even[...])
    whole = part[first : first + height, :] + jnp.concatenate([before, after], axis=0)
    whole = jnp.where(lanes_of(whole.shape) < PY, whole, 0.0)
    folded[...] = whole
    lanes = lanes_of((height, 128))
    moved = pltpu.roll(whole, LW - 255, 1)
    odd[...], even[...] = to_pairs(
        "gy",
        jnp.where(lanes < 33, moved[:, :128], 0.0),
        jnp.where(lanes < 33, whole[:, :128], 0.0),
    )


def folded_columns(folded, odd, even):
    height = folded.shape[0]
    zero = jnp.zeros((height, 256), f32)
    from_left, from_right = from_pairs("gy", odd[...], even[...])
    one = pltpu.roll(jnp.concatenate([from_left, zero], axis=1), LW - 1, 1)
    two = jnp.concatenate([zero, from_right], axis=1)
    return folded[...] + one + two


def apply_first(
    suby, live, folded, odd, even, coefs, patch, scalars, basis, row_odd, row_even, half_odd, half_even,
    direction, image, solved, gather, tiles, flat,
):
    field = folded_columns(folded, odd, even)
    direction[...] = field[OV : OV + CX]
    diagonal = coefs[0]
    faces = [coefs[1 + f] for f in range(4)]
    shape = (PX, LW)
    rows, lanes = rows_of(shape), lanes_of(shape)
    inner = (rows >= 1) & (rows < PX - 1) & (lanes < PY)
    vector = jnp.where(inner, operate(field, diagonal, faces), 0.0)
    image[...] = vector[OV : OV + CX]
    own = own_mask((CX, LW), OV)
    mine = jnp.where(own, vector[OV : OV + CX], 0.0)
    first = patch[OV : OV + CX] * (1.0 / got(scalars, 0))
    cross = total(mine * first)
    square = total(mine * mine)
    local = relax(vector[8:56], diagonal[8:56], [face[8:56] for face in faces])
    solved[...] = jnp.where(own_mask((48, LW), 8), local, 0.0)
    residual = restrict(basis, vector, tiles, flat) * live[:, 0:1]
    fourth = vector[32:40]
    third = pltpu.roll(vector[24:32], 96, 1)
    for_next = for_before = jnp.zeros((K, 128), f32)
    for t in range(3):
        cols = slice(t * 128, (t + 1) * 128)
        at = slice(160 + t * K, 160 + (t + 1) * K)
        before, after = from_pairs("gx", row_odd[at, :], row_even[at, :])
        for_next = for_next + after * fourth[0:1, cols]
        for_before = for_before + before * third[7:8, cols]
    before, after = from_pairs(
        "gx", half_odd[:, LIVE : LIVE + 1], half_even[:, LIVE : LIVE + 1]
    )
    for_next = after * jnp.sum(for_next, axis=1, keepdims=True)
    for_before = before * jnp.sum(for_before, axis=1, keepdims=True)
    row = to_row(residual)
    row = row + pltpu.roll(to_row(for_next), 32, 1)
    row = row + pltpu.roll(to_row(for_before), 64, 1)
    lanes = lanes_of((1, 128))
    row = jnp.where(lanes == SCALARS, cross, jnp.where(lanes == SCALARS + 1, square, row))
    gather[...] = jnp.broadcast_to(row, gather.shape)


def spread_second(
    suby, live, rows, inverse, basis, solved_first, solved, weights, scalars_in,
    part, odd, even, scalars, coarse, tiles, flat,
):
    sums = gathered(rows, coarse, suby)
    cross = pick(sums, SCALARS)
    square = pick(sums, SCALARS + 1)
    norm = got(scalars_in, 0)
    unit = got(scalars_in, 1)
    rest = square - 2.0 * cross * cross + cross * cross * unit
    second = jnp.sqrt(jnp.maximum(rest, 0.0) + EPSILON)
    scale = 1.0 / second
    solution = coarse_solve(inverse, coarse) * live[:, 0:1]
    solution = (solution - cross * weights[:, 0:1]) * scale
    put(scalars, 0, norm)
    put(scalars, 1, unit)
    put(scalars, 2, cross)
    put(scalars, 3, second)
    part[...] = prolong(basis, solution, tiles, flat)
    local = (solved[...] - (cross / norm) * solved_first[...]) * scale
    part[8:56, :] = part[8:56, :] + local
    odd[...], even[...] = to_pairs("gx", part[40:, :], part[:24, :])


def apply_second(
    folded, odd, even, coefs, patch, image, scalars, direction, third, gather
):
    field = folded_columns(folded, odd, even)
    vector = operate(field, coefs[0, 8:56, :], [coefs[1 + f, 8:56, :] for f in range(4)])
    own = own_mask((CX, LW), OV)
    direction[...] = field[8 : 8 + CX]
    vector = jnp.where(own, vector[8 : 8 + CX], 0.0)
    third[...] = vector
    first = jnp.where(own, patch[OV : OV + CX] * (1.0 / got(scalars, 0)), 0.0)
    second = (image[...] - got(scalars, 2) * first) * (1.0 / got(scalars, 3))
    second = jnp.where(own, second, 0.0)
    lanes = lanes_of((1, 128))
    row = jnp.zeros((1, 128), f32)
    for lane, value in enumerate(
        (first * vector, second * vector, vector * vector, first * second, second * second)
    ):
        row = jnp.where(lanes == lane, total(value), row)
    gather[...] = jnp.broadcast_to(row, gather.shape)


def add_rows(rows, gather):
    row = jnp.sum(rows[...], axis=0, keepdims=True)
    gather[...] = jnp.broadcast_to(row, gather.shape)


def finish(rows, patch, image, third_image, direction_one, direction_two, scalars, solution, residual):
    sums = jnp.sum(rows[...], axis=0, keepdims=True)
    first_second = pick(sums, 0)
    second_second = pick(sums, 1)
    square = pick(sums, 2)
    cross = pick(sums, 3)
    unit_two = pick(sums, 4)
    source_norm = got(scalars, 0)
    unit = got(scalars, 1)
    first_first = got(scalars, 2)
    second_first = got(scalars, 3)
    rest = square - first_second * first_second * (2.0 - unit)
    rest = rest - second_second * second_second * (2.0 - unit_two)
    rest = rest + 2.0 * first_second * second_second * cross
    third_second = jnp.sqrt(jnp.maximum(rest, 0.0) + EPSILON)
    radius = jnp.sqrt(first_first * first_first + second_first * second_first)
    cosine = first_first / radius
    sine = second_first / radius
    upper_right = cosine * first_second + sine * second_second
    lower_right = cosine * second_second - sine * first_second
    radius_two = jnp.sqrt(lower_right * lower_right + third_second * third_second)
    weight_two = lower_right / radius_two * (-sine * source_norm) / radius_two
    weight_one = (cosine * source_norm - upper_right * weight_two) / radius
    remainder_one = source_norm - first_first * weight_one - first_second * weight_two
    remainder_two = -second_first * weight_one - second_second * weight_two
    remainder_three = -third_second * weight_two
    first = patch[OV : OV + CX] * (1.0 / source_norm)
    second = (image[...] - first_first * first) * (1.0 / second_first)
    third = (third_image[...] - first_second * first - second_second * second) * (1.0 / third_second)
    found = weight_one * direction_one[...] + weight_two * direction_two[...]
    left_over = remainder_one * first + remainder_two * second + remainder_three * third
    solution[...] = pltpu.roll(found, LW - OV, 1)[:, :CY]
    residual[...] = pltpu.roll(left_over, LW - OV, 1)[:, :CY]


def shape_of(*dims):
    return jax.ShapeDtypeStruct(dims, f32)


VMEM = pl.BlockSpec(memory_space=pltpu.VMEM)
PARAMS = pltpu.CompilerParams(vmem_limit_bytes=24 * 1024 * 1024)


def kernel(body, outs, scratch=(), first_smem=False):
    def call(*args):
        specs = [VMEM] * len(args)
        if first_smem:
            specs[0] = pl.BlockSpec(memory_space=pltpu.SMEM)
        return pl.pallas_call(
            body,
            out_shape=outs,
            in_specs=specs,
            out_specs=[VMEM] * len(outs),
            scratch_shapes=list(scratch),
            compiler_params=PARAMS,
        )(*args)

    return call


def swap(axis, odd, even):
    count = lax.axis_size(axis)
    even = lax.ppermute(even, axis, [(i, i ^ 1) for i in range(count)])
    odd = lax.ppermute(
        odd, axis, [(i, i + 1 if i % 2 else i - 1) for i in range(1, count - 1)]
    )
    return odd, even


def everywhere(rows, axes=AXES):
    count = lax.axis_size(axes)
    slots = rows.reshape(count, rows.shape[0] // count, 128)
    return lax.all_to_all(slots, axes, 0, 0).reshape(rows.shape)


def on_device(
    source, potential, mobility_along, mobility_across, recombination, counts, basis, coarse_inverse
):
    suby = lax.axis_size("gy")
    devices = lax.axis_size("gx") * suby
    rows = shape_of(devices, 128)
    patch_shape, own_shape = shape_of(PX, LW), shape_of(CX, LW)
    tiles = pltpu.VMEM((3, PX, 128), f32)
    flat = pltpu.VMEM((9, GROUPS, 128), f32)
    coarse = pltpu.VMEM((devices // 4, 128), f32)
    fields = (source, potential, mobility_along, mobility_across, recombination)

    def bind(body):
        def run(*refs):
            return body(suby, *refs)

        return run

    edge = pltpu.VMEM((K, 3 * 128), f32)
    held, odd, even = pl.pallas_call(
        pack_rows,
        out_shape=[shape_of(5, CX, CY), shape_of(256, 128), shape_of(256, 128)],
        in_specs=[pl.BlockSpec(memory_space=pltpu.HBM)] * 6,
        out_specs=[VMEM] * 3,
        scratch_shapes=[edge, edge, pltpu.SemaphoreType.DMA((7,))],
        compiler_params=PARAMS,
    )(*[pltpu.with_memory_space_constraint(x, pltpu.HBM) for x in (*fields, basis)])
    row_odd, row_even = swap("gx", odd, even)
    strip = shape_of(PX, 128)
    grown, odd, even = kernel(pack_columns, [shape_of(5, PX, CY), strip, strip])(
        held, row_odd, row_even
    )
    odd, even = swap("gy", odd, even)
    live, patch, coefs, solved_one, row = kernel(
        bind(prepare),
        [shape_of(K, 128), patch_shape, shape_of(5, PX, LW), shape_of(48, LW), shape_of(suby, 128)],
        [tiles, flat],
        True,
    )(counts, grown, odd, even, basis)
    (row,) = kernel(compact, [shape_of(devices // suby * slot_rows(suby), 128)])(
        everywhere(row, "gy")
    )
    half = shape_of(PX // 2, LW)
    part, odd, even, weights, scalars_one = kernel(
        bind(spread_first),
        [patch_shape, half, half, shape_of(K, 128), shape_of(8, 128)],
        [coarse, tiles, flat],
    )(live, everywhere(row, "gx"), coarse_inverse, basis, solved_one)
    half_odd, half_even = swap("gx", odd, even)
    folded, odd, even = kernel(fold_rows, [patch_shape, strip, strip])(part, half_odd, half_even)
    odd, even = swap("gy", odd, even)
    direction_one, image_one, solved_two, row = kernel(
        bind(apply_first),
        [own_shape, own_shape, shape_of(48, LW), rows],
        [tiles, flat],
    )(
        live, folded, odd, even, coefs, patch, scalars_one, basis,
        row_odd, row_even, half_odd, half_even,
    )
    half = shape_of(24, LW)
    part, odd, even, scalars_two = kernel(
        bind(spread_second),
        [patch_shape, half, half, shape_of(8, 128)],
        [coarse, tiles, flat],
    )(
        live, everywhere(row), coarse_inverse, basis, solved_one, solved_two, weights, scalars_one
    )
    half_odd, half_even = swap("gx", odd, even)
    strip = shape_of(48, 128)
    folded, odd, even = kernel(fold_rows, [shape_of(48, LW), strip, strip])(
        part, half_odd, half_even
    )
    odd, even = swap("gy", odd, even)
    direction_two, image_two, row = kernel(
        apply_second, [own_shape, own_shape, shape_of(suby, 128)]
    )(
        folded, odd, even, coefs, patch, image_one, scalars_two
    )
    (row,) = kernel(add_rows, [shape_of(devices // suby, 128)])(everywhere(row, "gy"))
    out = shape_of(CX, CY)
    answer, residual = kernel(finish, [out, out])(
        everywhere(row, "gx"), patch, image_one, image_two, direction_one, direction_two, scalars_two
    )
    return answer, residual


def solution(mesh):
    grid = P("gx", "gy")
    return jax.shard_map(
        on_device,
        mesh=mesh,
        in_specs=(grid,) * 7 + (P(("gx", "gy"), None),),
        out_specs=(grid, grid),
        check_vma=False,
    )
```

```python
import jax
import jax.numpy as jnp
from jax import lax
from jax.experimental import pallas as pl
from jax.experimental.pallas import tpu as pltpu
from jax.sharding import PartitionSpec as P

OV = 16
SWEEPS = 8
OMEGA = 0.8
EPSILON = 1e-06
CX = 32
CY = 256
K = 32
PX = CX + 2 * OV
PY = CY + 2 * OV
LW = 384
GROUPS = PX // 4
STRIP = 24
LIVE = PY
SCALARS = 96
f32 = jnp.float32
AXES = ("gx", "gy")


def lanes_of(shape):
    return lax.broadcasted_iota(jnp.int32, shape, len(shape) - 1)


def rows_of(shape):
    return lax.broadcasted_iota(jnp.int32, shape, len(shape) - 2)


def left(x):
    return pltpu.roll(x, LW - 1, 1)


def right(x):
    return pltpu.roll(x, 1, 1)


def up(x):
    return pltpu.roll(x, x.shape[0] - 1, 0)


def down(x):
    return pltpu.roll(x, 1, 0)


def own_mask(shape, first):
    rows, lanes = rows_of(shape) + first, lanes_of(shape)
    return (rows >= OV) & (rows < OV + CX) & (lanes >= OV) & (lanes < OV + CY)


def is_even(axis):
    return lax.rem(lax.axis_index(axis), 2) == 0


def to_pairs(axis, ahead, back):
    even = is_even(axis)
    return jnp.where(even, back, ahead), jnp.where(even, ahead, back)


def from_pairs(axis, odd, even_pairs):
    even = is_even(axis)
    return jnp.where(even, odd, even_pairs), jnp.where(even, even_pairs, odd)


def total(x):
    return jnp.sum(jnp.sum(x, axis=0, keepdims=True), axis=1, keepdims=True)


def to_row(column):
    shape = (K, 128)
    spread = jnp.broadcast_to(column, shape)
    return jnp.sum(jnp.where(rows_of(shape) == lanes_of(shape), spread, 0.0), axis=0, keepdims=True)


def restrict(basis, patch, tiles, flat):
    for t in range(3):
        tiles[t] = patch[:, t * 128 : (t + 1) * 128]
    parts = [None] * 9
    for m in range(4):
        rows = jnp.concatenate(
            [tiles[t, pl.ds(m, GROUPS, stride=4), :] for t in range(3)], axis=1
        )
        if m:
            rows = pltpu.roll(rows, 32 * m, 1)
        for t in range(3):
            piece = rows[:, t * 128 : (t + 1) * 128]
            at = 2 * m + t
            parts[at] = piece if parts[at] is None else parts[at] + piece
    for t in range(9):
        flat[t] = parts[t]
    sums = [jnp.zeros((K, 128), f32) for _ in range(3)]
    for g in range(GROUPS):
        for t in range(9):
            block = (g * 9 + t) * 128
            row = jnp.broadcast_to(flat[t, pl.ds(g, 1), :], (K, 128))
            sums[t % 3] = sums[t % 3] + basis[:, block : block + 128] * row
    return jnp.sum(sums[0] + sums[1] + sums[2], axis=1, keepdims=True)


def prolong(basis, weights, tiles, flat):
    wide = jnp.broadcast_to(weights, (K, 128))
    for g in range(GROUPS):
        for t in range(9):
            block = (g * 9 + t) * 128
            flat[t, pl.ds(g, 1), :] = jnp.sum(
                basis[:, block : block + 128] * wide, axis=0, keepdims=True
            )
    for m in range(4):
        rows = jnp.concatenate([flat[2 * m + t] for t in range(3)], axis=1)
        if m:
            rows = pltpu.roll(rows, LW - 32 * m, 1)
        rows = jnp.where(lanes_of(rows.shape) < PY, rows, 0.0)
        for t in range(3):
            tiles[t, pl.ds(m, GROUPS, stride=4), :] = rows[:, t * 128 : (t + 1) * 128]
    return jnp.concatenate([tiles[t] for t in range(3)], axis=1)


def gathered(rows, coarse, suby):
    count = rows.shape[0] // 4
    shift = suby // 4
    taken = [rows[pl.ds(q, count, stride=4), :] for q in range(4)]
    zero = jnp.zeros((shift, 128), f32)
    lanes = lanes_of((count, 128))
    result = None
    for s in range(4):
        own = taken[s]
        later = jnp.concatenate([zero, taken[(s + 1) % 4][: count - shift]], axis=0)
        earlier = jnp.concatenate([taken[(s + 2) % 4][shift:], zero], axis=0)
        piece = jnp.where(
            lanes < 32, own, jnp.where(lanes < 64, later, jnp.where(lanes < 96, earlier, 0.0))
        )
        if s:
            piece = pltpu.roll(piece, 32 * s, 1)
        result = piece if result is None else result + piece
    coarse[...] = result
    return jnp.sum(taken[0] + taken[1] + (taken[2] + taken[3]), axis=0, keepdims=True)


def compact(rows, gather):
    count = rows.shape[0] // 4
    slot = slot_rows(rows.shape[0])
    taken = [rows[pl.ds(q, count, stride=4), :] for q in range(4)]
    lanes = lanes_of((count, 128))
    result = None
    for q in range(4):
        piece = jnp.where(lanes < 32, taken[q], 0.0)
        if q:
            piece = pltpu.roll(piece, 32 * q, 1)
        result = piece if result is None else result + piece
    sums = jnp.sum(taken[0] + taken[1] + (taken[2] + taken[3]), axis=0, keepdims=True)
    tail = jnp.broadcast_to(sums, (slot - count, 128))
    block = jnp.concatenate([result, tail], axis=0)
    for at in range(0, gather.shape[0], slot):
        gather[at : at + slot, :] = block


def slot_rows(suby):
    return suby // 4 + 8


def unpacked(rows, coarse, suby):
    count, slot = suby // 4, slot_rows(suby)
    sums = None
    for i in range(rows.shape[0] // slot):
        coarse[i * count : (i + 1) * count, :] = rows[i * slot : i * slot + count, :]
        row = rows[i * slot + count : i * slot + count + 1, :]
        sums = row if sums is None else sums + row
    return sums


def pick(row, lane):
    return row[:, lane : lane + 1]


def coarse_solve(inverse, coarse):
    sums = [jnp.zeros((K, 128), f32) for _ in range(4)]
    for b in range(coarse.shape[0]):
        row = jnp.broadcast_to(coarse[pl.ds(b, 1), :], (K, 128))
        sums[b % 4] = sums[b % 4] + inverse[:, b * 128 : (b + 1) * 128] * row
    return jnp.sum((sums[0] + sums[1]) + (sums[2] + sums[3]), axis=1, keepdims=True)


def relax(vector, diagonal, faces):
    inverse = OMEGA / jnp.where(diagonal > 0.0, diagonal, 1.0)
    below, above, east, west = [inverse * face for face in faces]
    start = inverse * vector
    field = start
    for _ in range(SWEEPS - 1):
        moved = below * up(field) + above * down(field)
        moved = moved + (east * left(field) + west * right(field))
        field = (start + (1.0 - OMEGA) * field) + moved
    return field


def operate(field, diagonal, faces):
    below, above, east, west = faces
    moved = below * up(field) + above * down(field)
    moved = moved + (east * left(field) + west * right(field))
    return diagonal * field - moved


def pack_rows(
    source, potential, along, across, recombination, basis, held, odd, even, head, tail, sems
):
    edge = head.shape[1]
    copies = [
        pltpu.make_async_copy(field, held.at[f], sems.at[f])
        for f, field in enumerate((source, potential, along, across, recombination))
    ]
    copies.append(pltpu.make_async_copy(basis.at[:, :edge], head, sems.at[5]))
    copies.append(
        pltpu.make_async_copy(basis.at[:, basis.shape[1] - edge :], tail, sems.at[6])
    )
    for copy in copies:
        copy.start()
    for copy in copies:
        copy.wait()
    for f in range(5):
        for t in range(2):
            at = slice((2 * f + t) * OV, (2 * f + t + 1) * OV)
            cols = slice(t * 128, (t + 1) * 128)
            odd[at, :], even[at, :] = to_pairs(
                "gx", held[f, CX - OV :, cols], held[f, :OV, cols]
            )
    for t in range(3):
        at = slice(160 + t * K, 160 + (t + 1) * K)
        cols = slice(t * 128, (t + 1) * 128)
        odd[at, :], even[at, :] = to_pairs("gx", tail[:, cols], head[:, cols])


def pack_columns(held, row_odd, row_even, rows, odd, even):
    before, after = from_pairs("gx", row_odd[: 10 * OV, :], row_even[: 10 * OV, :])
    lanes = lanes_of((PX, 128))
    to_right = to_left = None
    for f in range(5):
        tiles = []
        for t in range(2):
            at = (2 * f + t) * OV
            cols = slice(t * 128, (t + 1) * 128)
            tile = jnp.concatenate(
                [before[at : at + OV, :], held[f, :, cols], after[at : at + OV, :]], axis=0
            )
            rows[f, :, cols] = tile
            tiles.append(tile)
        last = pltpu.roll(jnp.where(lanes >= 111, tiles[1], 0.0), 17 + STRIP * f, 1)
        first = jnp.where(lanes < 17, tiles[0], 0.0)
        if f:
            first = pltpu.roll(first, STRIP * f, 1)
        to_right = last if f == 0 else to_right + last
        to_left = first if f == 0 else to_left + first
    odd[...], even[...] = to_pairs("gy", to_right, to_left)


def prepare(suby, counts, rows, odd, even, basis, live, patch, coefs, solved, gather, tiles, flat):
    zero = jnp.zeros((PX, LW - CY), f32)
    lanes = lanes_of((PX, 128))
    from_left, from_right = from_pairs("gy", odd[...], even[...])
    fields = []
    for f in range(5):
        middle = pltpu.roll(jnp.concatenate([rows[f], zero], axis=1), OV, 1)
        band = (lanes >= STRIP * f) & (lanes < STRIP * f + 17)
        one = pltpu.roll(jnp.where(band, from_left, 0.0), 127 - STRIP * f, 1)
        two = pltpu.roll(jnp.where(band, from_right, 0.0), (128 + OV - STRIP * f) % 128, 1)
        one, end = jnp.where(lanes < OV, one, 0.0), jnp.where(lanes == 127, one, 0.0)
        sides = jnp.concatenate([one, jnp.zeros((PX, 128), f32), two + end], axis=1)
        fields.append(middle + sides)
    source, potential, along, across, recombination = fields
    weight = jnp.sqrt(along * up(along))
    rise = 0.5 * (up(potential) - potential)
    below = weight * jnp.exp(rise)
    above = weight * jnp.exp(-rise)
    diagonal = recombination + above + down(below)
    weight = jnp.sqrt(across * left(across))
    rise = 0.5 * (left(potential) - potential)
    east = weight * jnp.exp(rise)
    west = weight * jnp.exp(-rise)
    diagonal = diagonal + west + right(east)
    faces = (below, down(above), east, right(west))
    coefs[0] = diagonal
    for f in range(4):
        coefs[1 + f] = faces[f]
    source = jnp.where(lanes_of((PX, LW)) < PY, source, 0.0)
    patch[...] = source
    own = own_mask((PX, LW), 0)
    square = total(jnp.where(own, source * source, 0.0))
    local = relax(source[8:56], diagonal[8:56], [face[8:56] for face in faces])
    solved[...] = jnp.where(own_mask((48, LW), 8), local, 0.0)
    live[...] = (rows_of((K, 128)) < counts[0, 0]).astype(f32)
    residual = restrict(basis, source, tiles, flat) * live[:, 0:1]
    row = to_row(residual)
    row = jnp.where(lanes_of((1, 128)) == SCALARS, square, row)
    gather[...] = jnp.broadcast_to(row, gather.shape)


def put(scalars, at, value):
    scalars[pl.ds(at, 1), :] = jnp.broadcast_to(value, (1, 128))


def got(scalars, at):
    return scalars[pl.ds(at, 1), :][:, 0:1]


def spread_first(
    suby, live, rows, inverse, basis, solved, part, odd, even, weights, scalars, coarse, tiles, flat
):
    sums = unpacked(rows, coarse, suby)
    square = pick(sums, SCALARS)
    norm = jnp.sqrt(square + EPSILON)
    scale = 1.0 / norm
    solution = coarse_solve(inverse, coarse) * live[:, 0:1] * scale
    weights[...] = jnp.broadcast_to(solution, (K, 128))
    put(scalars, 0, norm)
    put(scalars, 1, square / (square + EPSILON))
    part[...] = prolong(basis, solution, tiles, flat)
    part[8:56, :] = part[8:56, :] + solved[...] * scale
    odd[...], even[...] = to_pairs("gx", part[PX // 2 :, :], part[: PX // 2, :])
    odd[:, LIVE:] = live[:, : LW - LIVE]
    even[:, LIVE:] = live[:, : LW - LIVE]


def fold_rows(part, row_odd, row_even, folded, odd, even):
    height = folded.shape[0]
    first = (PX - height) // 2
    before, after = from_pairs("gx", row_odd[...], row_even[...])
    whole = part[first : first + height, :] + jnp.concatenate([before, after], axis=0)
    whole = jnp.where(lanes_of(whole.shape) < PY, whole, 0.0)
    folded[...] = whole
    lanes = lanes_of((height, 128))
    moved = pltpu.roll(jnp.where(lanes == 127, whole[:, 128:256], whole[:, 256:]), 1, 1)
    odd[...], even[...] = to_pairs(
        "gy",
        jnp.where(lanes < 33, moved, 0.0),
        jnp.where(lanes < 33, whole[:, :128], 0.0),
    )


def folded_columns(folded, odd, even):
    height = folded.shape[0]
    from_left, from_right = from_pairs("gy", odd[...], even[...])
    lanes = lanes_of((height, 128))
    one = pltpu.roll(from_left, 127, 1)
    one, end = jnp.where(lanes < 32, one, 0.0), jnp.where(lanes == 127, one, 0.0)
    sides = jnp.concatenate([one, jnp.zeros((height, 128), f32), from_right + end], axis=1)
    return folded[...] + sides


def apply_first(
    suby, live, folded, odd, even, coefs, patch, scalars, basis, row_odd, row_even, half_odd, half_even,
    direction, image, solved, gather, tiles, flat,
):
    field = folded_columns(folded, odd, even)
    direction[...] = field[OV : OV + CX]
    diagonal = coefs[0]
    faces = [coefs[1 + f] for f in range(4)]
    shape = (PX, LW)
    rows, lanes = rows_of(shape), lanes_of(shape)
    inner = (rows >= 1) & (rows < PX - 1) & (lanes < PY)
    vector = jnp.where(inner, operate(field, diagonal, faces), 0.0)
    image[...] = vector[OV : OV + CX]
    own = own_mask((CX, LW), OV)
    mine = jnp.where(own, vector[OV : OV + CX], 0.0)
    first = patch[OV : OV + CX] * (1.0 / got(scalars, 0))
    cross = total(mine * first)
    square = total(mine * mine)
    local = relax(vector[8:56], diagonal[8:56], [face[8:56] for face in faces])
    solved[...] = jnp.where(own_mask((48, LW), 8), local, 0.0)
    residual = restrict(basis, vector, tiles, flat) * live[:, 0:1]
    fourth = vector[32:40]
    third = pltpu.roll(vector[24:32], 96, 1)
    for_next = for_before = jnp.zeros((K, 128), f32)
    for t in range(3):
        cols = slice(t * 128, (t + 1) * 128)
        at = slice(160 + t * K, 160 + (t + 1) * K)
        before, after = from_pairs("gx", row_odd[at, :], row_even[at, :])
        for_next = for_next + after * fourth[0:1, cols]
        for_before = for_before + before * third[7:8, cols]
    before, after = from_pairs(
        "gx", half_odd[:, LIVE : LIVE + 1], half_even[:, LIVE : LIVE + 1]
    )
    for_next = after * jnp.sum(for_next, axis=1, keepdims=True)
    for_before = before * jnp.sum(for_before, axis=1, keepdims=True)
    row = to_row(residual)
    row = row + pltpu.roll(to_row(for_next), 32, 1)
    row = row + pltpu.roll(to_row(for_before), 64, 1)
    lanes = lanes_of((1, 128))
    row = jnp.where(lanes == SCALARS, cross, jnp.where(lanes == SCALARS + 1, square, row))
    gather[...] = jnp.broadcast_to(row, gather.shape)


def spread_second(
    suby, live, rows, inverse, basis, solved_first, solved, weights, scalars_in,
    part, odd, even, scalars, coarse, tiles, flat,
):
    sums = gathered(rows, coarse, suby)
    cross = pick(sums, SCALARS)
    square = pick(sums, SCALARS + 1)
    norm = got(scalars_in, 0)
    unit = got(scalars_in, 1)
    rest = square - 2.0 * cross * cross + cross * cross * unit
    second = jnp.sqrt(jnp.maximum(rest, 0.0) + EPSILON)
    scale = 1.0 / second
    solution = coarse_solve(inverse, coarse) * live[:, 0:1]
    solution = (solution - cross * weights[:, 0:1]) * scale
    put(scalars, 0, norm)
    put(scalars, 1, unit)
    put(scalars, 2, cross)
    put(scalars, 3, second)
    radius = 1.0 / jnp.sqrt(cross * cross + second * second)
    put(scalars, 4, radius)
    put(scalars, 5, 1.0 / norm)
    put(scalars, 6, scale)
    part[...] = prolong(basis, solution, tiles, flat)
    local = (solved[...] - (cross / norm) * solved_first[...]) * scale
    part[8:56, :] = part[8:56, :] + local
    odd[...], even[...] = to_pairs("gx", part[40:, :], part[:24, :])


def apply_second(
    folded, odd, even, coefs, patch, image, scalars, direction, third, gather
):
    field = folded_columns(folded, odd, even)
    vector = operate(field, coefs[0, 8:56, :], [coefs[1 + f, 8:56, :] for f in range(4)])
    own = own_mask((CX, LW), OV)
    direction[...] = field[8 : 8 + CX]
    vector = jnp.where(own, vector[8 : 8 + CX], 0.0)
    third[...] = vector
    first = jnp.where(own, patch[OV : OV + CX] * got(scalars, 5), 0.0)
    second = (image[...] - got(scalars, 2) * first) * got(scalars, 6)
    second = jnp.where(own, second, 0.0)
    lanes = lanes_of((1, 128))
    row = jnp.zeros((1, 128), f32)
    for lane, value in enumerate(
        (first * vector, second * vector, vector * vector, first * second, second * second)
    ):
        row = jnp.where(lanes == lane, total(value), row)
    gather[...] = jnp.broadcast_to(row, gather.shape)


def add_rows(rows, gather):
    row = jnp.sum(rows[...], axis=0, keepdims=True)
    gather[...] = jnp.broadcast_to(row, gather.shape)


def finish(rows, patch, image, third_image, direction_one, direction_two, scalars, solution, residual):
    sums = jnp.sum(rows[...], axis=0, keepdims=True)
    first_second = pick(sums, 0)
    second_second = pick(sums, 1)
    square = pick(sums, 2)
    cross = pick(sums, 3)
    unit_two = pick(sums, 4)
    source_norm = got(scalars, 0)
    unit = got(scalars, 1)
    first_first = got(scalars, 2)
    second_first = got(scalars, 3)
    inverse_radius = got(scalars, 4)
    cosine = first_first * inverse_radius
    sine = second_first * inverse_radius
    rest = square - first_second * first_second * (2.0 - unit)
    rest = rest - second_second * second_second * (2.0 - unit_two)
    rest = rest + 2.0 * first_second * second_second * cross
    third_square = jnp.maximum(rest, 0.0) + EPSILON
    upper_right = cosine * first_second + sine * second_second
    lower_right = cosine * second_second - sine * first_second
    weight_two = lower_right * (-sine * source_norm) / (lower_right * lower_right + third_square)
    weight_one = (cosine * source_norm - upper_right * weight_two) * inverse_radius
    remainder_one = source_norm - first_first * weight_one - first_second * weight_two
    remainder_two = -second_first * weight_one - second_second * weight_two
    first = patch[OV : OV + CX] * got(scalars, 5)
    second = (image[...] - first_first * first) * got(scalars, 6)
    third = third_image[...] - first_second * first - second_second * second
    found = weight_one * direction_one[...] + weight_two * direction_two[...]
    left_over = remainder_one * first + remainder_two * second - weight_two * third
    solution[...] = pltpu.roll(found, LW - OV, 1)[:, :CY]
    residual[...] = pltpu.roll(left_over, LW - OV, 1)[:, :CY]


def shape_of(*dims):
    return jax.ShapeDtypeStruct(dims, f32)


VMEM = pl.BlockSpec(memory_space=pltpu.VMEM)
PARAMS = pltpu.CompilerParams(vmem_limit_bytes=24 * 1024 * 1024)


def kernel(body, outs, scratch=(), first_smem=False):
    def call(*args):
        specs = [VMEM] * len(args)
        if first_smem:
            specs[0] = pl.BlockSpec(memory_space=pltpu.SMEM)
        return pl.pallas_call(
            body,
            out_shape=outs,
            in_specs=specs,
            out_specs=[VMEM] * len(outs),
            scratch_shapes=list(scratch),
            compiler_params=PARAMS,
        )(*args)

    return call


def swap(axis, odd, even):
    count = lax.axis_size(axis)
    even = lax.ppermute(even, axis, [(i, i ^ 1) for i in range(count)])
    odd = lax.ppermute(
        odd, axis, [(i, i + 1 if i % 2 else i - 1) for i in range(1, count - 1)]
    )
    return odd, even


def everywhere(rows, axes=AXES):
    count = lax.axis_size(axes)
    slots = rows.reshape(count, rows.shape[0] // count, 128)
    return lax.all_to_all(slots, axes, 0, 0).reshape(rows.shape)


def on_device(
    source, potential, mobility_along, mobility_across, recombination, counts, basis, coarse_inverse
):
    suby = lax.axis_size("gy")
    devices = lax.axis_size("gx") * suby
    rows = shape_of(devices, 128)
    patch_shape, own_shape = shape_of(PX, LW), shape_of(CX, LW)
    tiles = pltpu.VMEM((3, PX, 128), f32)
    flat = pltpu.VMEM((9, GROUPS, 128), f32)
    coarse = pltpu.VMEM((devices // 4, 128), f32)
    fields = (source, potential, mobility_along, mobility_across, recombination)

    def bind(body):
        def run(*refs):
            return body(suby, *refs)

        return run

    edge = pltpu.VMEM((K, 3 * 128), f32)
    held, odd, even = pl.pallas_call(
        pack_rows,
        out_shape=[shape_of(5, CX, CY), shape_of(256, 128), shape_of(256, 128)],
        in_specs=[pl.BlockSpec(memory_space=pltpu.HBM)] * 6,
        out_specs=[VMEM] * 3,
        scratch_shapes=[edge, edge, pltpu.SemaphoreType.DMA((7,))],
        compiler_params=PARAMS,
    )(*[pltpu.with_memory_space_constraint(x, pltpu.HBM) for x in (*fields, basis)])
    row_odd, row_even = swap("gx", odd, even)
    strip = shape_of(PX, 128)
    grown, odd, even = kernel(pack_columns, [shape_of(5, PX, CY), strip, strip])(
        held, row_odd, row_even
    )
    odd, even = swap("gy", odd, even)
    live, patch, coefs, solved_one, row = kernel(
        bind(prepare),
        [shape_of(K, 128), patch_shape, shape_of(5, PX, LW), shape_of(48, LW), shape_of(suby, 128)],
        [tiles, flat],
        True,
    )(counts, grown, odd, even, basis)
    (row,) = kernel(compact, [shape_of(devices // suby * slot_rows(suby), 128)])(
        everywhere(row, "gy")
    )
    half = shape_of(PX // 2, LW)
    part, odd, even, weights, scalars_one = kernel(
        bind(spread_first),
        [patch_shape, half, half, shape_of(K, 128), shape_of(8, 128)],
        [coarse, tiles, flat],
    )(live, everywhere(row, "gx"), coarse_inverse, basis, solved_one)
    half_odd, half_even = swap("gx", odd, even)
    folded, odd, even = kernel(fold_rows, [patch_shape, strip, strip])(part, half_odd, half_even)
    odd, even = swap("gy", odd, even)
    direction_one, image_one, solved_two, row = kernel(
        bind(apply_first),
        [own_shape, own_shape, shape_of(48, LW), rows],
        [tiles, flat],
    )(
        live, folded, odd, even, coefs, patch, scalars_one, basis,
        row_odd, row_even, half_odd, half_even,
    )
    half = shape_of(24, LW)
    part, odd, even, scalars_two = kernel(
        bind(spread_second),
        [patch_shape, half, half, shape_of(8, 128)],
        [coarse, tiles, flat],
    )(
        live, everywhere(row), coarse_inverse, basis, solved_one, solved_two, weights, scalars_one
    )
    half_odd, half_even = swap("gx", odd, even)
    strip = shape_of(48, 128)
    folded, odd, even = kernel(fold_rows, [shape_of(48, LW), strip, strip])(
        part, half_odd, half_even
    )
    odd, even = swap("gy", odd, even)
    direction_two, image_two, row = kernel(
        apply_second, [own_shape, own_shape, shape_of(suby, 128)]
    )(
        folded, odd, even, coefs, patch, image_one, scalars_two
    )
    (row,) = kernel(add_rows, [shape_of(devices // suby, 128)])(everywhere(row, "gy"))
    out = shape_of(CX, CY)
    answer, residual = kernel(finish, [out, out])(
        everywhere(row, "gx"), patch, image_one, image_two, direction_one, direction_two, scalars_two
    )
    return answer, residual


def solution(mesh):
    grid = P("gx", "gy")
    return jax.shard_map(
        on_device,
        mesh=mesh,
        in_specs=(grid,) * 7 + (P(("gx", "gy"), None),),
        out_specs=(grid, grid),
        check_vma=False,
    )
```

```python
import jax
import jax.numpy as jnp
from jax import lax
from jax.experimental import pallas as pl
from jax.experimental.pallas import tpu as pltpu
from jax.sharding import PartitionSpec as P

OV = 16
SWEEPS = 8
OMEGA = 0.8
EPSILON = 1e-06
CX = 32
CY = 256
K = 32
PX = CX + 2 * OV
PY = CY + 2 * OV
LW = 384
GROUPS = PX // 4
STRIP = 24
LIVE = PY
SCALARS = 96
f32 = jnp.float32
AXES = ("gx", "gy")


def lanes_of(shape):
    return lax.broadcasted_iota(jnp.int32, shape, len(shape) - 1)


def rows_of(shape):
    return lax.broadcasted_iota(jnp.int32, shape, len(shape) - 2)


def left(x):
    return pltpu.roll(x, LW - 1, 1)


def right(x):
    return pltpu.roll(x, 1, 1)


def up(x):
    return pltpu.roll(x, x.shape[0] - 1, 0)


def down(x):
    return pltpu.roll(x, 1, 0)


def own_mask(shape, first):
    rows, lanes = rows_of(shape) + first, lanes_of(shape)
    return (rows >= OV) & (rows < OV + CX) & (lanes >= OV) & (lanes < OV + CY)


def is_even(axis):
    return lax.rem(lax.axis_index(axis), 2) == 0


def to_pairs(axis, ahead, back):
    even = is_even(axis)
    return jnp.where(even, back, ahead), jnp.where(even, ahead, back)


def from_pairs(axis, odd, even_pairs):
    even = is_even(axis)
    return jnp.where(even, odd, even_pairs), jnp.where(even, even_pairs, odd)


def total(x):
    return jnp.sum(jnp.sum(x, axis=0, keepdims=True), axis=1, keepdims=True)


def to_row(column):
    shape = (K, 128)
    spread = jnp.broadcast_to(column, shape)
    return jnp.sum(jnp.where(rows_of(shape) == lanes_of(shape), spread, 0.0), axis=0, keepdims=True)


def restrict(basis, patch, tiles, flat):
    for t in range(3):
        tiles[t] = patch[:, t * 128 : (t + 1) * 128]
    parts = [None] * 9
    for m in range(4):
        rows = jnp.concatenate(
            [tiles[t, pl.ds(m, GROUPS, stride=4), :] for t in range(3)], axis=1
        )
        if m:
            rows = pltpu.roll(rows, 32 * m, 1)
        for t in range(3):
            piece = rows[:, t * 128 : (t + 1) * 128]
            at = 2 * m + t
            parts[at] = piece if parts[at] is None else parts[at] + piece
    for t in range(9):
        flat[t] = parts[t]
    sums = [jnp.zeros((K, 128), f32) for _ in range(3)]
    for g in range(GROUPS):
        for t in range(9):
            block = (g * 9 + t) * 128
            row = jnp.broadcast_to(flat[t, pl.ds(g, 1), :], (K, 128))
            sums[t % 3] = sums[t % 3] + basis[:, block : block + 128] * row
    return jnp.sum(sums[0] + sums[1] + sums[2], axis=1, keepdims=True)


def prolong(basis, weights, tiles, flat):
    wide = jnp.broadcast_to(weights, (K, 128))
    for g in range(GROUPS):
        for t in range(9):
            block = (g * 9 + t) * 128
            flat[t, pl.ds(g, 1), :] = jnp.sum(
                basis[:, block : block + 128] * wide, axis=0, keepdims=True
            )
    for m in range(4):
        rows = jnp.concatenate([flat[2 * m + t] for t in range(3)], axis=1)
        if m:
            rows = pltpu.roll(rows, LW - 32 * m, 1)
        rows = jnp.where(lanes_of(rows.shape) < PY, rows, 0.0)
        for t in range(3):
            tiles[t, pl.ds(m, GROUPS, stride=4), :] = rows[:, t * 128 : (t + 1) * 128]
    return jnp.concatenate([tiles[t] for t in range(3)], axis=1)


def gathered(rows, coarse, suby):
    count = rows.shape[0] // 4
    shift = suby // 4
    taken = [rows[pl.ds(q, count, stride=4), :] for q in range(4)]
    zero = jnp.zeros((shift, 128), f32)
    lanes = lanes_of((count, 128))
    result = None
    for s in range(4):
        own = taken[s]
        later = jnp.concatenate([zero, taken[(s + 1) % 4][: count - shift]], axis=0)
        earlier = jnp.concatenate([taken[(s + 2) % 4][shift:], zero], axis=0)
        piece = jnp.where(
            lanes < 32, own, jnp.where(lanes < 64, later, jnp.where(lanes < 96, earlier, 0.0))
        )
        if s:
            piece = pltpu.roll(piece, 32 * s, 1)
        result = piece if result is None else result + piece
    coarse[...] = result
    return jnp.sum(taken[0] + taken[1] + (taken[2] + taken[3]), axis=0, keepdims=True)


def compact(rows, gather):
    count = rows.shape[0] // 4
    slot = slot_rows(rows.shape[0])
    taken = [rows[pl.ds(q, count, stride=4), :] for q in range(4)]
    lanes = lanes_of((count, 128))
    result = None
    for q in range(4):
        piece = jnp.where(lanes < 32, taken[q], 0.0)
        if q:
            piece = pltpu.roll(piece, 32 * q, 1)
        result = piece if result is None else result + piece
    sums = jnp.sum(taken[0] + taken[1] + (taken[2] + taken[3]), axis=0, keepdims=True)
    tail = jnp.broadcast_to(sums, (slot - count, 128))
    block = jnp.concatenate([result, tail], axis=0)
    for at in range(0, gather.shape[0], slot):
        gather[at : at + slot, :] = block


def slot_rows(suby):
    return suby // 4 + 8


def unpacked(rows, coarse, suby):
    count, slot = suby // 4, slot_rows(suby)
    sums = None
    for i in range(rows.shape[0] // slot):
        coarse[i * count : (i + 1) * count, :] = rows[i * slot : i * slot + count, :]
        row = rows[i * slot + count : i * slot + count + 1, :]
        sums = row if sums is None else sums + row
    return sums


def pick(row, lane):
    return jnp.sum(jnp.where(lanes_of(row.shape) == lane, row, 0.0), axis=1, keepdims=True)


def coarse_solve(inverse, coarse):
    sums = [jnp.zeros((K, 128), f32) for _ in range(4)]
    for b in range(coarse.shape[0]):
        row = jnp.broadcast_to(coarse[pl.ds(b, 1), :], (K, 128))
        sums[b % 4] = sums[b % 4] + inverse[:, b * 128 : (b + 1) * 128] * row
    return jnp.sum((sums[0] + sums[1]) + (sums[2] + sums[3]), axis=1, keepdims=True)


def relax(vector, diagonal, faces):
    inverse = OMEGA / jnp.where(diagonal > 0.0, diagonal, 1.0)
    below, above, east, west = [inverse * face for face in faces]
    start = inverse * vector
    field = start
    for _ in range(SWEEPS - 1):
        moved = below * up(field) + above * down(field)
        moved = moved + (east * left(field) + west * right(field))
        field = (start + (1.0 - OMEGA) * field) + moved
    return field


def operate(field, diagonal, faces):
    below, above, east, west = faces
    moved = below * up(field) + above * down(field)
    moved = moved + (east * left(field) + west * right(field))
    return diagonal * field - moved


def pack_rows(
    source, potential, along, across, recombination, basis, held, odd, even, head, tail, sems
):
    edge = head.shape[1]
    copies = [
        pltpu.make_async_copy(field, held.at[f], sems.at[f])
        for f, field in enumerate((source, potential, along, across, recombination))
    ]
    copies.append(pltpu.make_async_copy(basis.at[:, :edge], head, sems.at[5]))
    copies.append(
        pltpu.make_async_copy(basis.at[:, basis.shape[1] - edge :], tail, sems.at[6])
    )
    for copy in copies:
        copy.start()
    for copy in copies:
        copy.wait()
    for f in range(5):
        for t in range(2):
            at = slice((2 * f + t) * OV, (2 * f + t + 1) * OV)
            cols = slice(t * 128, (t + 1) * 128)
            odd[at, :], even[at, :] = to_pairs(
                "gx", held[f, CX - OV :, cols], held[f, :OV, cols]
            )
    for t in range(3):
        at = slice(160 + t * K, 160 + (t + 1) * K)
        cols = slice(t * 128, (t + 1) * 128)
        odd[at, :], even[at, :] = to_pairs("gx", tail[:, cols], head[:, cols])


def pack_columns(held, row_odd, row_even, rows, odd, even):
    before, after = from_pairs("gx", row_odd[: 10 * OV, :], row_even[: 10 * OV, :])
    lanes = lanes_of((PX, 128))
    to_right = to_left = None
    for f in range(5):
        tiles = []
        for t in range(2):
            at = (2 * f + t) * OV
            cols = slice(t * 128, (t + 1) * 128)
            tile = jnp.concatenate(
                [before[at : at + OV, :], held[f, :, cols], after[at : at + OV, :]], axis=0
            )
            rows[f, :, cols] = tile
            tiles.append(tile)
        last = pltpu.roll(jnp.where(lanes >= 111, tiles[1], 0.0), 17 + STRIP * f, 1)
        first = jnp.where(lanes < 17, tiles[0], 0.0)
        if f:
            first = pltpu.roll(first, STRIP * f, 1)
        to_right = last if f == 0 else to_right + last
        to_left = first if f == 0 else to_left + first
    odd[...], even[...] = to_pairs("gy", to_right, to_left)


def prepare(suby, counts, rows, odd, even, basis, live, patch, coefs, solved, gather, tiles, flat):
    zero = jnp.zeros((PX, LW - CY), f32)
    lanes = lanes_of((PX, 128))
    from_left, from_right = from_pairs("gy", odd[...], even[...])
    fields = []
    for f in range(5):
        middle = pltpu.roll(jnp.concatenate([rows[f], zero], axis=1), OV, 1)
        band = (lanes >= STRIP * f) & (lanes < STRIP * f + 17)
        one = pltpu.roll(jnp.where(band, from_left, 0.0), 127 - STRIP * f, 1)
        two = pltpu.roll(jnp.where(band, from_right, 0.0), (128 + OV - STRIP * f) % 128, 1)
        one, end = jnp.where(lanes < OV, one, 0.0), jnp.where(lanes == 127, one, 0.0)
        sides = jnp.concatenate([one, jnp.zeros((PX, 128), f32), two + end], axis=1)
        fields.append(middle + sides)
    source, potential, along, across, recombination = fields
    weight = jnp.sqrt(along * up(along))
    rise = 0.5 * (up(potential) - potential)
    below = weight * jnp.exp(rise)
    above = weight * jnp.exp(-rise)
    diagonal = recombination + above + down(below)
    weight = jnp.sqrt(across * left(across))
    rise = 0.5 * (left(potential) - potential)
    east = weight * jnp.exp(rise)
    west = weight * jnp.exp(-rise)
    diagonal = diagonal + west + right(east)
    faces = (below, down(above), east, right(west))
    coefs[0] = diagonal
    for f in range(4):
        coefs[1 + f] = faces[f]
    source = jnp.where(lanes_of((PX, LW)) < PY, source, 0.0)
    patch[...] = source
    own = own_mask((PX, LW), 0)
    square = total(jnp.where(own, source * source, 0.0))
    local = relax(source[8:56], diagonal[8:56], [face[8:56] for face in faces])
    solved[...] = jnp.where(own_mask((48, LW), 8), local, 0.0)
    live[...] = (rows_of((K, 128)) < counts[0, 0]).astype(f32)
    residual = restrict(basis, source, tiles, flat) * live[:, 0:1]
    row = to_row(residual)
    row = jnp.where(lanes_of((1, 128)) == SCALARS, square, row)
    gather[...] = jnp.broadcast_to(row, gather.shape)


def put(scalars, at, value):
    scalars[pl.ds(at, 1), :] = jnp.broadcast_to(value, (1, 128))


def got(scalars, at):
    return scalars[pl.ds(at, 1), :][:, 0:1]


def spread_first(
    suby, live, rows, inverse, basis, solved, part, odd, even, weights, scalars, coarse, tiles, flat
):
    sums = unpacked(rows, coarse, suby)
    square = pick(sums, SCALARS)
    norm = jnp.sqrt(square + EPSILON)
    scale = 1.0 / norm
    solution = coarse_solve(inverse, coarse) * live[:, 0:1] * scale
    weights[...] = jnp.broadcast_to(solution, (K, 128))
    put(scalars, 0, norm)
    put(scalars, 1, square / (square + EPSILON))
    part[...] = prolong(basis, solution, tiles, flat)
    part[8:56, :] = part[8:56, :] + solved[...] * scale
    odd[...], even[...] = to_pairs("gx", part[PX // 2 :, :], part[: PX // 2, :])
    odd[:, LIVE:] = live[:, : LW - LIVE]
    even[:, LIVE:] = live[:, : LW - LIVE]


def fold_rows(part, row_odd, row_even, folded, odd, even):
    height = folded.shape[0]
    first = (PX - height) // 2
    before, after = from_pairs("gx", row_odd[...], row_even[...])
    whole = part[first : first + height, :] + jnp.concatenate([before, after], axis=0)
    whole = jnp.where(lanes_of(whole.shape) < PY, whole, 0.0)
    folded[...] = whole
    lanes = lanes_of((height, 128))
    moved = pltpu.roll(jnp.where(lanes == 127, whole[:, 128:256], whole[:, 256:]), 1, 1)
    odd[...], even[...] = to_pairs(
        "gy",
        jnp.where(lanes < 33, moved, 0.0),
        jnp.where(lanes < 33, whole[:, :128], 0.0),
    )


def folded_columns(folded, odd, even):
    height = folded.shape[0]
    from_left, from_right = from_pairs("gy", odd[...], even[...])
    lanes = lanes_of((height, 128))
    one = pltpu.roll(from_left, 127, 1)
    one, end = jnp.where(lanes < 32, one, 0.0), jnp.where(lanes == 127, one, 0.0)
    sides = jnp.concatenate([one, jnp.zeros((height, 128), f32), from_right + end], axis=1)
    return folded[...] + sides


def apply_first(
    suby, live, folded, odd, even, coefs, patch, scalars, basis, row_odd, row_even, half_odd, half_even,
    direction, image, solved, gather, tiles, flat,
):
    field = folded_columns(folded, odd, even)
    direction[...] = field[OV : OV + CX]
    diagonal = coefs[0]
    faces = [coefs[1 + f] for f in range(4)]
    shape = (PX, LW)
    rows, lanes = rows_of(shape), lanes_of(shape)
    inner = (rows >= 1) & (rows < PX - 1) & (lanes < PY)
    vector = jnp.where(inner, operate(field, diagonal, faces), 0.0)
    image[...] = vector[OV : OV + CX]
    own = own_mask((CX, LW), OV)
    mine = jnp.where(own, vector[OV : OV + CX], 0.0)
    first = patch[OV : OV + CX] * (1.0 / got(scalars, 0))
    cross = total(mine * first)
    square = total(mine * mine)
    local = relax(vector[8:56], diagonal[8:56], [face[8:56] for face in faces])
    solved[...] = jnp.where(own_mask((48, LW), 8), local, 0.0)
    residual = restrict(basis, vector, tiles, flat) * live[:, 0:1]
    fourth = vector[32:40]
    third = pltpu.roll(vector[24:32], 96, 1)
    for_next = for_before = jnp.zeros((K, 128), f32)
    for t in range(3):
        cols = slice(t * 128, (t + 1) * 128)
        at = slice(160 + t * K, 160 + (t + 1) * K)
        before, after = from_pairs("gx", row_odd[at, :], row_even[at, :])
        for_next = for_next + after * fourth[0:1, cols]
        for_before = for_before + before * third[7:8, cols]
    before, after = from_pairs(
        "gx", half_odd[:, LIVE : LIVE + 1], half_even[:, LIVE : LIVE + 1]
    )
    for_next = after * jnp.sum(for_next, axis=1, keepdims=True)
    for_before = before * jnp.sum(for_before, axis=1, keepdims=True)
    row = to_row(residual)
    row = row + pltpu.roll(to_row(for_next), 32, 1)
    row = row + pltpu.roll(to_row(for_before), 64, 1)
    lanes = lanes_of((1, 128))
    row = jnp.where(lanes == SCALARS, cross, jnp.where(lanes == SCALARS + 1, square, row))
    gather[...] = jnp.broadcast_to(row, gather.shape)


def spread_second(
    suby, live, rows, inverse, basis, solved_first, solved, weights, scalars_in,
    part, odd, even, scalars, coarse, tiles, flat,
):
    sums = gathered(rows, coarse, suby)
    cross = pick(sums, SCALARS)
    square = pick(sums, SCALARS + 1)
    norm = got(scalars_in, 0)
    unit = got(scalars_in, 1)
    rest = square - 2.0 * cross * cross + cross * cross * unit
    second = jnp.sqrt(jnp.maximum(rest, 0.0) + EPSILON)
    scale = 1.0 / second
    solution = coarse_solve(inverse, coarse) * live[:, 0:1]
    solution = (solution - cross * weights[:, 0:1]) * scale
    put(scalars, 0, norm)
    put(scalars, 1, unit)
    put(scalars, 2, cross)
    put(scalars, 3, second)
    radius = 1.0 / jnp.sqrt(cross * cross + second * second)
    put(scalars, 4, radius)
    put(scalars, 5, 1.0 / norm)
    put(scalars, 6, scale)
    part[...] = prolong(basis, solution, tiles, flat)
    local = (solved[...] - (cross / norm) * solved_first[...]) * scale
    part[8:56, :] = part[8:56, :] + local
    odd[...], even[...] = to_pairs("gx", part[40:, :], part[:24, :])


def apply_second(
    folded, odd, even, coefs, patch, image, scalars, direction, third, gather
):
    field = folded_columns(folded, odd, even)
    vector = operate(field, coefs[0, 8:56, :], [coefs[1 + f, 8:56, :] for f in range(4)])
    own = own_mask((CX, LW), OV)
    direction[...] = field[8 : 8 + CX]
    vector = jnp.where(own, vector[8 : 8 + CX], 0.0)
    third[...] = vector
    first = jnp.where(own, patch[OV : OV + CX] * got(scalars, 5), 0.0)
    second = (image[...] - got(scalars, 2) * first) * got(scalars, 6)
    second = jnp.where(own, second, 0.0)
    lanes = lanes_of((1, 128))
    row = jnp.zeros((1, 128), f32)
    for lane, value in enumerate(
        (first * vector, second * vector, vector * vector, first * second, second * second)
    ):
        row = jnp.where(lanes == lane, total(value), row)
    gather[...] = jnp.broadcast_to(row, gather.shape)


def add_rows(rows, gather):
    row = jnp.sum(rows[...], axis=0, keepdims=True)
    gather[...] = jnp.broadcast_to(row, gather.shape)


def finish(rows, patch, image, third_image, direction_one, direction_two, scalars, solution, residual):
    sums = jnp.sum(rows[...], axis=0, keepdims=True)
    first_second = pick(sums, 0)
    second_second = pick(sums, 1)
    square = pick(sums, 2)
    cross = pick(sums, 3)
    unit_two = pick(sums, 4)
    source_norm = got(scalars, 0)
    unit = got(scalars, 1)
    first_first = got(scalars, 2)
    second_first = got(scalars, 3)
    inverse_radius = got(scalars, 4)
    cosine = first_first * inverse_radius
    sine = second_first * inverse_radius
    rest = square - first_second * first_second * (2.0 - unit)
    rest = rest - second_second * second_second * (2.0 - unit_two)
    rest = rest + 2.0 * first_second * second_second * cross
    third_square = jnp.maximum(rest, 0.0) + EPSILON
    upper_right = cosine * first_second + sine * second_second
    lower_right = cosine * second_second - sine * first_second
    weight_two = lower_right * (-sine * source_norm) / (lower_right * lower_right + third_square)
    weight_one = (cosine * source_norm - upper_right * weight_two) * inverse_radius
    remainder_one = source_norm - first_first * weight_one - first_second * weight_two
    remainder_two = -second_first * weight_one - second_second * weight_two
    first = patch[OV : OV + CX] * got(scalars, 5)
    second = (image[...] - first_first * first) * got(scalars, 6)
    third = third_image[...] - first_second * first - second_second * second
    found = weight_one * direction_one[...] + weight_two * direction_two[...]
    left_over = remainder_one * first + remainder_two * second - weight_two * third
    solution[...] = pltpu.roll(found, LW - OV, 1)[:, :CY]
    residual[...] = pltpu.roll(left_over, LW - OV, 1)[:, :CY]


def shape_of(*dims):
    return jax.ShapeDtypeStruct(dims, f32)


VMEM = pl.BlockSpec(memory_space=pltpu.VMEM)
PARAMS = pltpu.CompilerParams(vmem_limit_bytes=24 * 1024 * 1024)


def kernel(body, outs, scratch=(), first_smem=False):
    def call(*args):
        specs = [VMEM] * len(args)
        if first_smem:
            specs[0] = pl.BlockSpec(memory_space=pltpu.SMEM)
        return pl.pallas_call(
            body,
            out_shape=outs,
            in_specs=specs,
            out_specs=[VMEM] * len(outs),
            scratch_shapes=list(scratch),
            compiler_params=PARAMS,
        )(*args)

    return call


def swap(axis, odd, even):
    count = lax.axis_size(axis)
    even = lax.ppermute(even, axis, [(i, i ^ 1) for i in range(count)])
    odd = lax.ppermute(
        odd, axis, [(i, i + 1 if i % 2 else i - 1) for i in range(1, count - 1)]
    )
    return odd, even


def everywhere(rows, axes=AXES):
    count = lax.axis_size(axes)
    slots = rows.reshape(count, rows.shape[0] // count, 128)
    return lax.all_to_all(slots, axes, 0, 0).reshape(rows.shape)


def on_device(
    source, potential, mobility_along, mobility_across, recombination, counts, basis, coarse_inverse
):
    suby = lax.axis_size("gy")
    devices = lax.axis_size("gx") * suby
    rows = shape_of(devices, 128)
    patch_shape, own_shape = shape_of(PX, LW), shape_of(CX, LW)
    tiles = pltpu.VMEM((3, PX, 128), f32)
    flat = pltpu.VMEM((9, GROUPS, 128), f32)
    coarse = pltpu.VMEM((devices // 4, 128), f32)
    fields = (source, potential, mobility_along, mobility_across, recombination)

    def bind(body):
        def run(*refs):
            return body(suby, *refs)

        return run

    edge = pltpu.VMEM((K, 3 * 128), f32)
    held, odd, even = pl.pallas_call(
        pack_rows,
        out_shape=[shape_of(5, CX, CY), shape_of(256, 128), shape_of(256, 128)],
        in_specs=[pl.BlockSpec(memory_space=pltpu.HBM)] * 6,
        out_specs=[VMEM] * 3,
        scratch_shapes=[edge, edge, pltpu.SemaphoreType.DMA((7,))],
        compiler_params=PARAMS,
    )(*[pltpu.with_memory_space_constraint(x, pltpu.HBM) for x in (*fields, basis)])
    row_odd, row_even = swap("gx", odd, even)
    strip = shape_of(PX, 128)
    grown, odd, even = kernel(pack_columns, [shape_of(5, PX, CY), strip, strip])(
        held, row_odd, row_even
    )
    odd, even = swap("gy", odd, even)
    live, patch, coefs, solved_one, row = kernel(
        bind(prepare),
        [shape_of(K, 128), patch_shape, shape_of(5, PX, LW), shape_of(48, LW), shape_of(suby, 128)],
        [tiles, flat],
        True,
    )(counts, grown, odd, even, basis)
    (row,) = kernel(compact, [shape_of(devices // suby * slot_rows(suby), 128)])(
        everywhere(row, "gy")
    )
    half = shape_of(PX // 2, LW)
    part, odd, even, weights, scalars_one = kernel(
        bind(spread_first),
        [patch_shape, half, half, shape_of(K, 128), shape_of(8, 128)],
        [coarse, tiles, flat],
    )(live, everywhere(row, "gx"), coarse_inverse, basis, solved_one)
    half_odd, half_even = swap("gx", odd, even)
    folded, odd, even = kernel(fold_rows, [patch_shape, strip, strip])(part, half_odd, half_even)
    odd, even = swap("gy", odd, even)
    direction_one, image_one, solved_two, row = kernel(
        bind(apply_first),
        [own_shape, own_shape, shape_of(48, LW), rows],
        [tiles, flat],
    )(
        live, folded, odd, even, coefs, patch, scalars_one, basis,
        row_odd, row_even, half_odd, half_even,
    )
    half = shape_of(24, LW)
    part, odd, even, scalars_two = kernel(
        bind(spread_second),
        [patch_shape, half, half, shape_of(8, 128)],
        [coarse, tiles, flat],
    )(
        live, everywhere(row), coarse_inverse, basis, solved_one, solved_two, weights, scalars_one
    )
    half_odd, half_even = swap("gx", odd, even)
    strip = shape_of(48, 128)
    folded, odd, even = kernel(fold_rows, [shape_of(48, LW), strip, strip])(
        part, half_odd, half_even
    )
    odd, even = swap("gy", odd, even)
    direction_two, image_two, row = kernel(
        apply_second, [own_shape, own_shape, shape_of(suby, 128)]
    )(
        folded, odd, even, coefs, patch, image_one, scalars_two
    )
    (row,) = kernel(add_rows, [shape_of(devices // suby, 128)])(everywhere(row, "gy"))
    out = shape_of(CX, CY)
    answer, residual = kernel(finish, [out, out])(
        everywhere(row, "gx"), patch, image_one, image_two, direction_one, direction_two, scalars_two
    )
    return answer, residual


def solution(mesh):
    grid = P("gx", "gy")
    return jax.shard_map(
        on_device,
        mesh=mesh,
        in_specs=(grid,) * 7 + (P(("gx", "gy"), None),),
        out_specs=(grid, grid),
        check_vma=False,
    )
```
